256 devices in a mesh: narrow: 2 (over core), wide: 128 (over y, z, x).
Axes of the slice: x: 4, y: 4, z: 8, core: 2. Of those that a mesh axis runs over, the one named last changes fastest.
Arguments:
- embeddings: bfloat16 [196608, 4096], P(('narrow', 'wide')), may hold values from -32 to 32
- sketch_seed: int32 [4096, 256], replicated, may hold values from -1 to 1
- list_ids: int32 [196608], P(('narrow', 'wide')), may hold values from 0 to 262143, as said below
- owner_map: int32 [262144], replicated, may hold values from 0 to 255, as said below
Outputs:
- received: bfloat16 [256, 256, 12, 256], P(('narrow', 'wide'))
- received_lists: int32 [256, 256, 12], P(('narrow', 'wide'))
The draws below stay inside these ranges and needn't reach their ends.
Inputs may be any that keep to these rules, and one draw needn't show every extreme that they name: `owner_map`: each device owns exactly 1024 lists. `list_ids`: among the rows of one device at most 12 have lists owned by one device; in every draw some owners get exactly 12 rows from every device.
All inputs are finite; a program needn't handle non-finite values.
Results may differ from the reference program's by a relative error of at most 0.0029.
The reference program's roundings to bfloat16 on the way (of `sketch`, `projector` and `reduced`) count: a program that leaves them out, or rounds other values in their place, can miss the bound.
Values may be sent and summed in bfloat16 or wider, within the bound.
No kernel may reach another device: no remote copies, remote signals or barrier semaphores. Data moves between devices by JAX's collectives and lax.ppermute only.
A program may use at most 128 MiB of HBM per device.

```python
import math
import jax
import jax.numpy as jnp
from jax import lax

D = 4096
K = 256
LIST_DEV = 1024
ROWS_DEV = 768
NS_STEPS = 6
TOTAL = 196608
LISTS = 262144
CAP = 12
HOT = 16
DEVICES = 256


def owner_table(base_key):
    shuffled = jax.random.permutation(base_key, LISTS).astype(jnp.int32)
    inverse = jnp.zeros((LISTS,), jnp.int32).at[shuffled].set(jnp.arange(LISTS, dtype=jnp.int32))
    return (shuffled % DEVICES, inverse)


def draw_owner_map(key, part):
    owners, inverse = owner_table(key)
    return owners.astype(jnp.int32)


def draw_list_ids(key, part):
    owners, inverse = owner_table(key)
    key = jax.random.fold_in(key, 7)
    hot_key, rows_key = jax.random.split(key)
    hot_owner = (jax.random.permutation(hot_key, DEVICES) < HOT).astype(jnp.int32)

    def one_device(dev_key):
        noise_key, shuffle_key, pick_key = jax.random.split(dev_key, 3)
        slots = jnp.arange(DEVICES * CAP, dtype=jnp.int32)
        slot_owner = slots // CAP
        noise = jax.random.randint(noise_key, (DEVICES * CAP,), 0, 1024, dtype=jnp.int32)
        score = hot_owner[slot_owner] * (1 << 22) + noise * (DEVICES * CAP) + slots
        top_score, picked = lax.top_k(score, ROWS_DEV)
        chosen = jax.random.permutation(shuffle_key, slot_owner[picked])
        pick_keys = jax.random.split(pick_key, 3)
        depth = jax.random.randint(pick_keys[0], (ROWS_DEV,), 0, LIST_DEV, dtype=jnp.int32)
        depth = jnp.minimum(depth, jax.random.randint(pick_keys[1], (ROWS_DEV,), 0, LIST_DEV, dtype=jnp.int32))
        depth = jnp.minimum(depth, jax.random.randint(pick_keys[2], (ROWS_DEV,), 0, LIST_DEV, dtype=jnp.int32))
        return inverse[chosen + DEVICES * depth]
    return jax.vmap(one_device)(jax.random.split(rows_key, DEVICES)).reshape(TOTAL).astype(jnp.int32)


def draw_embeddings(key, part):
    key = jax.random.fold_in(key, 11)
    base_key, col_key, jitter_key = jax.random.split(key, 3)
    position = jnp.arange(TOTAL, dtype=jnp.float32) / TOTAL
    col_scale = jnp.exp(jax.random.uniform(col_key, (D,), jnp.float32, math.log(0.3), math.log(3.0)))
    jitter = jnp.exp(jax.random.uniform(jitter_key, (TOTAL, 1), jnp.float32, math.log(0.7), math.log(1.4)))
    row_scale = (1.0 + 2.0 * position)[:, None] * jitter
    values = jax.random.normal(base_key, (TOTAL, D), jnp.float32)
    return jnp.clip(values * col_scale[None, :] * row_scale, -32.0, 32.0).astype(jnp.bfloat16)


def set_ends(drawn, rng, low, high):
    longest = drawn.shape.index(max(drawn.shape))
    spots = []
    for shift in (0, 1):
        where = [jax.random.randint(jax.random.fold_in(rng, axis), (), 0, length) for axis, length in enumerate(drawn.shape)]
        where[longest] = (where[longest] + shift) % drawn.shape[longest]
        spots.append(tuple(where))
    return drawn.at[spots[0]].set(low).at[spots[1]].set(high)


def setup_inputs(seed: int = 0) -> dict:
    key_list = jax.random.split(jax.random.key(seed), 5)
    embeddings = draw_embeddings(jax.random.fold_in(key_list[4], 71), 0)
    sketch_seed = set_ends(jax.random.randint(key_list[1], (D, K), -1, 2), jax.random.fold_in(key_list[1], 1), -1, 1).astype(jnp.int32)
    list_ids = draw_list_ids(jax.random.fold_in(key_list[4], 71), 0)
    owner_map = draw_owner_map(jax.random.fold_in(key_list[4], 71), 0)
    return dict(embeddings=embeddings, sketch_seed=sketch_seed, list_ids=list_ids, owner_map=owner_map)


def whiten_root(cov_total):
    trace_value = jnp.trace(cov_total)
    normed = cov_total / trace_value
    eye_matrix = jnp.eye(cov_total.shape[0], dtype=jnp.float32)
    left_iter = normed
    right_iter = eye_matrix
    for step_index in range(NS_STEPS):
        middle = 1.5 * eye_matrix - 0.5 * jnp.dot(right_iter, left_iter, precision=lax.Precision.HIGHEST)
        left_iter = jnp.dot(left_iter, middle, precision=lax.Precision.HIGHEST)
        right_iter = jnp.dot(middle, right_iter, precision=lax.Precision.HIGHEST)
    return right_iter / jnp.sqrt(trace_value)

def block_slots(block_owner):
    onehot = (block_owner[:, None] == jnp.arange(DEVICES, dtype=jnp.int32)[None, :]).astype(jnp.int32)
    before = jnp.cumsum(onehot, axis=0) - onehot
    return lax.optimization_barrier(jnp.sum(before * onehot, axis=1)).astype(jnp.int32)

def reference(embeddings, sketch_seed, list_ids, owner_map):
    seed_matrix = sketch_seed.astype(jnp.bfloat16)
    sketch = jnp.dot(embeddings.astype(jnp.float32), seed_matrix.astype(jnp.float32), preferred_element_type=jnp.float32).astype(jnp.bfloat16)
    gram_total = jnp.dot(sketch.T.astype(jnp.float32), sketch.astype(jnp.float32), preferred_element_type=jnp.float32)
    cross_sum = jnp.dot(sketch.T.astype(jnp.float32), embeddings.astype(jnp.float32), preferred_element_type=jnp.float32)
    lower_factor = jnp.linalg.cholesky(gram_total)
    proj_basis = jax.scipy.linalg.solve_triangular(lower_factor, cross_sum, lower=True)
    cov_total = jnp.dot(proj_basis, proj_basis.T, precision=lax.Precision.HIGHEST)
    factor = whiten_root(cov_total)
    projector = jnp.dot(proj_basis.T, factor, precision=lax.Precision.HIGHEST).astype(jnp.bfloat16)
    reduced = jnp.dot(embeddings.astype(jnp.float32), projector.astype(jnp.float32), preferred_element_type=jnp.float32).astype(jnp.bfloat16)
    owners = owner_map[list_ids].astype(jnp.int32).reshape(DEVICES, ROWS_DEV)
    slot_index = lax.map(block_slots, owners)
    source = jnp.arange(DEVICES, dtype=jnp.int32)[:, None]
    flat_index = ((owners * DEVICES + source) * CAP + slot_index).reshape(TOTAL).astype(jnp.int32)
    received = jnp.zeros((DEVICES * DEVICES * CAP, K), jnp.bfloat16).at[flat_index].set(reduced)
    received_lists = jnp.full((DEVICES * DEVICES * CAP,), -1, jnp.int32).at[flat_index].set(list_ids)
    return (received.reshape(DEVICES, DEVICES, CAP, K), received_lists.reshape(DEVICES, DEVICES, CAP))
```

```python
import jax
import jax.numpy as jnp
from jax import lax
from jax.experimental import pallas as pl
from jax.experimental.pallas import tpu as pltpu
from jax.sharding import Mesh
from jax.sharding import PartitionSpec as P

NS_STEPS = 6
BLOCK = 32
TILE = 8
ALL = ("narrow", "y", "z", "x")
PLANE = ("y", "z")
HIGHEST = lax.Precision.HIGHEST


def dot_f32(a, b, dims=(((1,), (0,)), ((), ()))):
    return lax.dot_general(a, b, dims, precision=HIGHEST, preferred_element_type=jnp.float32)


def invert_kernel(gram_ref, inverse_ref, work_ref):
    rank = gram_ref.shape[0]
    row_ids = lax.broadcasted_iota(jnp.int32, (rank, rank), 0)
    col_ids = lax.broadcasted_iota(jnp.int32, (rank, rank), 1)
    work_ref[:, :rank] = gram_ref[...]
    work_ref[:, rank:] = (row_ids == col_ids).astype(jnp.float32)
    lane = lax.broadcasted_iota(jnp.int32, (BLOCK, 128), 1)
    row = lax.broadcasted_iota(jnp.int32, (BLOCK, 128), 0)
    panel_lane = lax.broadcasted_iota(jnp.int32, (BLOCK, rank), 1)

    def block_step(step, carry):
        start = pl.multiple_of(step * BLOCK, BLOCK)
        panel = work_ref[pl.ds(start, BLOCK), :]
        shifted = pltpu.roll(panel[:, :rank], rank - start, 1)[:, :128]
        rest = jnp.where(lane < BLOCK, shifted, (lane - BLOCK == row).astype(jnp.float32))
        done = []
        for tile in range(BLOCK // TILE):
            height = BLOCK - tile * TILE
            sub = lax.broadcasted_iota(jnp.int32, (height, 128), 0)
            columns = [
                jnp.broadcast_to(rest[:, tile * TILE + j : tile * TILE + j + 1], (height, 128))
                for j in range(TILE)
            ]
            for j in range(TILE):
                pivot = columns[j][j : j + 1, :]
                scale = lax.rsqrt(pivot)
                scale = scale * (1.5 - 0.5 * (pivot * scale) * scale)
                below = jnp.where(sub > j, columns[j] * scale, 0.0)
                lead = rest[j : j + 1, :] * scale
                done.append(lead)
                rest = rest - below * lead
                for m in range(j + 1, TILE):
                    columns[m] = columns[m] - below * (columns[m][j : j + 1, :] * scale)
            rest = rest[TILE:, :]
        solved = jnp.concatenate(done, axis=0)
        small = pltpu.roll(solved, 128 - BLOCK, 1)[:, :BLOCK]
        panel = dot_f32(small, panel)
        inverse_ref[pl.ds(start, BLOCK), :] = panel[:, rank:]
        later = jnp.where(panel_lane >= start + BLOCK, panel[:, :rank], 0.0)
        work_ref[...] -= dot_f32(later, panel, (((0,), (0,)), ((), ())))
        return carry

    lax.fori_loop(0, rank // BLOCK, block_step, 0)


def invert_factor(gram):
    rank = gram.shape[0]
    return pl.pallas_call(
        invert_kernel,
        out_shape=jax.ShapeDtypeStruct((rank, rank), jnp.float32),
        scratch_shapes=[pltpu.VMEM((rank, 2 * rank), jnp.float32)],
        cost_estimate=pl.CostEstimate(flops=20_000_000_000, bytes_accessed=524288, transcendentals=0),
        name="invert_factor",
    )(gram)


def whiten_kernel(inverse_ref, moment_ref, weight_ref):
    inverse = inverse_ref[...]
    rank = inverse.shape[0]
    cov_total = dot_f32(dot_f32(inverse, moment_ref[...]), inverse, (((1,), (1,)), ((), ())))
    row_ids = lax.broadcasted_iota(jnp.int32, (rank, rank), 0)
    col_ids = lax.broadcasted_iota(jnp.int32, (rank, rank), 1)
    eye_matrix = (row_ids == col_ids).astype(jnp.float32)
    trace_value = jnp.sum(cov_total * eye_matrix, axis=(0, 1), keepdims=True)
    left_iter = cov_total / trace_value
    right_iter = 1.5 * eye_matrix - 0.5 * left_iter
    left_iter = dot_f32(left_iter, right_iter)
    for step_index in range(1, NS_STEPS):
        middle = 1.5 * eye_matrix - 0.5 * dot_f32(right_iter, left_iter)
        if step_index < NS_STEPS - 1:
            left_iter = dot_f32(left_iter, middle)
        right_iter = dot_f32(middle, right_iter)
    factor = right_iter / jnp.sqrt(trace_value)
    weight_ref[...] = dot_f32(inverse, factor, (((0,), (0,)), ((), ())))


def whiten_weight(inverse, moment):
    rank = inverse.shape[0]
    return pl.pallas_call(
        whiten_kernel,
        out_shape=jax.ShapeDtypeStruct((rank, rank), jnp.float32),
        cost_estimate=pl.CostEstimate(flops=10_000_000_000, bytes_accessed=786432, transcendentals=0),
        name="whiten_weight",
    )(inverse, moment)


def place_kernel(target_ref, rows_ref, out_ref):
    tile = out_ref.shape[0]
    base = pl.program_id(0) * tile
    slots = base + lax.broadcasted_iota(jnp.int32, (tile, target_ref.shape[1]), 0)
    onehot = (slots == target_ref[...]).astype(jnp.bfloat16)
    out_ref[...] = jnp.dot(onehot, rows_ref[...], preferred_element_type=jnp.float32).astype(
        jnp.bfloat16
    )


def place_rows(target, rows, count):
    tile = 256
    depth, width = rows.shape
    return pl.pallas_call(
        place_kernel,
        grid=(count // tile,),
        in_specs=[
            pl.BlockSpec((1, depth), lambda i: (0, 0)),
            pl.BlockSpec((depth, width), lambda i: (0, 0)),
        ],
        out_specs=pl.BlockSpec((tile, width), lambda i: (i, 0)),
        out_shape=jax.ShapeDtypeStruct((count, width), jnp.bfloat16),
        cost_estimate=pl.CostEstimate(
            flops=2 * count * depth * width, bytes_accessed=4 * count * width, transcendentals=0
        ),
        name="place_rows",
    )(target.reshape(1, depth), rows)


def shift(value, axis, step):
    size = lax.axis_size(axis)
    return lax.ppermute(value, axis, [(i, (i + step) % size) for i in range(size)])


def split_terms(value):
    high = value.astype(jnp.bfloat16)
    rest = value - high.astype(jnp.float32)
    middle = rest.astype(jnp.bfloat16)
    low = (rest - middle.astype(jnp.float32)).astype(jnp.bfloat16)
    return high, middle, low


def sum_over_slice(cross_part, gram_part):
    dim, rank = cross_part.shape
    core = lax.axis_index("narrow")
    spot = lax.axis_index("x")
    cores, line = lax.axis_size("narrow"), lax.axis_size("x")
    plane = lax.axis_size("y") * lax.axis_size("z")
    half, chunk = dim // cores, dim // cores // line
    piece, gram_chunk = chunk // plane, rank // line
    gram_piece = gram_chunk // plane
    f32 = jnp.float32

    keep = lax.dynamic_slice_in_dim(cross_part, core * half, half)
    give = lax.dynamic_slice_in_dim(cross_part, (1 - core) * half, half)
    cross_half = keep + shift(give, "narrow", 1)
    gram_chip = gram_part + shift(gram_part, "narrow", 1)

    packed = jnp.concatenate(
        [cross_half.astype(jnp.bfloat16).reshape(line, chunk, rank)]
        + [t.reshape(line, gram_chunk, rank) for t in split_terms(gram_chip)],
        axis=1,
    )
    cross_line = lax.dynamic_slice_in_dim(cross_half, spot * chunk, chunk)
    gram_line = lax.dynamic_slice_in_dim(gram_chip, spot * gram_chunk, gram_chunk)
    for step in range(1, line):
        got = shift(
            lax.dynamic_index_in_dim(packed, (spot + step) % line, 0, keepdims=False), "x", step
        ).astype(f32)
        cross_line = cross_line + got[:chunk]
        gram_got = got[chunk:].reshape(3, gram_chunk, rank)
        gram_line = gram_line + (gram_got[0] + gram_got[1] + gram_got[2])

    fill = -(piece + 3 * gram_piece) % 8
    packed = jnp.concatenate(
        [cross_line.astype(jnp.bfloat16).reshape(plane, piece, rank)]
        + [t.reshape(plane, gram_piece, rank) for t in split_terms(gram_line)]
        + [jnp.zeros((plane, fill, rank), jnp.bfloat16)],
        axis=1,
    )
    total = jnp.sum(lax.all_to_all(packed, PLANE, 0, 0, tiled=True).astype(f32), axis=0)
    gram_got = total[piece : piece + 3 * gram_piece].reshape(3, gram_piece, rank)
    gram_own = gram_got[0] + gram_got[1] + gram_got[2]

    fill = -(piece + gram_piece) % 8
    packed = jnp.concatenate([total[:piece], gram_own, jnp.zeros((fill, rank), f32)], axis=0)
    packed = jnp.broadcast_to(packed[None], (plane,) + packed.shape)
    packed = lax.all_to_all(packed, PLANE, 0, 0, tiled=True)
    cross_line = packed[:, :piece].reshape(chunk, rank)
    gram_line = packed[:, piece : piece + gram_piece].reshape(gram_chunk, rank)
    gram_total = jnp.zeros((rank, rank), f32)
    gram_total = lax.dynamic_update_slice_in_dim(gram_total, gram_line, spot * gram_chunk, 0)
    for step in range(1, line):
        got = shift(gram_line, "x", step)
        place = (spot - step) % line
        gram_total = lax.dynamic_update_slice_in_dim(gram_total, got, place * gram_chunk, 0)
    cross_half = jnp.zeros((half, rank), f32)
    cross_half = lax.dynamic_update_slice_in_dim(cross_half, cross_line, spot * chunk, 0)
    for step in range(1, line):
        got = shift(cross_line, "x", step)
        place = (spot - step) % line
        cross_half = lax.dynamic_update_slice_in_dim(cross_half, got, place * chunk, 0)
    other = shift(cross_half, "narrow", 1)
    cross_sum = jnp.concatenate(
        [jnp.where(core == 0, cross_half, other), jnp.where(core == 0, other, cross_half)], axis=0
    )
    return cross_sum, gram_total


def local(embeddings, sketch_seed, list_ids, owner_map):
    row_count = embeddings.shape[0]
    rank = sketch_seed.shape[1]
    cores = lax.axis_size("narrow")
    chips = lax.axis_size("y") * lax.axis_size("z") * lax.axis_size("x")
    dev_count = cores * chips
    core = lax.axis_index("narrow")
    seed_matrix = sketch_seed.astype(jnp.bfloat16)
    sketch = jnp.dot(embeddings, seed_matrix, preferred_element_type=jnp.float32).astype(
        jnp.bfloat16
    )
    row_dims = (((0,), (0,)), ((), ()))
    gram_part = lax.dot_general(sketch, sketch, row_dims, preferred_element_type=jnp.float32)
    cross_part = lax.dot_general(embeddings, sketch, row_dims, preferred_element_type=jnp.float32)
    cross_sum, gram_total = sum_over_slice(cross_part, gram_part)

    capacity = 4 * row_count // dev_count
    owners = owner_map[list_ids]
    onehot = owners[:, None] == jnp.arange(dev_count, dtype=jnp.int32)[None, :]
    ids = jnp.arange(row_count, dtype=jnp.int32)
    earlier = (ids[:, None] > ids[None, :]).astype(jnp.bfloat16)
    before = jnp.dot(earlier, onehot.astype(jnp.bfloat16), preferred_element_type=jnp.float32)
    slot_index = jnp.sum(jnp.where(onehot, before, 0.0), axis=1).astype(jnp.int32)
    dest_index = owners * capacity + slot_index

    labels = jnp.full((dev_count * capacity,), -1, jnp.int32).at[dest_index].set(list_ids)
    labels = labels.reshape(dev_count, capacity)
    arrived_labels = lax.all_to_all(labels, ALL, 0, 0, tiled=True)

    both_dest = jnp.stack([dest_index, shift(dest_index, "narrow", 1)])
    both_owner = both_dest // capacity
    source = jnp.stack([core, 1 - core])[:, None]
    target = ((both_owner % chips) * cores + source) * capacity + both_dest % capacity
    target = jnp.where(both_owner // chips == core, target, -1).reshape(cores * row_count)

    inverse = invert_factor(gram_total)
    moment = dot_f32(cross_sum, cross_sum, row_dims)
    weight = whiten_weight(inverse, moment)
    projector = dot_f32(cross_sum, weight).astype(jnp.bfloat16)
    reduced = jnp.dot(embeddings, projector, preferred_element_type=jnp.float32).astype(
        jnp.bfloat16
    )
    both_rows = jnp.concatenate([reduced, shift(reduced, "narrow", 1)], axis=0)
    send_rows = place_rows(target, both_rows, chips * cores * capacity)
    send_rows = send_rows.reshape(chips, cores * capacity, rank)
    arrived = lax.all_to_all(send_rows, ("y", "z", "x"), 0, 0, tiled=True)
    arrived = arrived.reshape(chips, cores, capacity, rank).transpose(1, 0, 2, 3)
    return (
        arrived.reshape(1, dev_count, capacity, rank),
        arrived_labels.reshape(1, dev_count, capacity),
    )


def solution(mesh):
    grid = Mesh(mesh.devices.reshape(2, 4, 8, 4), ALL)
    in_specs = (P(ALL, None), P(), P(ALL), P())
    out_specs = (P(ALL, None, None, None), P(ALL, None, None))
    return jax.shard_map(local, mesh=grid, in_specs=in_specs, out_specs=out_specs, check_vma=False)
```

```python
import functools

import jax
import jax.numpy as jnp
from jax import lax
from jax.experimental import pallas as pl
from jax.experimental.pallas import tpu as pltpu
from jax.sharding import Mesh
from jax.sharding import PartitionSpec as P

NS_STEPS = 6
BLOCK = 32
TILE = 8
ALL = ("narrow", "y", "z", "x")
PLANE = ("y", "z")
HIGHEST = lax.Precision.HIGHEST
ROW_DIMS = (((0,), (0,)), ((), ()))


def dot_f32(a, b, dims=(((1,), (0,)), ((), ()))):
    return lax.dot_general(a, b, dims, precision=HIGHEST, preferred_element_type=jnp.float32)


def invert_kernel(spot_ref, *refs):
    parts, inverse_ref, work_ref = refs[:-2], refs[-2], refs[-1]
    rank = inverse_ref.shape[0]
    height = rank // len(parts)
    row_ids = lax.broadcasted_iota(jnp.int32, (rank, rank), 0)
    col_ids = lax.broadcasted_iota(jnp.int32, (rank, rank), 1)
    for step, part_ref in enumerate(parts):
        place = lax.rem(spot_ref[0] + len(parts) - step, len(parts))
        work_ref[pl.ds(pl.multiple_of(place * height, height), height), :rank] = part_ref[...]
    work_ref[:, rank:] = (row_ids == col_ids).astype(jnp.float32)
    lane = lax.broadcasted_iota(jnp.int32, (BLOCK, 128), 1)
    row = lax.broadcasted_iota(jnp.int32, (BLOCK, 128), 0)
    panel_lane = lax.broadcasted_iota(jnp.int32, (BLOCK, rank), 1)

    def block_step(step, carry):
        start = pl.multiple_of(step * BLOCK, BLOCK)
        panel = work_ref[pl.ds(start, BLOCK), :]
        shifted = pltpu.roll(panel[:, :rank], rank - start, 1)[:, :128]
        rest = jnp.where(lane < BLOCK, shifted, (lane - BLOCK == row).astype(jnp.float32))
        done = []
        for tile in range(BLOCK // TILE):
            height = BLOCK - tile * TILE
            sub = lax.broadcasted_iota(jnp.int32, (height, 128), 0)
            columns = [
                jnp.broadcast_to(rest[:, tile * TILE + j : tile * TILE + j + 1], (height, 128))
                for j in range(TILE)
            ]
            for j in range(TILE):
                pivot = columns[j][j : j + 1, :]
                scale = lax.rsqrt(pivot)
                scale = scale * (1.5 - 0.5 * (pivot * scale) * scale)
                below = jnp.where(sub > j, columns[j] * scale, 0.0)
                lead = rest[j : j + 1, :] * scale
                done.append(lead)
                rest = rest - below * lead
                for m in range(j + 1, TILE):
                    columns[m] = columns[m] - below * (columns[m][j : j + 1, :] * scale)
            rest = rest[TILE:, :]
        solved = jnp.concatenate(done, axis=0)
        small = pltpu.roll(solved, 128 - BLOCK, 1)[:, :BLOCK]
        panel = dot_f32(small, panel)
        inverse_ref[pl.ds(start, BLOCK), :] = panel[:, rank:]
        later = jnp.where(panel_lane >= start + BLOCK, panel[:, :rank], 0.0)
        work_ref[...] -= dot_f32(later, panel, (((0,), (0,)), ((), ())))
        return carry

    lax.fori_loop(0, rank // BLOCK, block_step, 0)


def invert_factor(spot, parts):
    rank = parts[0].shape[1]
    return pl.pallas_call(
        invert_kernel,
        in_specs=[pl.BlockSpec(memory_space=pltpu.SMEM)]
        + [pl.BlockSpec(memory_space=pltpu.VMEM)] * len(parts),
        out_shape=jax.ShapeDtypeStruct((rank, rank), jnp.float32),
        scratch_shapes=[pltpu.VMEM((rank, 2 * rank), jnp.float32)],
        cost_estimate=pl.CostEstimate(flops=20_000_000_000, bytes_accessed=524288, transcendentals=0),
        name="invert_factor",
    )(spot, *parts)


def moment_kernel(*refs):
    total = None
    for part_ref in refs[:-1]:
        part = part_ref[...]
        term = dot_f32(part, part, ROW_DIMS)
        total = term if total is None else total + term
    refs[-1][...] = total


def moment_of(parts):
    rank = parts[0].shape[1]
    return pl.pallas_call(
        moment_kernel,
        out_shape=jax.ShapeDtypeStruct((rank, rank), jnp.float32),
        cost_estimate=pl.CostEstimate(flops=4_000_000_000, bytes_accessed=2359296, transcendentals=0),
        name="moment_of",
    )(*parts)


def whiten_kernel(spot_ref, inverse_ref, moment_ref, other_ref, *refs):
    parts, out_ref = refs[:-1], refs[-1]
    inverse = inverse_ref[...]
    rank = inverse.shape[0]
    moment = moment_ref[...] + other_ref[...]
    cov_total = dot_f32(dot_f32(inverse, moment), inverse, (((1,), (1,)), ((), ())))
    row_ids = lax.broadcasted_iota(jnp.int32, (rank, rank), 0)
    col_ids = lax.broadcasted_iota(jnp.int32, (rank, rank), 1)
    eye_matrix = (row_ids == col_ids).astype(jnp.float32)
    trace_value = jnp.sum(cov_total * eye_matrix, axis=(0, 1), keepdims=True)
    left_iter = cov_total / trace_value
    right_iter = 1.5 * eye_matrix - 0.5 * left_iter
    left_iter = dot_f32(left_iter, right_iter)
    for step_index in range(1, NS_STEPS):
        middle = 1.5 * eye_matrix - 0.5 * dot_f32(right_iter, left_iter)
        if step_index < NS_STEPS - 1:
            left_iter = dot_f32(left_iter, middle)
        right_iter = dot_f32(middle, right_iter)
    factor = right_iter / jnp.sqrt(trace_value)
    weight = dot_f32(inverse, factor, ROW_DIMS)
    height = out_ref.shape[0] // len(parts)
    for step, part_ref in enumerate(parts):
        place = lax.rem(spot_ref[0] + len(parts) - step, len(parts))
        rows = pl.ds(pl.multiple_of(place * height, height), height)
        out_ref[rows, :] = dot_f32(part_ref[...], weight).astype(jnp.bfloat16)


def project_half(spot, inverse, moment, other, parts):
    chunk, rank = parts[0].shape
    return pl.pallas_call(
        whiten_kernel,
        in_specs=[pl.BlockSpec(memory_space=pltpu.SMEM)]
        + [pl.BlockSpec(memory_space=pltpu.VMEM)] * (3 + len(parts)),
        out_shape=jax.ShapeDtypeStruct((chunk * len(parts), rank), jnp.bfloat16),
        cost_estimate=pl.CostEstimate(flops=12_000_000_000, bytes_accessed=4194304, transcendentals=0),
        name="project_half",
    )(spot, inverse, moment, other, *parts)


def cross_kernel(half_ref, rows_ref, sketch_ref, cross_ref, *rest):
    sketch = sketch_ref[...]
    cross_ref[...] = lax.dot_general(
        rows_ref[...], sketch, ROW_DIMS, preferred_element_type=jnp.float32
    )
    if rest:

        @pl.when(pl.program_id(0) == 0)
        def _():
            rest[0][...] = lax.dot_general(
                sketch, sketch, ROW_DIMS, preferred_element_type=jnp.float32
            )


def cross_of_half(half, embeddings, sketch, with_gram):
    depth, dim = embeddings.shape
    rank = sketch.shape[1]
    width, steps = 512, dim // 2 // 512
    out_shape = [jax.ShapeDtypeStruct((dim // 2, rank), jnp.float32)]
    out_specs = [pl.BlockSpec((width, rank), lambda i, half: (i, 0))]
    if with_gram:
        out_shape.append(jax.ShapeDtypeStruct((rank, rank), jnp.float32))
        out_specs.append(pl.BlockSpec((rank, rank), lambda i, half: (0, 0)))
    return pl.pallas_call(
        cross_kernel,
        grid_spec=pltpu.PrefetchScalarGridSpec(
            num_scalar_prefetch=1,
            grid=(steps,),
            in_specs=[
                pl.BlockSpec((depth, width), lambda i, half: (0, half[0] * steps + i)),
                pl.BlockSpec((depth, rank), lambda i, half: (0, 0)),
            ],
            out_specs=out_specs,
        ),
        out_shape=out_shape,
        cost_estimate=pl.CostEstimate(
            flops=depth * dim * rank, bytes_accessed=depth * dim + dim * rank * 2, transcendentals=0
        ),
        name="cross_of_half",
    )(half, embeddings, sketch)


def product_kernel(half_ref, rows_ref, basis_ref, *refs):
    begin_ref, out_ref, sum_ref = (None,) * (3 - len(refs)) + refs
    step = pl.program_id(0)
    term = jnp.dot(rows_ref[...], basis_ref[...], preferred_element_type=jnp.float32)

    @pl.when(step == 0)
    def _():
        sum_ref[...] = term if begin_ref is None else term + begin_ref[...]

    @pl.when(step > 0)
    def _():
        sum_ref[...] += term

    @pl.when(step == pl.num_programs(0) - 1)
    def _():
        out_ref[...] = sum_ref[...].astype(out_ref.dtype)


def product_of_half(half, embeddings, basis, begin, out_type):
    depth, dim = embeddings.shape
    rank = basis.shape[1]
    width, steps = 512, dim // 2 // 512
    whole = pl.BlockSpec((depth, rank), lambda i, half: (0, 0))
    extra = [] if begin is None else [begin]
    return pl.pallas_call(
        product_kernel,
        grid_spec=pltpu.PrefetchScalarGridSpec(
            num_scalar_prefetch=1,
            grid=(steps,),
            in_specs=[
                pl.BlockSpec((depth, width), lambda i, half: (0, half[0] * steps + i)),
                pl.BlockSpec((width, rank), lambda i, half: (i, 0)),
            ]
            + [whole] * len(extra),
            out_specs=whole,
            scratch_shapes=[pltpu.VMEM((depth, rank), jnp.float32)],
        ),
        out_shape=jax.ShapeDtypeStruct((depth, rank), out_type),
        cost_estimate=pl.CostEstimate(
            flops=depth * dim * rank, bytes_accessed=depth * dim + dim * rank, transcendentals=0
        ),
        name="product_of_half",
    )(half, embeddings, basis, *extra)


def pack_kernel(keep_ref, got_ref, gram_ref, gram_got_ref, out_ref):
    count, _, rank = out_ref.shape
    cross = keep_ref[...] + got_ref[...]
    gram = gram_ref[...] + gram_got_ref[...]
    pieces = [cross.reshape(count, -1, rank)]
    for term in range(3):
        short = gram.astype(jnp.bfloat16).astype(jnp.float32)
        pieces.append(short.reshape(count, -1, rank))
        gram = gram - short
    filled = sum(p.shape[1] for p in pieces)
    pieces.append(jnp.zeros((count, out_ref.shape[1] - filled, rank), jnp.float32))
    out_ref[...] = jnp.concatenate(pieces, axis=1).astype(jnp.bfloat16)


def pack_partials(keep, got, gram, gram_got, chips):
    half, rank = keep.shape
    steps = 8
    rows = half // chips + 3 * rank // chips
    rows += -rows % 8
    return pl.pallas_call(
        pack_kernel,
        grid=(steps,),
        in_specs=[pl.BlockSpec((half // steps, rank), lambda i: (i, 0))] * 2
        + [pl.BlockSpec((rank // steps, rank), lambda i: (i, 0))] * 2,
        out_specs=pl.BlockSpec((chips // steps, rows, rank), lambda i: (i, 0, 0)),
        out_shape=jax.ShapeDtypeStruct((chips, rows, rank), jnp.bfloat16),
        cost_estimate=pl.CostEstimate(flops=4000000, bytes_accessed=6000000, transcendentals=0),
        name="pack_partials",
    )(keep, got, gram, gram_got)


def total_kernel(piece, gram_piece, parts_ref, out_ref):
    total = jnp.sum(parts_ref[...].astype(jnp.float32), axis=0)
    gram = sum(total[piece + t * gram_piece : piece + (t + 1) * gram_piece] for t in range(3))
    fill = jnp.zeros((out_ref.shape[1] - piece - gram_piece, total.shape[1]), jnp.float32)
    mine = jnp.concatenate([total[:piece], gram, fill], axis=0)
    out_ref[...] = jnp.broadcast_to(mine[None], out_ref.shape)


def total_partials(parts, piece, gram_piece, copies):
    rows = piece + gram_piece
    rows += -rows % 8
    return pl.pallas_call(
        functools.partial(total_kernel, piece, gram_piece),
        out_shape=jax.ShapeDtypeStruct((copies, rows, parts.shape[2]), jnp.float32),
        cost_estimate=pl.CostEstimate(flops=1000000, bytes_accessed=1600000, transcendentals=0),
        name="total_partials",
    )(parts)


def place_kernel(target_ref, first_ref, second_ref, out_ref):
    tile = out_ref.shape[0]
    base = pl.program_id(0) * tile
    depth = first_ref.shape[0]
    slots = base + lax.broadcasted_iota(jnp.int32, (tile, depth), 0)
    total = None
    for part, rows_ref in enumerate((first_ref, second_ref)):
        onehot = (slots == target_ref[part : part + 1, :]).astype(jnp.bfloat16)
        term = jnp.dot(onehot, rows_ref[...], preferred_element_type=jnp.float32)
        total = term if total is None else total + term
    out_ref[...] = total.astype(jnp.bfloat16)


def place_rows(target, first, second, count):
    tile = 512
    depth, width = first.shape
    return pl.pallas_call(
        place_kernel,
        grid=(count // tile,),
        in_specs=[pl.BlockSpec((2, depth), lambda i: (0, 0))]
        + [pl.BlockSpec((depth, width), lambda i: (0, 0))] * 2,
        out_specs=pl.BlockSpec((tile, width), lambda i: (i, 0)),
        out_shape=jax.ShapeDtypeStruct((count, width), jnp.bfloat16),
        cost_estimate=pl.CostEstimate(
            flops=4 * count * depth * width, bytes_accessed=4 * count * width, transcendentals=0
        ),
        name="place_rows",
    )(target, first, second)


def shift(value, axis, step):
    size = lax.axis_size(axis)
    return lax.ppermute(value, axis, [(i, (i + step) % size) for i in range(size)])


def local(embeddings, sketch_seed, list_ids, owner_map):
    row_count, dim = embeddings.shape
    rank = sketch_seed.shape[1]
    cores, line = lax.axis_size("narrow"), lax.axis_size("x")
    plane = lax.axis_size("y") * lax.axis_size("z")
    chips = plane * line
    dev_count = cores * chips
    core = lax.axis_index("narrow")
    spot = lax.axis_index("x").reshape(1)
    own_half, other_half = core.reshape(1), (1 - core).reshape(1)
    piece, gram_piece = dim // dev_count, rank // chips
    seed_matrix = sketch_seed.astype(jnp.bfloat16)
    sketch = jnp.dot(embeddings, seed_matrix, preferred_element_type=jnp.float32).astype(
        jnp.bfloat16
    )

    give, gram_part = cross_of_half(other_half, embeddings, sketch, True)
    got, gram_got = shift(give, "narrow", 1), shift(gram_part, "narrow", 1)
    (keep,) = cross_of_half(own_half, embeddings, sketch, False)
    packed = pack_partials(keep, got, gram_part, gram_got, chips)
    packed = lax.all_to_all(packed, ("x", "y", "z"), 0, 0, tiled=True)

    packed = total_partials(packed, piece, gram_piece, plane)
    packed = lax.all_to_all(packed, PLANE, 0, 0, tiled=True)
    gram_line = packed[:, piece : piece + gram_piece].reshape(-1, rank)
    gram_parts = [gram_line] + [shift(gram_line, "x", step) for step in range(1, line)]
    packed, gram_parts[1] = lax.optimization_barrier((packed, gram_parts[1]))
    cross_line = packed[:, :piece].reshape(-1, rank)
    cross_parts = [cross_line] + [shift(cross_line, "x", step) for step in range(1, line)]

    capacity = 4 * row_count // dev_count
    owners = owner_map[list_ids]
    onehot = owners[:, None] == jnp.arange(dev_count, dtype=jnp.int32)[None, :]
    ids = jnp.arange(row_count, dtype=jnp.int32)
    earlier = (ids[:, None] > ids[None, :]).astype(jnp.bfloat16)
    before = jnp.dot(earlier, onehot.astype(jnp.bfloat16), preferred_element_type=jnp.float32)
    slot_index = jnp.sum(jnp.where(onehot, before, 0.0), axis=1).astype(jnp.int32)
    dest_index = owners * capacity + slot_index

    labels = jnp.full((dev_count * capacity,), -1, jnp.int32).at[dest_index].set(list_ids)
    labels = labels.reshape(dev_count, capacity)
    arrived_labels = lax.all_to_all(labels, ALL, 0, 0, tiled=True)

    both_dest = jnp.stack([dest_index, shift(dest_index, "narrow", 1)])
    both_owner = both_dest // capacity
    source = jnp.stack([core, 1 - core])[:, None]
    target = ((both_owner % chips) * cores + source) * capacity + both_dest % capacity
    target = jnp.where(both_owner // chips == core, target, -1)

    inverse = invert_factor(spot, gram_parts)
    moment = moment_of(cross_parts)
    basis = project_half(spot, inverse, moment, shift(moment, "narrow", 1), cross_parts)
    other_basis = shift(basis, "narrow", 1)
    begun = product_of_half(own_half, embeddings, basis, None, jnp.float32)
    reduced = product_of_half(other_half, embeddings, other_basis, begun, jnp.bfloat16)
    send_rows = place_rows(
        target, reduced, shift(reduced, "narrow", 1), chips * cores * capacity
    )
    send_rows = send_rows.reshape(chips, cores * capacity, rank)
    arrived = lax.all_to_all(send_rows, ("y", "z", "x"), 0, 0, tiled=True)
    arrived = arrived.reshape(chips, cores, capacity, rank).transpose(1, 0, 2, 3)
    return (
        arrived.reshape(1, dev_count, capacity, rank),
        arrived_labels.reshape(1, dev_count, capacity),
    )


def solution(mesh):
    grid = Mesh(mesh.devices.reshape(2, 4, 8, 4), ALL)
    in_specs = (P(ALL, None), P(), P(ALL), P())
    out_specs = (P(ALL, None, None, None), P(ALL, None, None))
    return jax.shard_map(local, mesh=grid, in_specs=in_specs, out_specs=out_specs, check_vma=False)
```

```python
import functools

import jax
import jax.numpy as jnp
from jax import lax
from jax.experimental import pallas as pl
from jax.experimental.pallas import tpu as pltpu
from jax.sharding import Mesh
from jax.sharding import PartitionSpec as P

NS_STEPS = 6
BLOCK = 32
TILE = 8
ALL = ("narrow", "y", "z", "x")
PLANE = ("y", "z")
HIGHEST = lax.Precision.HIGHEST
ROW_DIMS = (((0,), (0,)), ((), ()))


def dot_f32(a, b, dims=(((1,), (0,)), ((), ()))):
    return lax.dot_general(a, b, dims, precision=HIGHEST, preferred_element_type=jnp.float32)


def split_two(a):
    high = a.astype(jnp.bfloat16)
    return high, (a - high.astype(jnp.float32)).astype(jnp.bfloat16)


def dot_split(a, b):
    (ah, al), (bh, bl) = a, b
    mul = functools.partial(jnp.dot, preferred_element_type=jnp.float32)
    return mul(ah, bh) + (mul(ah, bl) + mul(al, bh))


def invert_kernel(spot_ref, *refs):
    parts, inverse_ref, work_ref = refs[:-2], refs[-2], refs[-1]
    rank = inverse_ref.shape[0]
    height = rank // len(parts)
    row_ids = lax.broadcasted_iota(jnp.int32, (rank, rank), 0)
    col_ids = lax.broadcasted_iota(jnp.int32, (rank, rank), 1)
    for step, part_ref in enumerate(parts):
        place = lax.rem(spot_ref[0] + len(parts) - step, len(parts))
        work_ref[pl.ds(pl.multiple_of(place * height, height), height), :rank] = part_ref[...]
    work_ref[:, rank:] = (row_ids == col_ids).astype(jnp.float32)
    lane = lax.broadcasted_iota(jnp.int32, (BLOCK, 128), 1)
    row = lax.broadcasted_iota(jnp.int32, (BLOCK, 128), 0)
    panel_lane = lax.broadcasted_iota(jnp.int32, (BLOCK, rank), 1)

    def block_step(step, carry):
        start = pl.multiple_of(step * BLOCK, BLOCK)
        panel = work_ref[pl.ds(start, BLOCK), :]
        shifted = pltpu.roll(panel[:, :rank], rank - start, 1)[:, :128]
        rest = jnp.where(lane < BLOCK, shifted, (lane - BLOCK == row).astype(jnp.float32))
        done = []
        for tile in range(BLOCK // TILE):
            height = BLOCK - tile * TILE
            sub = lax.broadcasted_iota(jnp.int32, (height, 128), 0)
            columns = [
                jnp.broadcast_to(rest[:, tile * TILE + j : tile * TILE + j + 1], (height, 128))
                for j in range(TILE)
            ]
            for j in range(TILE):
                pivot = columns[j][j : j + 1, :]
                scale = lax.rsqrt(pivot)
                scale = scale * (1.5 - 0.5 * (pivot * scale) * scale)
                below = jnp.where(sub > j, columns[j] * scale, 0.0)
                lead = rest[j : j + 1, :] * scale
                done.append(lead)
                rest = rest - below * lead
                for m in range(j + 1, TILE):
                    columns[m] = columns[m] - below * (columns[m][j : j + 1, :] * scale)
            rest = rest[TILE:, :]
        solved = jnp.concatenate(done, axis=0)
        small = pltpu.roll(solved, 128 - BLOCK, 1)[:, :BLOCK]
        panel = dot_f32(small, panel)
        inverse_ref[pl.ds(start, BLOCK), :] = panel[:, rank:]
        later = jnp.where(panel_lane >= start + BLOCK, panel[:, :rank], 0.0)
        work_ref[...] -= dot_f32(later, panel, (((0,), (0,)), ((), ())))
        return carry

    lax.fori_loop(0, rank // BLOCK, block_step, 0)


def invert_factor(spot, parts):
    rank = parts[0].shape[1]
    return pl.pallas_call(
        invert_kernel,
        in_specs=[pl.BlockSpec(memory_space=pltpu.SMEM)]
        + [pl.BlockSpec(memory_space=pltpu.VMEM)] * len(parts),
        out_shape=jax.ShapeDtypeStruct((rank, rank), jnp.float32),
        scratch_shapes=[pltpu.VMEM((rank, 2 * rank), jnp.float32)],
        cost_estimate=pl.CostEstimate(flops=20_000_000_000, bytes_accessed=524288, transcendentals=0),
        name="invert_factor",
    )(spot, *parts)


def moment_kernel(*refs):
    total = None
    for part_ref in refs[:-1]:
        part = part_ref[...]
        term = dot_f32(part, part, ROW_DIMS)
        total = term if total is None else total + term
    refs[-1][...] = total


def moment_of(parts):
    rank = parts[0].shape[1]
    return pl.pallas_call(
        moment_kernel,
        out_shape=jax.ShapeDtypeStruct((rank, rank), jnp.float32),
        cost_estimate=pl.CostEstimate(flops=4_000_000_000, bytes_accessed=2359296, transcendentals=0),
        name="moment_of",
    )(*parts)


def whiten_kernel(spot_ref, inverse_ref, moment_ref, other_ref, *refs):
    parts, out_ref = refs[:-1], refs[-1]
    inverse = inverse_ref[...]
    rank = inverse.shape[0]
    moment = moment_ref[...] + other_ref[...]
    cov_total = dot_f32(dot_f32(inverse, moment), inverse, (((1,), (1,)), ((), ())))
    row_ids = lax.broadcasted_iota(jnp.int32, (rank, rank), 0)
    col_ids = lax.broadcasted_iota(jnp.int32, (rank, rank), 1)
    eye_matrix = (row_ids == col_ids).astype(jnp.float32)
    trace_value = jnp.sum(cov_total * eye_matrix, axis=(0, 1), keepdims=True)
    left_iter = cov_total / trace_value
    right_iter = 1.5 * eye_matrix - 0.5 * left_iter
    right_parts = split_two(right_iter)
    left_parts = split_two(dot_split(split_two(left_iter), right_parts))
    for step_index in range(1, NS_STEPS):
        middle = split_two(1.5 * eye_matrix - 0.5 * dot_split(right_parts, left_parts))
        right_iter = dot_split(middle, right_parts)
        if step_index < NS_STEPS - 1:
            left_parts = split_two(dot_split(left_parts, middle))
            right_parts = split_two(right_iter)
    factor = right_iter / jnp.sqrt(trace_value)
    weight = split_two(dot_f32(inverse, factor, ROW_DIMS))
    height = out_ref.shape[0] // len(parts)
    for step, part_ref in enumerate(parts):
        place = lax.rem(spot_ref[0] + len(parts) - step, len(parts))
        rows = pl.ds(pl.multiple_of(place * height, height), height)
        out_ref[rows, :] = dot_split(split_two(part_ref[...]), weight).astype(jnp.bfloat16)


def project_half(spot, inverse, moment, other, parts):
    chunk, rank = parts[0].shape
    return pl.pallas_call(
        whiten_kernel,
        in_specs=[pl.BlockSpec(memory_space=pltpu.SMEM)]
        + [pl.BlockSpec(memory_space=pltpu.VMEM)] * (3 + len(parts)),
        out_shape=jax.ShapeDtypeStruct((chunk * len(parts), rank), jnp.bfloat16),
        cost_estimate=pl.CostEstimate(flops=12_000_000_000, bytes_accessed=4194304, transcendentals=0),
        name="project_half",
    )(spot, inverse, moment, other, *parts)


def chunk_kernel(spot_ref, rows_ref, sketch_ref, give_ref, keep_ref):
    chunk, core = spot_ref[0], spot_ref[1]
    rank = sketch_ref.shape[1]
    width = give_ref.shape[1] - 128
    half = rows_ref.shape[1] // 2
    sketch = sketch_ref[...]
    mul = functools.partial(
        lax.dot_general, dimension_numbers=ROW_DIMS, preferred_element_type=jnp.float32
    )
    gram = mul(sketch, sketch)
    gram = pltpu.roll(gram, rank - chunk * (rank * width // half), 1)[:, :128]
    for out_ref, place in ((give_ref, 1 - core), (keep_ref, core)):
        columns = pl.ds(pl.multiple_of(place * half + chunk * width, width), width)
        out_ref[:, :width] = mul(sketch, rows_ref[:, columns])
        out_ref[:, width:] = gram


def cross_chunk(spot, embeddings, sketch, chunks):
    depth, dim = embeddings.shape
    rank = sketch.shape[1]
    width = dim // 2 // chunks
    shape = jax.ShapeDtypeStruct((rank, width + 128), jnp.float32)
    return pl.pallas_call(
        chunk_kernel,
        in_specs=[pl.BlockSpec(memory_space=pltpu.SMEM)]
        + [pl.BlockSpec(memory_space=pltpu.VMEM)] * 2,
        out_shape=[shape, shape],
        compiler_params=pltpu.CompilerParams(vmem_limit_bytes=32 * 2**20),
        cost_estimate=pl.CostEstimate(
            flops=2 * depth * rank * (2 * width + rank), bytes_accessed=3000000, transcendentals=0
        ),
        name="cross_chunk",
    )(spot, embeddings, sketch)


def line_kernel(gram_piece, *refs):
    parts, out_ref = refs[:-1], refs[-1]
    plane, _, rank = out_ref.shape
    width = parts[0].shape[1] - 128
    total = parts[0][...] + parts[1][...]
    for part_ref in parts[2:]:
        total = total + part_ref[...]
    piece = width // plane
    out_ref[:, :piece, :] = total[:, :width].T.reshape(plane, piece, rank)
    gram = total[:, width:].T[: plane * gram_piece].reshape(plane, gram_piece, rank)
    fill = jnp.zeros((plane, out_ref.shape[1] - piece - gram_piece, rank), jnp.float32)
    out_ref[:, piece:, :] = jnp.concatenate([gram, fill], axis=1)


def line_total(parts, plane, gram_piece):
    rank, width = parts[0].shape
    rows = (width - 128) // plane + gram_piece
    rows += -rows % 8
    return pl.pallas_call(
        functools.partial(line_kernel, gram_piece),
        out_shape=jax.ShapeDtypeStruct((plane, rows, rank), jnp.float32),
        compiler_params=pltpu.CompilerParams(vmem_limit_bytes=32 * 2**20),
        cost_estimate=pl.CostEstimate(flops=1000000, bytes_accessed=4000000, transcendentals=0),
        name="line_total",
    )(*parts)


def plane_kernel(parts_ref, out_ref):
    out_ref[...] = jnp.broadcast_to(jnp.sum(parts_ref[...], axis=0, keepdims=True), out_ref.shape)


def plane_total(parts):
    return pl.pallas_call(
        plane_kernel,
        out_shape=jax.ShapeDtypeStruct(parts.shape, jnp.float32),
        cost_estimate=pl.CostEstimate(flops=1000000, bytes_accessed=1600000, transcendentals=0),
        name="plane_total",
    )(parts)


def product_kernel(core_ref, rows_ref, basis_ref, *refs):
    half, width = basis_ref.shape[0], 512
    total = None if len(refs) == 1 else refs[0][...]
    for step in range(half // width):
        columns = pl.ds(pl.multiple_of(core_ref[0] * half + step * width, width), width)
        basis = basis_ref[step * width : (step + 1) * width, :]
        term = jnp.dot(rows_ref[:, columns], basis, preferred_element_type=jnp.float32)
        total = term if total is None else total + term
    refs[-1][...] = total.astype(refs[-1].dtype)


def product_of_half(half, embeddings, basis, begin, out_type):
    depth, dim = embeddings.shape
    rank = basis.shape[1]
    extra = [] if begin is None else [begin]
    return pl.pallas_call(
        product_kernel,
        in_specs=[pl.BlockSpec(memory_space=pltpu.SMEM)]
        + [pl.BlockSpec(memory_space=pltpu.VMEM)] * (2 + len(extra)),
        out_shape=jax.ShapeDtypeStruct((depth, rank), out_type),
        compiler_params=pltpu.CompilerParams(vmem_limit_bytes=32 * 2**20),
        cost_estimate=pl.CostEstimate(
            flops=depth * dim * rank, bytes_accessed=depth * dim + dim * rank, transcendentals=0
        ),
        name="product_of_half",
    )(half, embeddings, basis, *extra)


def route_kernel(capacity, ids_ref, map_ref, dest_ref, label_ref):
    ids = ids_ref[...]
    count, (high, low) = ids.shape[1], map_ref.shape
    owner_count = label_ref.shape[0]
    bf16 = jnp.bfloat16

    def rows_of(size):
        return lax.broadcasted_iota(jnp.int32, (size, count), 0)

    picked = (rows_of(high) == ids // low).astype(bf16)
    found = lax.dot_general(
        map_ref[...].astype(bf16), picked, ROW_DIMS, preferred_element_type=jnp.float32
    )
    owner = jnp.sum(jnp.where(rows_of(low) == ids % low, found, 0.0), axis=0, keepdims=True)
    owner = owner.astype(jnp.int32)
    mine = rows_of(owner_count) == owner
    order = lax.broadcasted_iota(jnp.int32, (count, count), 1)
    earlier = (lax.broadcasted_iota(jnp.int32, (count, count), 0) < order).astype(bf16)
    onehot = mine.astype(bf16)
    before = jnp.dot(onehot, earlier, preferred_element_type=jnp.float32)
    slot = jnp.sum(jnp.where(mine, before, 0.0), axis=0, keepdims=True).astype(jnp.int32)
    dest_ref[...] = owner * capacity + slot
    value = ids + 1
    labels = None
    for digit in range(3):
        short = (value // 128**digit) % 128
        spread = jnp.where(rows_of(16) == slot, short.astype(jnp.float32), 0.0).astype(bf16)
        term = lax.dot_general(
            onehot, spread, (((1,), (1,)), ((), ())), preferred_element_type=jnp.float32
        )
        term = term.astype(jnp.int32) * 128**digit
        labels = term if labels is None else labels + term
    label_ref[...] = (labels - 1)[:, :capacity]


def route_rows(list_ids, owner_map, owner_count, capacity):
    count = list_ids.shape[0]
    return pl.pallas_call(
        functools.partial(route_kernel, capacity),
        out_shape=[
            jax.ShapeDtypeStruct((1, count), jnp.int32),
            jax.ShapeDtypeStruct((owner_count, capacity), jnp.int32),
        ],
        compiler_params=pltpu.CompilerParams(vmem_limit_bytes=32 * 2**20),
        cost_estimate=pl.CostEstimate(
            flops=2_000_000_000, bytes_accessed=1048576, transcendentals=0
        ),
        name="route_rows",
    )(list_ids.reshape(1, count), owner_map.reshape(-1, 128))


def place_kernel(target_ref, first_ref, second_ref, out_ref):
    tile = out_ref.shape[0]
    base = pl.program_id(0) * tile
    depth = first_ref.shape[0]
    slots = base + lax.broadcasted_iota(jnp.int32, (tile, depth), 0)
    total = None
    for part, rows_ref in enumerate((first_ref, second_ref)):
        onehot = (slots == target_ref[part : part + 1, :]).astype(jnp.bfloat16)
        term = jnp.dot(onehot, rows_ref[...], preferred_element_type=jnp.float32)
        total = term if total is None else total + term
    out_ref[...] = total.astype(jnp.bfloat16)


def place_rows(target, first, second, count):
    tile = 512
    depth, width = first.shape
    return pl.pallas_call(
        place_kernel,
        grid=(count // tile,),
        in_specs=[pl.BlockSpec((2, depth), lambda i: (0, 0))]
        + [pl.BlockSpec((depth, width), lambda i: (0, 0))] * 2,
        out_specs=pl.BlockSpec((tile, width), lambda i: (i, 0)),
        out_shape=jax.ShapeDtypeStruct((count, width), jnp.bfloat16),
        cost_estimate=pl.CostEstimate(
            flops=4 * count * depth * width, bytes_accessed=4 * count * width, transcendentals=0
        ),
        name="place_rows",
    )(target, first, second)


def shift(value, axis, step):
    size = lax.axis_size(axis)
    return lax.ppermute(value, axis, [(i, (i + step) % size) for i in range(size)])


def local(embeddings, sketch_seed, list_ids, owner_map):
    row_count, dim = embeddings.shape
    rank = sketch_seed.shape[1]
    cores, line = lax.axis_size("narrow"), lax.axis_size("x")
    plane = lax.axis_size("y") * lax.axis_size("z")
    chips = plane * line
    dev_count = cores * chips
    core = lax.axis_index("narrow")
    spot = lax.axis_index("x").reshape(1)
    own_half, other_half = core.reshape(1), (1 - core).reshape(1)
    piece, gram_piece = dim // dev_count, rank // chips
    seed_matrix = sketch_seed.astype(jnp.bfloat16)
    sketch = jnp.dot(embeddings, seed_matrix, preferred_element_type=jnp.float32).astype(
        jnp.bfloat16
    )

    capacity = 4 * row_count // dev_count
    dest_index, labels = route_rows(list_ids, owner_map, dev_count, capacity)

    parts = []
    for step in list(range(1, line)) + [0]:
        where = jnp.stack([(lax.axis_index("x") + step) % line, core])
        give, keep = cross_chunk(where, embeddings, sketch, line)
        got = shift(give, "narrow", 1)
        if step:
            parts.append(shift(keep + got, "x", step))
        else:
            parts += [keep, got]
    labels, parts[0] = lax.optimization_barrier((labels, parts[0]))
    arrived_labels = lax.all_to_all(labels, ALL, 0, 0, tiled=True)

    packed = line_total(parts[::-1], plane, gram_piece)
    packed = plane_total(lax.all_to_all(packed, PLANE, 0, 0, tiled=True))
    packed = lax.all_to_all(packed, PLANE, 0, 0, tiled=True)
    gram_line = packed[:, piece : piece + gram_piece].reshape(-1, rank)
    gram_parts = [gram_line] + [shift(gram_line, "x", step) for step in range(1, line)]
    packed, gram_parts[1] = lax.optimization_barrier((packed, gram_parts[1]))
    cross_line = packed[:, :piece].reshape(-1, rank)
    cross_parts = [cross_line] + [shift(cross_line, "x", step) for step in range(1, line)]

    both_dest = jnp.concatenate([dest_index, shift(dest_index, "narrow", 1)])
    both_owner = both_dest // capacity
    source = jnp.stack([core, 1 - core])[:, None]
    target = ((both_owner % chips) * cores + source) * capacity + both_dest % capacity
    target = jnp.where(both_owner // chips == core, target, -1)

    inverse = invert_factor(spot, gram_parts)
    inverse, cross_parts = lax.optimization_barrier((inverse, cross_parts))
    moment = moment_of(cross_parts)
    basis = project_half(spot, inverse, moment, shift(moment, "narrow", 1), cross_parts)
    other_basis = shift(basis, "narrow", 1)
    begun = product_of_half(own_half, embeddings, basis, None, jnp.float32)
    reduced = product_of_half(other_half, embeddings, other_basis, begun, jnp.bfloat16)
    send_rows = place_rows(
        target, reduced, shift(reduced, "narrow", 1), chips * cores * capacity
    )
    send_rows = send_rows.reshape(chips, cores * capacity, rank)
    arrived = lax.all_to_all(send_rows, ("y", "z", "x"), 0, 0, tiled=True)
    arrived = arrived.reshape(chips, cores, capacity, rank).transpose(1, 0, 2, 3)
    return (
        arrived.reshape(1, dev_count, capacity, rank),
        arrived_labels.reshape(1, dev_count, capacity),
    )


def solution(mesh):
    grid = Mesh(mesh.devices.reshape(2, 4, 8, 4), ALL)
    in_specs = (P(ALL, None), P(), P(ALL), P())
    out_specs = (P(ALL, None, None, None), P(ALL, None, None))
    return jax.shard_map(local, mesh=grid, in_specs=in_specs, out_specs=out_specs, check_vma=False)
```

```python
import functools

import jax
import jax.numpy as jnp
from jax import lax
from jax.experimental import pallas as pl
from jax.experimental.pallas import tpu as pltpu
from jax.sharding import Mesh
from jax.sharding import PartitionSpec as P

NS_STEPS = 6
BLOCK = 64
TILE = 8
ALL = ("narrow", "y", "z", "x")
PLANE = ("y", "z")
HIGHEST = lax.Precision.HIGHEST
ROW_DIMS = (((0,), (0,)), ((), ()))
SLOTS = 16
GRANT = pltpu.CompilerParams(vmem_limit_bytes=16 * 2**20)


def dot_f32(a, b, dims=(((1,), (0,)), ((), ()))):
    return lax.dot_general(a, b, dims, precision=HIGHEST, preferred_element_type=jnp.float32)


def split_two(a):
    high = a.astype(jnp.bfloat16)
    return high, (a - high.astype(jnp.float32)).astype(jnp.bfloat16)


def dot_split(a, b):
    (ah, al), (bh, bl) = a, b
    mul = functools.partial(jnp.dot, preferred_element_type=jnp.float32)
    return mul(ah, bh) + (mul(ah, bl) + mul(al, bh))


def invert_kernel(spot_ref, *refs):
    parts, inverse_ref, work_ref = refs[:-2], refs[-2], refs[-1]
    rank = inverse_ref.shape[0]
    height = rank // len(parts)
    row_ids = lax.broadcasted_iota(jnp.int32, (rank, rank), 0)
    col_ids = lax.broadcasted_iota(jnp.int32, (rank, rank), 1)
    for step, part_ref in enumerate(parts):
        place = lax.rem(spot_ref[0] + len(parts) - step, len(parts))
        work_ref[pl.ds(pl.multiple_of(place * height, height), height), :rank] = part_ref[...]
    work_ref[:, rank:] = (row_ids == col_ids).astype(jnp.float32)
    lane = lax.broadcasted_iota(jnp.int32, (BLOCK, 128), 1)
    row = lax.broadcasted_iota(jnp.int32, (BLOCK, 128), 0)
    panel_lane = lax.broadcasted_iota(jnp.int32, (BLOCK, rank), 1)

    def block_step(step, carry):
        start = pl.multiple_of(step * BLOCK, BLOCK)
        panel = work_ref[pl.ds(start, BLOCK), :]
        shifted = pltpu.roll(panel[:, :rank], rank - start, 1)[:, :128]
        rest = jnp.where(lane < BLOCK, shifted, (lane - BLOCK == row).astype(jnp.float32))
        done = []
        for tile in range(BLOCK // TILE):
            height = BLOCK - tile * TILE
            sub = lax.broadcasted_iota(jnp.int32, (height, 128), 0)
            columns = [
                jnp.broadcast_to(rest[:, tile * TILE + j : tile * TILE + j + 1], (height, 128))
                for j in range(TILE)
            ]
            for j in range(TILE):
                pivot = columns[j][j : j + 1, :]
                scale = lax.rsqrt(pivot)
                scale = scale * (1.5 - 0.5 * (pivot * scale) * scale)
                below = jnp.where(sub > j, columns[j] * scale, 0.0)
                lead = rest[j : j + 1, :] * scale
                done.append(lead)
                rest = rest - below * lead
                for m in range(j + 1, TILE):
                    columns[m] = columns[m] - below * (columns[m][j : j + 1, :] * scale)
            rest = rest[TILE:, :]
        solved = jnp.concatenate(done, axis=0)
        small = pltpu.roll(solved, 128 - BLOCK, 1)[:, :BLOCK]
        panel = dot_f32(small, panel)
        inverse_ref[pl.ds(start, BLOCK), :] = panel[:, rank:]
        later = jnp.where(panel_lane >= start + BLOCK, panel[:, :rank], 0.0)
        work_ref[...] -= dot_f32(later, panel, (((0,), (0,)), ((), ())))
        return carry

    lax.fori_loop(0, rank // BLOCK, block_step, 0)


def invert_factor(spot, parts):
    rank = parts[0].shape[1]
    return pl.pallas_call(
        invert_kernel,
        in_specs=[pl.BlockSpec(memory_space=pltpu.SMEM)]
        + [pl.BlockSpec(memory_space=pltpu.VMEM)] * len(parts),
        out_shape=jax.ShapeDtypeStruct((rank, rank), jnp.float32),
        scratch_shapes=[pltpu.VMEM((rank, 2 * rank), jnp.float32)],
        compiler_params=GRANT,
        cost_estimate=pl.CostEstimate(flops=20_000_000_000, bytes_accessed=524288, transcendentals=0),
        name="invert_factor",
    )(spot, *parts)


def moment_kernel(*refs):
    total = None
    for part_ref in refs[:-1]:
        part = part_ref[...]
        term = dot_f32(part, part, ROW_DIMS)
        total = term if total is None else total + term
    refs[-1][...] = total


def moment_of(parts):
    rank = parts[0].shape[1]
    return pl.pallas_call(
        moment_kernel,
        out_shape=jax.ShapeDtypeStruct((rank, rank), jnp.float32),
        compiler_params=GRANT,
        cost_estimate=pl.CostEstimate(flops=4_000_000_000, bytes_accessed=2359296, transcendentals=0),
        name="moment_of",
    )(*parts)


def whiten_kernel(spot_ref, inverse_ref, moment_ref, other_ref, *refs):
    parts, out_ref = refs[:-1], refs[-1]
    inverse = inverse_ref[...]
    rank = inverse.shape[0]
    moment = moment_ref[...] + other_ref[...]
    cov_total = dot_f32(dot_f32(inverse, moment), inverse, (((1,), (1,)), ((), ())))
    row_ids = lax.broadcasted_iota(jnp.int32, (rank, rank), 0)
    col_ids = lax.broadcasted_iota(jnp.int32, (rank, rank), 1)
    eye_matrix = (row_ids == col_ids).astype(jnp.float32)
    trace_value = jnp.sum(cov_total * eye_matrix, axis=(0, 1), keepdims=True)
    left_iter = cov_total / trace_value
    right_iter = 1.5 * eye_matrix - 0.5 * left_iter
    right_parts = split_two(right_iter)
    left_parts = split_two(dot_split(split_two(left_iter), right_parts))
    for step_index in range(1, NS_STEPS):
        middle = split_two(1.5 * eye_matrix - 0.5 * dot_split(right_parts, left_parts))
        right_iter = dot_split(middle, right_parts)
        if step_index < NS_STEPS - 1:
            left_parts = split_two(dot_split(left_parts, middle))
            right_parts = split_two(right_iter)
    factor = right_iter / jnp.sqrt(trace_value)
    weight = split_two(dot_f32(inverse, factor, ROW_DIMS))
    height = out_ref.shape[0] // len(parts)
    for step, part_ref in enumerate(parts):
        place = lax.rem(spot_ref[0] + len(parts) - step, len(parts))
        rows = pl.ds(pl.multiple_of(place * height, height), height)
        out_ref[rows, :] = dot_split(split_two(part_ref[...]), weight).astype(jnp.bfloat16)


def project_half(spot, inverse, moment, other, parts):
    chunk, rank = parts[0].shape
    return pl.pallas_call(
        whiten_kernel,
        in_specs=[pl.BlockSpec(memory_space=pltpu.SMEM)]
        + [pl.BlockSpec(memory_space=pltpu.VMEM)] * (3 + len(parts)),
        out_shape=jax.ShapeDtypeStruct((chunk * len(parts), rank), jnp.bfloat16),
        compiler_params=GRANT,
        cost_estimate=pl.CostEstimate(flops=12_000_000_000, bytes_accessed=4194304, transcendentals=0),
        name="project_half",
    )(spot, inverse, moment, other, *parts)


def chunk_kernel(spot_ref, rows_ref, sketch_ref, label_ref, give_ref, keep_ref):
    chunk, core, here, line = (spot_ref[i] for i in range(4))
    rank = sketch_ref.shape[1]
    width = give_ref.shape[1] - 128
    half = rows_ref.shape[1] // 2
    sketch = sketch_ref[...]
    mul = functools.partial(
        lax.dot_general, dimension_numbers=ROW_DIMS, preferred_element_type=jnp.float32
    )
    gram = mul(sketch, sketch)
    gram = pltpu.roll(gram, rank - chunk * (rank * width // half), 1)[:, :128]
    lane = lax.broadcasted_iota(jnp.int32, gram.shape, 1)
    gram = jnp.where(lane < rank * width // half, gram, 0.0)
    mine = pl.ds(pl.multiple_of((core * line + here) * SLOTS, SLOTS), SLOTS)
    for out_ref, place in ((give_ref, 1 - core), (keep_ref, core)):
        columns = pl.ds(pl.multiple_of(place * half + chunk * width, width), width)
        out_ref[:, :width] = mul(sketch, rows_ref[:, columns])
        out_ref[:, width:] = gram
        theirs = pl.ds(pl.multiple_of((place * line + chunk) * SLOTS, SLOTS), SLOTS)
        out_ref[mine, width:] += label_ref[theirs, :]


def cross_chunk(spot, embeddings, sketch, labels, chunks):
    depth, dim = embeddings.shape
    rank = sketch.shape[1]
    width = dim // 2 // chunks
    shape = jax.ShapeDtypeStruct((rank, width + 128), jnp.float32)
    return pl.pallas_call(
        chunk_kernel,
        in_specs=[pl.BlockSpec(memory_space=pltpu.SMEM)]
        + [pl.BlockSpec(memory_space=pltpu.VMEM)] * 3,
        out_shape=[shape, shape],
        compiler_params=GRANT,
        cost_estimate=pl.CostEstimate(
            flops=2 * depth * rank * (2 * width + rank), bytes_accessed=3000000, transcendentals=0
        ),
        name="cross_chunk",
    )(spot, embeddings, sketch, labels)


def join_kernel(side, keep_ref, got_ref, extra_ref, out_ref):
    height = extra_ref.shape[0]
    out_ref[...] = keep_ref[...] + got_ref[...]
    out_ref[side * height : (side + 1) * height, :] += extra_ref[...]


def join_chunk(keep, got, extra, side):
    return pl.pallas_call(
        functools.partial(join_kernel, side),
        out_shape=jax.ShapeDtypeStruct(keep.shape, jnp.float32),
        compiler_params=GRANT,
        cost_estimate=pl.CostEstimate(flops=400000, bytes_accessed=2000000, transcendentals=0),
        name="join_chunk",
    )(keep, got, extra)


def line_kernel(gram_piece, *refs):
    parts, out_ref = refs[:-1], refs[-1]
    plane, _, rank = out_ref.shape
    width = parts[0].shape[1] - 128
    total = parts[0][...] + parts[1][...]
    for part_ref in parts[2:]:
        total = total + part_ref[...]
    piece = width // plane
    out_ref[:, :piece, :] = total[:, :width].T.reshape(plane, piece, rank)
    tail = total[:, width:].T.reshape(2, plane, gram_piece, rank)
    fill = jnp.zeros((plane, out_ref.shape[1] - piece - 2 * gram_piece, rank), jnp.float32)
    out_ref[:, piece:, :] = jnp.concatenate([tail[0], tail[1], fill], axis=1)


def line_total(parts, plane, gram_piece):
    rank, width = parts[0].shape
    rows = (width - 128) // plane + 2 * gram_piece
    rows += -rows % 8
    return pl.pallas_call(
        functools.partial(line_kernel, gram_piece),
        out_shape=jax.ShapeDtypeStruct((plane, rows, rank), jnp.float32),
        compiler_params=GRANT,
        cost_estimate=pl.CostEstimate(flops=1000000, bytes_accessed=4000000, transcendentals=0),
        name="line_total",
    )(*parts)


def plane_kernel(label_row, parts_ref, out_ref, label_ref):
    out_ref[...] = jnp.broadcast_to(jnp.sum(parts_ref[...], axis=0, keepdims=True), out_ref.shape)
    label_ref[...] = parts_ref[:, label_row, :].astype(jnp.int32) - 1


def plane_total(parts, label_row):
    plane, _, rank = parts.shape
    return pl.pallas_call(
        functools.partial(plane_kernel, label_row),
        out_shape=[
            jax.ShapeDtypeStruct(parts.shape, jnp.float32),
            jax.ShapeDtypeStruct((plane, rank), jnp.int32),
        ],
        compiler_params=GRANT,
        cost_estimate=pl.CostEstimate(flops=1000000, bytes_accessed=1600000, transcendentals=0),
        name="plane_total",
    )(parts)


def product_kernel(core_ref, rows_ref, basis_ref, *refs):
    half, width = basis_ref.shape[0], 512
    total = None if len(refs) == 1 else refs[0][...]
    for step in range(half // width):
        columns = pl.ds(pl.multiple_of(core_ref[0] * half + step * width, width), width)
        basis = basis_ref[step * width : (step + 1) * width, :]
        term = jnp.dot(rows_ref[:, columns], basis, preferred_element_type=jnp.float32)
        total = term if total is None else total + term
    refs[-1][...] = total.astype(refs[-1].dtype)


def product_of_half(half, embeddings, basis, begin, out_type):
    depth, dim = embeddings.shape
    rank = basis.shape[1]
    extra = [] if begin is None else [begin]
    return pl.pallas_call(
        product_kernel,
        in_specs=[pl.BlockSpec(memory_space=pltpu.SMEM)]
        + [pl.BlockSpec(memory_space=pltpu.VMEM)] * (2 + len(extra)),
        out_shape=jax.ShapeDtypeStruct((depth, rank), out_type),
        compiler_params=GRANT,
        cost_estimate=pl.CostEstimate(
            flops=depth * dim * rank, bytes_accessed=depth * dim + dim * rank, transcendentals=0
        ),
        name="product_of_half",
    )(half, embeddings, basis, *extra)


def route_kernel(capacity, line, plane, ids_ref, map_ref, dest_ref, label_ref):
    ids = ids_ref[...]
    count, (high, low) = ids.shape[1], map_ref.shape
    owner_count = 2 * plane * line
    bf16 = jnp.bfloat16

    def rows_of(size):
        return lax.broadcasted_iota(jnp.int32, (size, count), 0)

    picked = (rows_of(high) == ids // low).astype(bf16)
    found = lax.dot_general(
        map_ref[...].astype(bf16), picked, ROW_DIMS, preferred_element_type=jnp.float32
    )
    owner = jnp.sum(jnp.where(rows_of(low) == ids % low, found, 0.0), axis=0, keepdims=True)
    owner = owner.astype(jnp.int32)
    mine = rows_of(owner_count) == owner
    order = lax.broadcasted_iota(jnp.int32, (count, count), 1)
    earlier = (lax.broadcasted_iota(jnp.int32, (count, count), 0) < order).astype(bf16)
    before = jnp.dot(mine.astype(bf16), earlier, preferred_element_type=jnp.float32)
    slot = jnp.sum(jnp.where(mine, before, 0.0), axis=0, keepdims=True).astype(jnp.int32)
    dest_ref[...] = owner * capacity + slot
    value = ids + 1
    core, chip = owner // (plane * line), owner % (plane * line)
    row = (core * line + chip % line) * SLOTS + slot
    lane = rows_of(128) == 64 + 2 * (chip // line)
    lane = lane.astype(bf16)
    labels = None
    for digit in range(3):
        short = (value // 128**digit) % 128
        spread = jnp.where(rows_of(2 * line * SLOTS) == row, short.astype(jnp.float32), 0.0)
        term = lax.dot_general(
            spread.astype(bf16),
            lane,
            (((1,), (1,)), ((), ())),
            preferred_element_type=jnp.float32,
        )
        labels = term if labels is None else labels + term * 128**digit
    label_ref[...] = labels


def route_rows(list_ids, owner_map, capacity, line, plane):
    count = list_ids.shape[0]
    return pl.pallas_call(
        functools.partial(route_kernel, capacity, line, plane),
        out_shape=[
            jax.ShapeDtypeStruct((1, count), jnp.int32),
            jax.ShapeDtypeStruct((2 * line * SLOTS, 128), jnp.float32),
        ],
        compiler_params=GRANT,
        cost_estimate=pl.CostEstimate(
            flops=2_000_000_000, bytes_accessed=1048576, transcendentals=0
        ),
        name="route_rows",
    )(list_ids.reshape(1, count), owner_map.reshape(-1, 128))


def place_kernel(capacity, target_ref, first_ref, second_ref, out_ref):
    pairs, _, width = out_ref.shape
    count = pairs * 2 * capacity
    slots = pl.program_id(0) * count + lax.broadcasted_iota(
        jnp.int32, (count, first_ref.shape[0]), 0
    )
    found = []
    for part, rows_ref in enumerate((first_ref, second_ref)):
        onehot = (slots == target_ref[part : part + 1, :]).astype(jnp.bfloat16)
        term = jnp.dot(onehot, rows_ref[...], preferred_element_type=jnp.float32)
        found.append(term.reshape(pairs, 2 * capacity, width))
    a, b = found
    out_ref[...] = jnp.concatenate(
        [a[:, :capacity], b[:, :capacity], a[:, capacity:], b[:, capacity:]], axis=1
    ).astype(jnp.bfloat16)


def place_rows(target, first, second, chips, capacity):
    pairs = 16
    depth, width = first.shape
    return pl.pallas_call(
        functools.partial(place_kernel, capacity),
        grid=(chips // 2 // pairs,),
        in_specs=[pl.BlockSpec((2, depth), lambda i: (0, 0))]
        + [pl.BlockSpec((depth, width), lambda i: (0, 0))] * 2,
        out_specs=pl.BlockSpec((pairs, 4 * capacity, width), lambda i: (i, 0, 0)),
        out_shape=jax.ShapeDtypeStruct((chips // 2, 4 * capacity, width), jnp.bfloat16),
        compiler_params=GRANT,
        cost_estimate=pl.CostEstimate(
            flops=4 * chips * capacity * depth * width,
            bytes_accessed=8 * chips * capacity * width,
            transcendentals=0,
        ),
        name="place_rows",
    )(target, first, second)


def shift(value, axis, step):
    size = lax.axis_size(axis)
    return lax.ppermute(value, axis, [(i, (i + step) % size) for i in range(size)])


def local(embeddings, sketch_seed, list_ids, owner_map):
    row_count, dim = embeddings.shape
    rank = sketch_seed.shape[1]
    cores, line = lax.axis_size("narrow"), lax.axis_size("x")
    plane = lax.axis_size("y") * lax.axis_size("z")
    chips = plane * line
    dev_count = cores * chips
    core = lax.axis_index("narrow")
    spot = lax.axis_index("x").reshape(1)
    own_half, other_half = core.reshape(1), (1 - core).reshape(1)
    piece, gram_piece = dim // dev_count, rank // chips
    seed_matrix = sketch_seed.astype(jnp.bfloat16)
    sketch = jnp.dot(embeddings, seed_matrix, preferred_element_type=jnp.float32).astype(
        jnp.bfloat16
    )

    capacity = 4 * row_count // dev_count
    here = lax.axis_index("x")
    dest_index, labels = route_rows(list_ids, owner_map, capacity, line, plane)

    def chunk_at(step):
        where = jnp.stack([(here + step) % line, core, here, jnp.int32(line)])
        give, keep = cross_chunk(where, embeddings, sketch, labels, line)
        return keep, shift(give, "narrow", 1)

    far, up, down, near = (chunk_at(step) for step in (2, 1, 3, 0))
    far = far[0] + far[1]
    from_below = shift(far[: rank // 2], "x", 1)
    from_above = shift(far[rank // 2 :], "x", line - 1)
    from_below = shift(join_chunk(*up, from_below, 0), "x", 1)
    from_above = shift(join_chunk(*down, from_above, 1), "x", line - 1)

    packed = line_total([*near, from_below, from_above], plane, gram_piece)
    packed = lax.all_to_all(packed, PLANE, 0, 0, tiled=True)
    packed, arrived_labels = plane_total(packed, piece + gram_piece)
    packed = lax.all_to_all(packed, PLANE, 0, 0, tiled=True)
    gram_line = packed[:, piece : piece + gram_piece].reshape(-1, rank)
    gram_parts = [gram_line] + [shift(gram_line, "x", step) for step in range(1, line)]
    packed, gram_parts[1] = lax.optimization_barrier((packed, gram_parts[1]))
    cross_line = packed[:, :piece].reshape(-1, rank)
    cross_parts = [cross_line] + [shift(cross_line, "x", step) for step in range(1, line)]
    arrived_labels = arrived_labels[:, : cores * line * SLOTS].reshape(plane, cores, line, SLOTS)
    arrived_labels = arrived_labels[..., :capacity].transpose(1, 0, 2, 3)

    both_dest = jnp.concatenate([dest_index, shift(dest_index, "narrow", 1)])
    both_owner = both_dest // capacity
    target = (both_owner % chips) * capacity + both_dest % capacity
    target = jnp.where(both_owner // chips == core, target, -1)
    target = jnp.where(core == 0, target, target[::-1])

    inverse = invert_factor(spot, gram_parts)
    inverse, cross_parts = lax.optimization_barrier((inverse, cross_parts))
    moment = moment_of(cross_parts)
    basis = project_half(spot, inverse, moment, shift(moment, "narrow", 1), cross_parts)
    other_basis = shift(basis, "narrow", 1)
    begun = product_of_half(own_half, embeddings, basis, None, jnp.float32)
    reduced = product_of_half(other_half, embeddings, other_basis, begun, jnp.bfloat16)
    other = shift(reduced, "narrow", 1)
    send_rows = place_rows(
        target,
        jnp.where(core == 0, reduced, other),
        jnp.where(core == 0, other, reduced),
        chips,
        capacity,
    )
    send_rows = send_rows.reshape(chips, cores * capacity, rank)
    arrived = lax.all_to_all(send_rows, ("y", "z", "x"), 0, 0, tiled=True)
    arrived = arrived.reshape(chips, cores, capacity, rank).transpose(1, 0, 2, 3)
    return (
        arrived.reshape(1, dev_count, capacity, rank),
        arrived_labels.reshape(1, dev_count, capacity),
    )


def solution(mesh):
    grid = Mesh(mesh.devices.reshape(2, 4, 8, 4), ALL)
    in_specs = (P(ALL, None), P(), P(ALL), P())
    out_specs = (P(ALL, None, None, None), P(ALL, None, None))
    return jax.shard_map(local, mesh=grid, in_specs=in_specs, out_specs=out_specs, check_vma=False)
```

```python
import functools

import jax
import jax.numpy as jnp
from jax import lax
from jax.experimental import pallas as pl
from jax.experimental.pallas import tpu as pltpu
from jax.sharding import Mesh
from jax.sharding import PartitionSpec as P

NS_STEPS = 6
BLOCK = 64
TILE = 16
ALL = ("narrow", "y", "z", "x")
PLANE = ("y", "z")
HIGHEST = lax.Precision.HIGHEST
ROW_DIMS = (((0,), (0,)), ((), ()))
SLOTS = 16
SPOTS = 4
GRANT = pltpu.CompilerParams(vmem_limit_bytes=16 * 2**20)


def dot_f32(a, b, dims=(((1,), (0,)), ((), ()))):
    return lax.dot_general(a, b, dims, precision=HIGHEST, preferred_element_type=jnp.float32)


def split_two(a):
    high = a.astype(jnp.bfloat16)
    return high, (a - high.astype(jnp.float32)).astype(jnp.bfloat16)


def dot_split(a, b):
    (ah, al), (bh, bl) = a, b
    mul = functools.partial(jnp.dot, preferred_element_type=jnp.float32)
    return mul(ah, bh) + (mul(ah, bl) + mul(al, bh))


def invert_kernel(spot_ref, *refs):
    parts, inverse_ref, work_ref = refs[:-2], refs[-2], refs[-1]
    rank = inverse_ref.shape[0]
    height = rank // len(parts)
    row_ids = lax.broadcasted_iota(jnp.int32, (rank, rank), 0)
    col_ids = lax.broadcasted_iota(jnp.int32, (rank, rank), 1)
    for step, part_ref in enumerate(parts):
        place = lax.rem(spot_ref[0] + len(parts) - step, len(parts))
        work_ref[pl.ds(pl.multiple_of(place * height, height), height), :rank] = part_ref[...]
    work_ref[:, rank:] = (row_ids == col_ids).astype(jnp.float32)
    lane = lax.broadcasted_iota(jnp.int32, (BLOCK, 128), 1)
    row = lax.broadcasted_iota(jnp.int32, (BLOCK, 128), 0)
    panel_lane = lax.broadcasted_iota(jnp.int32, (BLOCK, rank), 1)

    def block_step(step, carry):
        start = pl.multiple_of(step * BLOCK, BLOCK)
        panel = work_ref[pl.ds(start, BLOCK), :]
        shifted = pltpu.roll(panel[:, :rank], rank - start, 1)[:, :128]
        rest = jnp.where(lane < BLOCK, shifted, (lane - BLOCK == row).astype(jnp.float32))
        done = []
        for tile in range(BLOCK // TILE):
            height = BLOCK - tile * TILE
            sub = lax.broadcasted_iota(jnp.int32, (height, 128), 0)
            columns = [
                jnp.broadcast_to(rest[:, tile * TILE + j : tile * TILE + j + 1], (height, 128))
                for j in range(TILE)
            ]
            for j in range(TILE):
                pivot = columns[j][j : j + 1, :]
                scale = lax.rsqrt(pivot)
                scale = scale * (1.5 - 0.5 * (pivot * scale) * scale)
                below = jnp.where(sub > j, columns[j] * scale, 0.0)
                lead = rest[j : j + 1, :] * scale
                done.append(lead)
                rest = rest - below * lead
                for m in range(j + 1, TILE):
                    columns[m] = columns[m] - below * (columns[m][j : j + 1, :] * scale)
            rest = rest[TILE:, :]
        solved = jnp.concatenate(done, axis=0)
        small = pltpu.roll(solved, 128 - BLOCK, 1)[:, :BLOCK]
        panel = dot_f32(small, panel)
        inverse_ref[pl.ds(start, BLOCK), :] = panel[:, rank:]
        later = jnp.where(panel_lane >= start + BLOCK, panel[:, :rank], 0.0)
        work_ref[...] -= dot_f32(later, panel, (((0,), (0,)), ((), ())))
        return carry

    lax.fori_loop(0, rank // BLOCK, block_step, 0)


def invert_factor(spot, parts):
    rank = parts[0].shape[1]
    return pl.pallas_call(
        invert_kernel,
        in_specs=[pl.BlockSpec(memory_space=pltpu.SMEM)]
        + [pl.BlockSpec(memory_space=pltpu.VMEM)] * len(parts),
        out_shape=jax.ShapeDtypeStruct((rank, rank), jnp.float32),
        scratch_shapes=[pltpu.VMEM((rank, 2 * rank), jnp.float32)],
        compiler_params=GRANT,
        cost_estimate=pl.CostEstimate(flops=20_000_000_000, bytes_accessed=524288, transcendentals=0),
        name="invert_factor",
    )(spot, *parts)


def moment_kernel(*refs):
    total = None
    for part_ref in refs[:-1]:
        part = part_ref[...]
        term = dot_f32(part, part, ROW_DIMS)
        total = term if total is None else total + term
    refs[-1][...] = total


def moment_of(parts):
    rank = parts[0].shape[1]
    return pl.pallas_call(
        moment_kernel,
        out_shape=jax.ShapeDtypeStruct((rank, rank), jnp.float32),
        compiler_params=GRANT,
        cost_estimate=pl.CostEstimate(flops=4_000_000_000, bytes_accessed=2359296, transcendentals=0),
        name="moment_of",
    )(*parts)


def whiten_kernel(spot_ref, inverse_ref, moment_ref, other_ref, *refs):
    parts, out_ref = refs[:-1], refs[-1]
    inverse = inverse_ref[...]
    rank = inverse.shape[0]
    moment = moment_ref[...] + other_ref[...]
    cov_total = dot_f32(dot_f32(inverse, moment), inverse, (((1,), (1,)), ((), ())))
    row_ids = lax.broadcasted_iota(jnp.int32, (rank, rank), 0)
    col_ids = lax.broadcasted_iota(jnp.int32, (rank, rank), 1)
    eye_matrix = (row_ids == col_ids).astype(jnp.float32)
    trace_value = jnp.sum(cov_total * eye_matrix, axis=(0, 1), keepdims=True)
    left_iter = cov_total / trace_value
    right_iter = 1.5 * eye_matrix - 0.5 * left_iter
    right_parts = split_two(right_iter)
    left_parts = split_two(dot_split(split_two(left_iter), right_parts))
    for step_index in range(1, NS_STEPS):
        middle = split_two(1.5 * eye_matrix - 0.5 * dot_split(right_parts, left_parts))
        right_iter = dot_split(middle, right_parts)
        if step_index < NS_STEPS - 1:
            left_parts = split_two(dot_split(left_parts, middle))
            right_parts = split_two(right_iter)
    factor = right_iter / jnp.sqrt(trace_value)
    weight = split_two(dot_f32(inverse, factor, ROW_DIMS))
    height = out_ref.shape[0] // len(parts)
    for step, part_ref in enumerate(parts):
        place = lax.rem(spot_ref[0] + len(parts) - step, len(parts))
        rows = pl.ds(pl.multiple_of(place * height, height), height)
        out_ref[rows, :] = dot_split(split_two(part_ref[...]), weight).astype(jnp.bfloat16)


def project_half(spot, inverse, moment, other, parts):
    chunk, rank = parts[0].shape
    return pl.pallas_call(
        whiten_kernel,
        in_specs=[pl.BlockSpec(memory_space=pltpu.SMEM)]
        + [pl.BlockSpec(memory_space=pltpu.VMEM)] * (3 + len(parts)),
        out_shape=jax.ShapeDtypeStruct((chunk * len(parts), rank), jnp.bfloat16),
        compiler_params=GRANT,
        cost_estimate=pl.CostEstimate(flops=12_000_000_000, bytes_accessed=4194304, transcendentals=0),
        name="project_half",
    )(spot, inverse, moment, other, *parts)


def chunk_kernel(spot_ref, rows_ref, sketch_ref, label_ref, give_ref, keep_ref):
    chunk, core, line = (spot_ref[i] for i in range(3))
    rank = sketch_ref.shape[1]
    width = give_ref.shape[1]
    half = rows_ref.shape[1] // 2
    count = label_ref.shape[0] // 2 // SPOTS
    sketch = sketch_ref[...]
    for out_ref, place in ((give_ref, 1 - core), (keep_ref, core)):
        columns = pl.ds(pl.multiple_of(place * half + chunk * width, width), width)
        out_ref[:rank, :] = lax.dot_general(
            sketch, rows_ref[:, columns], ROW_DIMS, preferred_element_type=jnp.float32
        )
        start = (place * line + chunk) * count
        for block in range(width // 128):
            rows = pl.ds(pl.multiple_of(start + 8 * block, 8), 8)
            out_ref[rank:, 128 * block : 128 * (block + 1)] = label_ref[rows, :]


def cross_chunk(spot, embeddings, sketch, labels, chunks):
    depth, dim = embeddings.shape
    rank = sketch.shape[1]
    width = dim // 2 // chunks
    shape = jax.ShapeDtypeStruct((rank + 8, width), jnp.float32)
    return pl.pallas_call(
        chunk_kernel,
        in_specs=[pl.BlockSpec(memory_space=pltpu.SMEM)]
        + [pl.BlockSpec(memory_space=pltpu.VMEM)] * 3,
        out_shape=[shape, shape],
        compiler_params=GRANT,
        cost_estimate=pl.CostEstimate(
            flops=4 * depth * rank * width, bytes_accessed=3000000, transcendentals=0
        ),
        name="cross_chunk",
    )(spot, embeddings, sketch, labels)


def join_kernel(side, keep_ref, got_ref, extra_ref, out_ref):
    height, whole = extra_ref.shape[0], out_ref.shape[0]
    rows = slice(0, height) if side == 0 else slice(whole - height, whole)
    out_ref[...] = keep_ref[...] + got_ref[...]
    out_ref[rows, :] += extra_ref[...]


def join_chunk(keep, got, extra, side):
    return pl.pallas_call(
        functools.partial(join_kernel, side),
        out_shape=jax.ShapeDtypeStruct(keep.shape, jnp.float32),
        compiler_params=GRANT,
        cost_estimate=pl.CostEstimate(flops=400000, bytes_accessed=2000000, transcendentals=0),
        name="join_chunk",
    )(keep, got, extra)


def line_kernel(*refs):
    parts, out_ref = refs[:-1], refs[-1]
    plane = out_ref.shape[0]
    total = parts[0][...] + parts[1][...]
    for part_ref in parts[2:]:
        total = total + part_ref[...]
    rank, width = total.shape[0] - 8, total.shape[1]
    piece = width // plane
    turned = total[:rank, :].T.reshape(plane, piece, rank)
    out_ref[:, :piece, :] = turned[:, :, :128]
    out_ref[:, piece : 2 * piece, :] = turned[:, :, 128:]
    labels = [total[rank:, 128 * k : 128 * (k + 1)] for k in range(width // 128)]
    labels = jnp.concatenate(labels, axis=0).reshape(plane, 1, 128)
    fill = jnp.zeros((plane, out_ref.shape[1] - 2 * piece - 1, 128), jnp.float32)
    out_ref[:, 2 * piece :, :] = jnp.concatenate([labels, fill], axis=1)


def line_total(parts, plane):
    rows = 2 * (parts[0].shape[1] // plane) + 8
    return pl.pallas_call(
        line_kernel,
        out_shape=jax.ShapeDtypeStruct((plane, rows, 128), jnp.float32),
        compiler_params=GRANT,
        cost_estimate=pl.CostEstimate(flops=1000000, bytes_accessed=4000000, transcendentals=0),
        name="line_total",
    )(*parts)


def plane_kernel(parts_ref, out_ref, label_ref):
    piece = out_ref.shape[1]
    total = jnp.sum(parts_ref[:, : 2 * piece, :], axis=0)
    total = jnp.concatenate([total[:piece], total[piece:]], axis=1)
    out_ref[...] = jnp.broadcast_to(total[None], out_ref.shape)
    label_ref[...] = parts_ref[:, 2 * piece, :].astype(jnp.int32) - 1


def plane_total(parts, piece):
    plane, _, lanes = parts.shape
    return pl.pallas_call(
        plane_kernel,
        out_shape=[
            jax.ShapeDtypeStruct((plane, piece, 2 * lanes), jnp.float32),
            jax.ShapeDtypeStruct((plane, lanes), jnp.int32),
        ],
        compiler_params=GRANT,
        cost_estimate=pl.CostEstimate(flops=1000000, bytes_accessed=1600000, transcendentals=0),
        name="plane_total",
    )(parts)


def product_kernel(core_ref, rows_ref, basis_ref, *refs):
    half, width = basis_ref.shape[0], 512
    total = None if len(refs) == 1 else refs[0][...]
    for step in range(half // width):
        columns = pl.ds(pl.multiple_of(core_ref[0] * half + step * width, width), width)
        basis = basis_ref[step * width : (step + 1) * width, :]
        term = jnp.dot(rows_ref[:, columns], basis, preferred_element_type=jnp.float32)
        total = term if total is None else total + term
    refs[-1][...] = total.astype(refs[-1].dtype)


def product_of_half(half, embeddings, basis, begin, out_type):
    depth, dim = embeddings.shape
    rank = basis.shape[1]
    extra = [] if begin is None else [begin]
    return pl.pallas_call(
        product_kernel,
        in_specs=[pl.BlockSpec(memory_space=pltpu.SMEM)]
        + [pl.BlockSpec(memory_space=pltpu.VMEM)] * (2 + len(extra)),
        out_shape=jax.ShapeDtypeStruct((depth, rank), out_type),
        compiler_params=GRANT,
        cost_estimate=pl.CostEstimate(
            flops=depth * dim * rank, bytes_accessed=depth * dim + dim * rank, transcendentals=0
        ),
        name="product_of_half",
    )(half, embeddings, basis, *extra)


def route_kernel(capacity, line, plane, spot_ref, ids_ref, map_ref, dest_ref, label_ref):
    ids = ids_ref[...]
    count, (high, low) = ids.shape[1], map_ref.shape
    owner_count = 2 * plane * line
    bf16 = jnp.bfloat16

    def rows_of(size):
        return lax.broadcasted_iota(jnp.int32, (size, count), 0)

    picked = (rows_of(high) == ids // low).astype(bf16)
    found = lax.dot_general(
        map_ref[...].astype(bf16), picked, ROW_DIMS, preferred_element_type=jnp.float32
    )
    owner = jnp.sum(jnp.where(rows_of(low) == ids % low, found, 0.0), axis=0, keepdims=True)
    owner = owner.astype(jnp.int32)
    mine = rows_of(owner_count) == owner
    order = lax.broadcasted_iota(jnp.int32, (count, count), 1)
    earlier = (lax.broadcasted_iota(jnp.int32, (count, count), 0) < order).astype(bf16)
    before = jnp.dot(mine.astype(bf16), earlier, preferred_element_type=jnp.float32)
    slot = jnp.sum(jnp.where(mine, before, 0.0), axis=0, keepdims=True).astype(jnp.int32)
    dest_ref[...] = owner * capacity + slot
    value = ids + 1
    core, chip = owner // (plane * line), owner % (plane * line)
    row = (core * line + chip % line) * plane + chip // line
    row = (rows_of(owner_count) == row).astype(bf16)
    lane = rows_of(2 * line * SLOTS) == spot_ref[0] * SLOTS + slot
    labels = None
    for digit in range(3):
        short = (value // 128**digit) % 128
        spread = jnp.where(lane, short.astype(jnp.float32), 0.0).astype(bf16)
        term = lax.dot_general(
            row, spread, (((1,), (1,)), ((), ())), preferred_element_type=jnp.float32
        )
        labels = term if labels is None else labels + term * 128**digit
    label_ref[...] = labels


def route_rows(spot, list_ids, owner_map, capacity, line, plane):
    count = list_ids.shape[0]
    return pl.pallas_call(
        functools.partial(route_kernel, capacity, line, plane),
        in_specs=[pl.BlockSpec(memory_space=pltpu.SMEM)]
        + [pl.BlockSpec(memory_space=pltpu.VMEM)] * 2,
        out_shape=[
            jax.ShapeDtypeStruct((1, count), jnp.int32),
            jax.ShapeDtypeStruct((2 * line * plane, 2 * line * SLOTS), jnp.float32),
        ],
        compiler_params=GRANT,
        cost_estimate=pl.CostEstimate(
            flops=2_000_000_000, bytes_accessed=1048576, transcendentals=0
        ),
        name="route_rows",
    )(spot, list_ids.reshape(1, count), owner_map.reshape(-1, 128))


def place_kernel(capacity, target_ref, first_ref, second_ref, out_ref):
    pairs, _, width = out_ref.shape
    count = pairs * 2 * capacity
    slots = pl.program_id(0) * count + lax.broadcasted_iota(
        jnp.int32, (count, first_ref.shape[0]), 0
    )
    found = []
    for part, rows_ref in enumerate((first_ref, second_ref)):
        onehot = (slots == target_ref[part : part + 1, :]).astype(jnp.bfloat16)
        term = jnp.dot(onehot, rows_ref[...], preferred_element_type=jnp.float32)
        found.append(term.reshape(pairs, 2 * capacity, width))
    a, b = found
    out_ref[...] = jnp.concatenate(
        [a[:, :capacity], b[:, :capacity], a[:, capacity:], b[:, capacity:]], axis=1
    ).astype(jnp.bfloat16)


def place_rows(target, first, second, chips, capacity):
    pairs = 16
    depth, width = first.shape
    return pl.pallas_call(
        functools.partial(place_kernel, capacity),
        grid=(chips // 2 // pairs,),
        in_specs=[pl.BlockSpec((2, depth), lambda i: (0, 0))]
        + [pl.BlockSpec((depth, width), lambda i: (0, 0))] * 2,
        out_specs=pl.BlockSpec((pairs, 4 * capacity, width), lambda i: (i, 0, 0)),
        out_shape=jax.ShapeDtypeStruct((chips // 2, 4 * capacity, width), jnp.bfloat16),
        compiler_params=GRANT,
        cost_estimate=pl.CostEstimate(
            flops=4 * chips * capacity * depth * width,
            bytes_accessed=8 * chips * capacity * width,
            transcendentals=0,
        ),
        name="place_rows",
    )(target, first, second)


def shift(value, axis, step):
    size = lax.axis_size(axis)
    return lax.ppermute(value, axis, [(i, (i + step) % size) for i in range(size)])


def pair_sum(value, axis, distance):
    size = lax.axis_size(axis)
    return value + lax.ppermute(value, axis, [(i, i ^ distance) for i in range(size)])


def local(embeddings, sketch_seed, list_ids, owner_map):
    row_count, dim = embeddings.shape
    rank = sketch_seed.shape[1]
    cores, line = lax.axis_size("narrow"), lax.axis_size("x")
    plane = lax.axis_size("y") * lax.axis_size("z")
    chips = plane * line
    dev_count = cores * chips
    core, here = lax.axis_index("narrow"), lax.axis_index("x")
    own_half, other_half = core.reshape(1), (1 - core).reshape(1)
    piece = dim // dev_count
    capacity = 4 * row_count // dev_count
    seed_matrix = sketch_seed.astype(jnp.bfloat16)
    sketch = jnp.dot(embeddings, seed_matrix, preferred_element_type=jnp.float32).astype(
        jnp.bfloat16
    )
    embeddings = jnp.where(core >= 0, embeddings, jnp.bfloat16(0))
    list_ids, sketch = lax.optimization_barrier((list_ids, sketch))
    spot = (core * line + here).reshape(1)
    dest_index, labels = route_rows(spot, list_ids, owner_map, capacity, line, plane)

    def chunk_at(step):
        where = jnp.stack([(here + step) % line, core, jnp.int32(line)])
        give, keep = cross_chunk(where, embeddings, sketch, labels, line)
        return keep, shift(give, "narrow", 1)

    far, up, down, near = (chunk_at(step) for step in (2, 1, 3, 0))
    far = far[0] + far[1]
    from_below = shift(far[: rank // 2], "x", 1)
    from_above = shift(far[rank // 2 :], "x", line - 1)
    from_below = shift(join_chunk(*up, from_below, 0), "x", 1)
    from_above = shift(join_chunk(*down, from_above, 1), "x", line - 1)

    gram = lax.dot_general(sketch, sketch, ROW_DIMS, preferred_element_type=jnp.float32)
    gram_give = lax.dynamic_slice_in_dim(gram, (1 - core) * (rank // 2), rank // 2)
    gram = lax.dynamic_slice_in_dim(gram, core * (rank // 2), rank // 2)
    gram = gram + shift(gram_give, "narrow", 1)
    steps = []
    for axis in ("x", "y", "z"):
        distance = 1
        while distance < lax.axis_size(axis):
            gram = pair_sum(gram, axis, distance)
            steps.append(gram)
            distance *= 2
    gram_parts = [gram, shift(gram, "narrow", 1)]

    packed = line_total([*near, from_below, from_above], plane)
    packed, _ = lax.optimization_barrier((packed, steps[-2]))
    packed = lax.all_to_all(packed, PLANE, 0, 0, tiled=True)
    packed, gram_parts = lax.optimization_barrier((packed, gram_parts))
    inverse = invert_factor(own_half, gram_parts)
    packed, arrived_labels = plane_total(packed, piece)
    packed = lax.all_to_all(packed, PLANE, 0, 0, tiled=True)
    cross_line = packed.reshape(-1, rank)
    cross_parts = [cross_line] + [shift(cross_line, "x", step) for step in range(1, line)]
    arrived_labels = arrived_labels.reshape(plane, cores, line, SLOTS)
    arrived_labels = arrived_labels[..., :capacity].transpose(1, 0, 2, 3)

    both_dest = jnp.concatenate([dest_index, shift(dest_index, "narrow", 1)])
    both_owner = both_dest // capacity
    target = (both_owner % chips) * capacity + both_dest % capacity
    target = jnp.where(both_owner // chips == core, target, -1)
    target = jnp.where(core == 0, target, target[::-1])

    cross_parts, inverse = lax.optimization_barrier((cross_parts, inverse))
    moment = moment_of(cross_parts)
    other_moment = shift(moment, "narrow", 1)
    basis = project_half(here.reshape(1), inverse, moment, other_moment, cross_parts)
    other_basis = shift(basis, "narrow", 1)
    begun = product_of_half(own_half, embeddings, basis, None, jnp.float32)
    reduced = product_of_half(other_half, embeddings, other_basis, begun, jnp.bfloat16)
    other = shift(reduced, "narrow", 1)
    send_rows = place_rows(
        target,
        jnp.where(core == 0, reduced, other),
        jnp.where(core == 0, other, reduced),
        chips,
        capacity,
    )
    send_rows = send_rows.reshape(chips, cores * capacity, rank)
    arrived = lax.all_to_all(send_rows, ("y", "z", "x"), 0, 0, tiled=True)
    arrived = arrived.reshape(chips, cores, capacity, rank).transpose(1, 0, 2, 3)
    return (
        arrived.reshape(1, dev_count, capacity, rank),
        arrived_labels.reshape(1, dev_count, capacity),
    )


def solution(mesh):
    grid = Mesh(mesh.devices.reshape(2, 4, 8, 4), ALL)
    in_specs = (P(ALL, None), P(), P(ALL), P())
    out_specs = (P(ALL, None, None, None), P(ALL, None, None))
    return jax.shard_map(local, mesh=grid, in_specs=in_specs, out_specs=out_specs, check_vma=False)
```

```python
import functools

import jax
import jax.numpy as jnp
from jax import lax
from jax.experimental import pallas as pl
from jax.experimental.pallas import tpu as pltpu
from jax.sharding import Mesh
from jax.sharding import PartitionSpec as P

NS_STEPS = 6
BLOCK = 64
TILE = 16
ALL = ("narrow", "y", "z", "x")
PLANE = ("y", "z")
HIGHEST = lax.Precision.HIGHEST
ROW_DIMS = (((0,), (0,)), ((), ()))
SLOTS = 16
GRANT = pltpu.CompilerParams(vmem_limit_bytes=16 * 2**20)


def dot_f32(a, b, dims=(((1,), (0,)), ((), ()))):
    return lax.dot_general(a, b, dims, precision=HIGHEST, preferred_element_type=jnp.float32)


def split_two(a):
    high = a.astype(jnp.bfloat16)
    return high, (a - high.astype(jnp.float32)).astype(jnp.bfloat16)


def dot_split(a, b):
    (ah, al), (bh, bl) = a, b
    mul = functools.partial(jnp.dot, preferred_element_type=jnp.float32)
    return mul(ah, bh) + (mul(ah, bl) + mul(al, bh))


def invert_kernel(spot_ref, *refs):
    parts, inverse_ref, work_ref = refs[:-2], refs[-2], refs[-1]
    rank = inverse_ref.shape[0]
    height = rank // len(parts)
    row_ids = lax.broadcasted_iota(jnp.int32, (rank, rank), 0)
    col_ids = lax.broadcasted_iota(jnp.int32, (rank, rank), 1)
    for step, part_ref in enumerate(parts):
        place = lax.rem(spot_ref[0] + len(parts) - step, len(parts))
        work_ref[pl.ds(pl.multiple_of(place * height, height), height), :rank] = part_ref[...]
    work_ref[:, rank:] = (row_ids == col_ids).astype(jnp.float32)
    lane = lax.broadcasted_iota(jnp.int32, (BLOCK, 128), 1)
    row = lax.broadcasted_iota(jnp.int32, (BLOCK, 128), 0)
    panel_lane = lax.broadcasted_iota(jnp.int32, (BLOCK, rank), 1)

    def block_step(step, carry):
        start = pl.multiple_of(step * BLOCK, BLOCK)
        panel = work_ref[pl.ds(start, BLOCK), :]
        shifted = pltpu.roll(panel[:, :rank], rank - start, 1)[:, :128]
        rest = jnp.where(lane < BLOCK, shifted, (lane - BLOCK == row).astype(jnp.float32))
        done = []
        for tile in range(BLOCK // TILE):
            height = BLOCK - tile * TILE
            sub = lax.broadcasted_iota(jnp.int32, (height, 128), 0)
            columns = [
                jnp.broadcast_to(rest[:, tile * TILE + j : tile * TILE + j + 1], (height, 128))
                for j in range(TILE)
            ]
            for j in range(TILE):
                pivot = columns[j][j : j + 1, :]
                scale = lax.rsqrt(pivot)
                scale = scale * (1.5 - 0.5 * (pivot * scale) * scale)
                below = jnp.where(sub > j, columns[j] * scale, 0.0)
                lead = rest[j : j + 1, :] * scale
                done.append(lead)
                rest = rest - below * lead
                for m in range(j + 1, TILE):
                    columns[m] = columns[m] - below * (columns[m][j : j + 1, :] * scale)
            rest = rest[TILE:, :]
        solved = jnp.concatenate(done, axis=0)
        small = pltpu.roll(solved, 128 - BLOCK, 1)[:, :BLOCK]
        panel = dot_f32(small, panel)
        inverse_ref[pl.ds(start, BLOCK), :] = panel[:, rank:]
        later = jnp.where(panel_lane >= start + BLOCK, panel[:, :rank], 0.0)
        work_ref[...] -= dot_f32(later, panel, (((0,), (0,)), ((), ())))
        return carry

    lax.fori_loop(0, rank // BLOCK, block_step, 0)


def invert_factor(spot, parts):
    rank = parts[0].shape[1]
    return pl.pallas_call(
        invert_kernel,
        in_specs=[pl.BlockSpec(memory_space=pltpu.SMEM)]
        + [pl.BlockSpec(memory_space=pltpu.VMEM)] * len(parts),
        out_shape=jax.ShapeDtypeStruct((rank, rank), jnp.float32),
        scratch_shapes=[pltpu.VMEM((rank, 2 * rank), jnp.float32)],
        compiler_params=GRANT,
        cost_estimate=pl.CostEstimate(flops=20_000_000_000, bytes_accessed=524288, transcendentals=0),
        name="invert_factor",
    )(spot, *parts)


def moment_kernel(*refs):
    total = None
    for part_ref in refs[:-1]:
        part = whole_rows(part_ref[...])
        term = dot_f32(part, part, ROW_DIMS)
        total = term if total is None else total + term
    refs[-1][...] = total


def moment_of(parts):
    rank = 2 * parts[0].shape[2]
    return pl.pallas_call(
        moment_kernel,
        out_shape=jax.ShapeDtypeStruct((rank, rank), jnp.float32),
        compiler_params=GRANT,
        cost_estimate=pl.CostEstimate(flops=4_000_000_000, bytes_accessed=2359296, transcendentals=0),
        name="moment_of",
    )(*parts)


def whiten_kernel(spot_ref, inverse_ref, moment_ref, other_ref, *refs):
    parts, out_ref = refs[:-1], refs[-1]
    inverse = inverse_ref[...]
    rank = inverse.shape[0]
    moment = moment_ref[...] + other_ref[...]
    cov_total = dot_f32(dot_f32(inverse, moment), inverse, (((1,), (1,)), ((), ())))
    row_ids = lax.broadcasted_iota(jnp.int32, (rank, rank), 0)
    col_ids = lax.broadcasted_iota(jnp.int32, (rank, rank), 1)
    eye_matrix = (row_ids == col_ids).astype(jnp.float32)
    trace_value = jnp.sum(cov_total * eye_matrix, axis=(0, 1), keepdims=True)
    left_iter = cov_total / trace_value
    right_iter = 1.5 * eye_matrix - 0.5 * left_iter
    right_parts = split_two(right_iter)
    left_parts = split_two(dot_split(split_two(left_iter), right_parts))
    for step_index in range(1, NS_STEPS):
        middle = split_two(1.5 * eye_matrix - 0.5 * dot_split(right_parts, left_parts))
        right_iter = dot_split(middle, right_parts)
        if step_index < NS_STEPS - 1:
            left_parts = split_two(dot_split(left_parts, middle))
            right_parts = split_two(right_iter)
    factor = right_iter / jnp.sqrt(trace_value)
    weight = split_two(dot_f32(inverse, factor, ROW_DIMS))
    height = out_ref.shape[0] // len(parts)
    for step, part_ref in enumerate(parts):
        place = lax.rem(spot_ref[0] + len(parts) - step, len(parts))
        rows = pl.ds(pl.multiple_of(place * height, height), height)
        out_ref[rows, :] = dot_split(split_two(whole_rows(part_ref[...])), weight).astype(jnp.bfloat16)


def project_half(spot, inverse, moment, other, parts):
    chunk, rank = parts[0].shape[0] * parts[0].shape[1] // 2, inverse.shape[0]
    return pl.pallas_call(
        whiten_kernel,
        in_specs=[pl.BlockSpec(memory_space=pltpu.SMEM)]
        + [pl.BlockSpec(memory_space=pltpu.VMEM)] * (3 + len(parts)),
        out_shape=jax.ShapeDtypeStruct((chunk * len(parts), rank), jnp.bfloat16),
        compiler_params=GRANT,
        cost_estimate=pl.CostEstimate(flops=12_000_000_000, bytes_accessed=4194304, transcendentals=0),
        name="project_half",
    )(spot, inverse, moment, other, *parts)


def chunk_kernel(spot_ref, rows_ref, sketch_ref, label_ref, *out_refs):
    core, here, line = (spot_ref[i] for i in range(3))
    rank = sketch_ref.shape[1]
    width = out_refs[0].shape[1] - 128
    half = rows_ref.shape[1] // 2
    sketch = sketch_ref[...]
    mul = functools.partial(
        lax.dot_general, dimension_numbers=ROW_DIMS, preferred_element_type=jnp.float32
    )
    gram_whole = mul(sketch, sketch)
    lane = lax.broadcasted_iota(jnp.int32, (rank, 128), 1)
    mine = pl.ds(pl.multiple_of((core * line + here) * SLOTS, SLOTS), SLOTS)
    for step in range(len(out_refs) // 2):
        chunk = spot_ref[3 + step]
        gram = pltpu.roll(gram_whole, rank - chunk * (rank * width // half), 1)[:, :128]
        gram = jnp.where(lane < rank * width // half, gram, 0.0)
        for out_ref, place in zip(out_refs[2 * step :], (1 - core, core)):
            columns = pl.ds(pl.multiple_of(place * half + chunk * width, width), width)
            out_ref[:, :width] = mul(sketch, rows_ref[:, columns])
            out_ref[:, width:] = gram
            theirs = pl.ds(pl.multiple_of((place * line + chunk) * SLOTS, SLOTS), SLOTS)
            out_ref[mine, width:] += label_ref[theirs, :]


def cross_chunks(spot, embeddings, sketch, labels, chunks, count):
    depth, dim = embeddings.shape
    rank = sketch.shape[1]
    width = dim // 2 // chunks
    shape = jax.ShapeDtypeStruct((rank, width + 128), jnp.float32)
    return pl.pallas_call(
        chunk_kernel,
        in_specs=[pl.BlockSpec(memory_space=pltpu.SMEM)]
        + [pl.BlockSpec(memory_space=pltpu.VMEM)] * 3,
        out_shape=[shape] * (2 * count),
        compiler_params=GRANT,
        cost_estimate=pl.CostEstimate(
            flops=4 * depth * rank * width * count, bytes_accessed=3000000, transcendentals=0
        ),
        name="cross_chunks",
    )(spot, embeddings, sketch, labels)


def join_kernel(side, keep_ref, got_ref, extra_ref, out_ref):
    height = extra_ref.shape[0]
    out_ref[...] = keep_ref[...] + got_ref[...]
    out_ref[side * height : (side + 1) * height, :] += extra_ref[...]


def join_chunk(keep, got, extra, side):
    return pl.pallas_call(
        functools.partial(join_kernel, side),
        out_shape=jax.ShapeDtypeStruct(keep.shape, jnp.float32),
        compiler_params=GRANT,
        cost_estimate=pl.CostEstimate(flops=400000, bytes_accessed=2000000, transcendentals=0),
        name="join_chunk",
    )(keep, got, extra)


def line_kernel(gram_piece, *refs):
    parts, out_ref = refs[:-1], refs[-1]
    plane = out_ref.shape[0]
    total = parts[0][...] + parts[1][...]
    for part_ref in parts[2:]:
        total = total + part_ref[...]
    rank, width = total.shape[0], total.shape[1] - 128
    piece = width // plane
    turned = total[:, :width].T.reshape(plane, piece, rank)
    out_ref[:, :piece, :] = turned[:, :, :128]
    out_ref[:, piece : 2 * piece, :] = turned[:, :, 128:]
    tail = total[:, width:].T.reshape(2, plane, gram_piece, rank)
    gram, labels = tail[0], tail[1][:, :1, :128]
    fill = jnp.zeros((plane, out_ref.shape[1] - 2 * (piece + gram_piece) - 1, 128), jnp.float32)
    out_ref[:, 2 * piece :, :] = jnp.concatenate(
        [gram[:, :, :128], gram[:, :, 128:], labels, fill], axis=1
    )


def line_total(parts, plane, gram_piece):
    width = parts[0].shape[1] - 128
    rows = 2 * (width // plane + gram_piece) + 1
    rows += -rows % 8
    return pl.pallas_call(
        functools.partial(line_kernel, gram_piece),
        out_shape=jax.ShapeDtypeStruct((plane, rows, 128), jnp.float32),
        compiler_params=GRANT,
        cost_estimate=pl.CostEstimate(flops=1000000, bytes_accessed=4000000, transcendentals=0),
        name="line_total",
    )(*parts)


def plane_kernel(label_row, parts_ref, out_ref, label_ref):
    out_ref[...] = jnp.broadcast_to(jnp.sum(parts_ref[...], axis=0, keepdims=True), out_ref.shape)
    label_ref[...] = parts_ref[:, label_row, :].astype(jnp.int32) - 1


def plane_total(parts, label_row):
    plane, _, lanes = parts.shape
    return pl.pallas_call(
        functools.partial(plane_kernel, label_row),
        out_shape=[
            jax.ShapeDtypeStruct(parts.shape, jnp.float32),
            jax.ShapeDtypeStruct((plane, lanes), jnp.int32),
        ],
        compiler_params=GRANT,
        cost_estimate=pl.CostEstimate(flops=1000000, bytes_accessed=1600000, transcendentals=0),
        name="plane_total",
    )(parts)


def whole_rows(part):
    plane, pair, lanes = part.shape
    sides = [part[:, : pair // 2], part[:, pair // 2 :]]
    return jnp.concatenate([t.reshape(plane * pair // 2, lanes) for t in sides], axis=1)


def product_kernel(core_ref, rows_ref, basis_ref, *refs):
    half, width = basis_ref.shape[0], 512
    total = None if len(refs) == 1 else refs[0][...]
    for step in range(half // width):
        columns = pl.ds(pl.multiple_of(core_ref[0] * half + step * width, width), width)
        basis = basis_ref[step * width : (step + 1) * width, :]
        term = jnp.dot(rows_ref[:, columns], basis, preferred_element_type=jnp.float32)
        total = term if total is None else total + term
    refs[-1][...] = total.astype(refs[-1].dtype)


def product_of_half(half, embeddings, basis, begin, out_type):
    depth, dim = embeddings.shape
    rank = basis.shape[1]
    extra = [] if begin is None else [begin]
    return pl.pallas_call(
        product_kernel,
        in_specs=[pl.BlockSpec(memory_space=pltpu.SMEM)]
        + [pl.BlockSpec(memory_space=pltpu.VMEM)] * (2 + len(extra)),
        out_shape=jax.ShapeDtypeStruct((depth, rank), out_type),
        compiler_params=GRANT,
        cost_estimate=pl.CostEstimate(
            flops=depth * dim * rank, bytes_accessed=depth * dim + dim * rank, transcendentals=0
        ),
        name="product_of_half",
    )(half, embeddings, basis, *extra)


def route_kernel(capacity, line, plane, ids_ref, map_ref, dest_ref, label_ref):
    ids = ids_ref[...]
    count, (high, low) = ids.shape[1], map_ref.shape
    owner_count = 2 * plane * line
    bf16 = jnp.bfloat16

    def rows_of(size):
        return lax.broadcasted_iota(jnp.int32, (size, count), 0)

    picked = (rows_of(high) == ids // low).astype(bf16)
    found = lax.dot_general(
        map_ref[...].astype(bf16), picked, ROW_DIMS, preferred_element_type=jnp.float32
    )
    owner = jnp.sum(jnp.where(rows_of(low) == ids % low, found, 0.0), axis=0, keepdims=True)
    owner = owner.astype(jnp.int32)
    mine = rows_of(owner_count) == owner
    order = lax.broadcasted_iota(jnp.int32, (count, count), 1)
    earlier = (lax.broadcasted_iota(jnp.int32, (count, count), 0) < order).astype(bf16)
    before = jnp.dot(mine.astype(bf16), earlier, preferred_element_type=jnp.float32)
    slot = jnp.sum(jnp.where(mine, before, 0.0), axis=0, keepdims=True).astype(jnp.int32)
    dest_ref[...] = owner * capacity + slot
    value = ids + 1
    core, chip = owner // (plane * line), owner % (plane * line)
    row = (core * line + chip % line) * SLOTS + slot
    lane = rows_of(128) == 64 + 2 * (chip // line)
    lane = lane.astype(bf16)
    labels = None
    for digit in range(3):
        short = (value // 128**digit) % 128
        spread = jnp.where(rows_of(2 * line * SLOTS) == row, short.astype(jnp.float32), 0.0)
        term = lax.dot_general(
            spread.astype(bf16),
            lane,
            (((1,), (1,)), ((), ())),
            preferred_element_type=jnp.float32,
        )
        labels = term if labels is None else labels + term * 128**digit
    label_ref[...] = labels


def route_rows(list_ids, owner_map, capacity, line, plane):
    count = list_ids.shape[0]
    return pl.pallas_call(
        functools.partial(route_kernel, capacity, line, plane),
        out_shape=[
            jax.ShapeDtypeStruct((1, count), jnp.int32),
            jax.ShapeDtypeStruct((2 * line * SLOTS, 128), jnp.float32),
        ],
        compiler_params=GRANT,
        cost_estimate=pl.CostEstimate(
            flops=2_000_000_000, bytes_accessed=1048576, transcendentals=0
        ),
        name="route_rows",
    )(list_ids.reshape(1, count), owner_map.reshape(-1, 128))


def place_kernel(capacity, target_ref, first_ref, second_ref, out_ref):
    pairs, _, width = out_ref.shape
    count = pairs * 2 * capacity
    slots = pl.program_id(0) * count + lax.broadcasted_iota(
        jnp.int32, (count, first_ref.shape[0]), 0
    )
    found = []
    for part, rows_ref in enumerate((first_ref, second_ref)):
        onehot = (slots == target_ref[part : part + 1, :]).astype(jnp.bfloat16)
        term = jnp.dot(onehot, rows_ref[...], preferred_element_type=jnp.float32)
        found.append(term.reshape(pairs, 2 * capacity, width))
    a, b = found
    out_ref[...] = jnp.concatenate(
        [a[:, :capacity], b[:, :capacity], a[:, capacity:], b[:, capacity:]], axis=1
    ).astype(jnp.bfloat16)


def place_rows(target, first, second, chips, capacity):
    pairs = 16
    depth, width = first.shape
    return pl.pallas_call(
        functools.partial(place_kernel, capacity),
        grid=(chips // 2 // pairs,),
        in_specs=[pl.BlockSpec((2, depth), lambda i: (0, 0))]
        + [pl.BlockSpec((depth, width), lambda i: (0, 0))] * 2,
        out_specs=pl.BlockSpec((pairs, 4 * capacity, width), lambda i: (i, 0, 0)),
        out_shape=jax.ShapeDtypeStruct((chips // 2, 4 * capacity, width), jnp.bfloat16),
        compiler_params=GRANT,
        cost_estimate=pl.CostEstimate(
            flops=4 * chips * capacity * depth * width,
            bytes_accessed=8 * chips * capacity * width,
            transcendentals=0,
        ),
        name="place_rows",
    )(target, first, second)


def shift(value, axis, step):
    size = lax.axis_size(axis)
    return lax.ppermute(value, axis, [(i, (i + step) % size) for i in range(size)])


def local(embeddings, sketch_seed, list_ids, owner_map):
    row_count, dim = embeddings.shape
    rank = sketch_seed.shape[1]
    cores, line = lax.axis_size("narrow"), lax.axis_size("x")
    plane = lax.axis_size("y") * lax.axis_size("z")
    chips = plane * line
    dev_count = cores * chips
    core = lax.axis_index("narrow")
    spot = lax.axis_index("x").reshape(1)
    own_half, other_half = core.reshape(1), (1 - core).reshape(1)
    piece, gram_piece = dim // dev_count, rank // chips
    seed_matrix = sketch_seed.astype(jnp.bfloat16)
    sketch = jnp.dot(embeddings, seed_matrix, preferred_element_type=jnp.float32).astype(
        jnp.bfloat16
    )

    capacity = 4 * row_count // dev_count
    here = lax.axis_index("x")
    dest_index, labels = route_rows(list_ids, owner_map, capacity, line, plane)

    def chunks_at(*steps):
        places = [(here + step) % line for step in steps]
        spot = jnp.stack([core, here, jnp.int32(line)] + places)
        pairs = cross_chunks(spot, embeddings, sketch, labels, line, len(steps))
        return [(pairs[2 * i + 1], shift(pairs[2 * i], "narrow", 1)) for i in range(len(steps))]

    (far,) = chunks_at(2)
    up, down, near = chunks_at(1, 3, 0)
    far = far[0] + far[1]
    from_below = shift(far[: rank // 2], "x", 1)
    from_above = shift(far[rank // 2 :], "x", line - 1)
    from_below = shift(join_chunk(*up, from_below, 0), "x", 1)
    from_above = shift(join_chunk(*down, from_above, 1), "x", line - 1)

    both_dest = jnp.concatenate([dest_index, shift(dest_index, "narrow", 1)])
    both_owner = both_dest // capacity
    target = (both_owner % chips) * capacity + both_dest % capacity
    target = jnp.where(both_owner // chips == core, target, -1)
    target = jnp.where(core == 0, target, target[::-1])

    packed = line_total([*near, from_below, from_above], plane, gram_piece)
    packed = lax.all_to_all(packed, PLANE, 0, 0, tiled=True)
    packed, target = lax.optimization_barrier((packed, target))
    packed, arrived_labels = plane_total(packed, 2 * (piece + gram_piece))
    packed = lax.all_to_all(packed, PLANE, 0, 0, tiled=True)
    gram_line = packed[:, 2 * piece : 2 * (piece + gram_piece)]
    gram_line = jnp.concatenate([gram_line[:, :gram_piece], gram_line[:, gram_piece:]], axis=2)
    gram_line = gram_line.reshape(-1, rank)
    gram_parts = [gram_line] + [shift(gram_line, "x", step) for step in range(1, line)]
    packed, gram_parts[1] = lax.optimization_barrier((packed, gram_parts[1]))
    cross_line = packed[:, : 2 * piece]
    cross_parts = [cross_line] + [shift(cross_line, "x", step) for step in range(1, line)]
    arrived_labels = arrived_labels[:, : cores * line * SLOTS].reshape(plane, cores, line, SLOTS)
    arrived_labels = arrived_labels[..., :capacity].transpose(1, 0, 2, 3)

    inverse = invert_factor(spot, gram_parts)
    inverse, cross_parts = lax.optimization_barrier((inverse, cross_parts))
    moment = moment_of(cross_parts)
    basis = project_half(spot, inverse, moment, shift(moment, "narrow", 1), cross_parts)
    other_basis = shift(basis, "narrow", 1)
    begun = product_of_half(own_half, embeddings, basis, None, jnp.float32)
    reduced = product_of_half(other_half, embeddings, other_basis, begun, jnp.bfloat16)
    other = shift(reduced, "narrow", 1)
    send_rows = place_rows(
        target,
        jnp.where(core == 0, reduced, other),
        jnp.where(core == 0, other, reduced),
        chips,
        capacity,
    )
    send_rows = send_rows.reshape(chips, cores * capacity, rank)
    arrived = lax.all_to_all(send_rows, ("y", "z", "x"), 0, 0, tiled=True)
    arrived = arrived.reshape(chips, cores, capacity, rank).transpose(1, 0, 2, 3)
    return (
        arrived.reshape(1, dev_count, capacity, rank),
        arrived_labels.reshape(1, dev_count, capacity),
    )


def solution(mesh):
    grid = Mesh(mesh.devices.reshape(2, 4, 8, 4), ALL)
    in_specs = (P(ALL, None), P(), P(ALL), P())
    out_specs = (P(ALL, None, None, None), P(ALL, None, None))
    return jax.shard_map(local, mesh=grid, in_specs=in_specs, out_specs=out_specs, check_vma=False)
```

```python
import functools

import jax
import jax.numpy as jnp
from jax import lax
from jax.experimental import pallas as pl
from jax.experimental.pallas import tpu as pltpu
from jax.sharding import Mesh
from jax.sharding import PartitionSpec as P

NS_STEPS = 6
BLOCK = 64
TILE = 16
ALL = ("narrow", "y", "z", "x")
PLANE = ("y", "z")
HIGHEST = lax.Precision.HIGHEST
ROW_DIMS = (((0,), (0,)), ((), ()))
SLOTS = 16
GRANT = pltpu.CompilerParams(vmem_limit_bytes=16 * 2**20)


def dot_f32(a, b, dims=(((1,), (0,)), ((), ()))):
    return lax.dot_general(a, b, dims, precision=HIGHEST, preferred_element_type=jnp.float32)


def split_two(a):
    high = a.astype(jnp.bfloat16)
    return high, (a - high.astype(jnp.float32)).astype(jnp.bfloat16)


def dot_split(a, b):
    (ah, al), (bh, bl) = a, b
    mul = functools.partial(jnp.dot, preferred_element_type=jnp.float32)
    return mul(ah, bh) + (mul(ah, bl) + mul(al, bh))


def invert_kernel(spot_ref, *refs):
    parts, inverse_ref, work_ref = refs[:-2], refs[-2], refs[-1]
    rank = inverse_ref.shape[0]
    height = rank // len(parts)
    row_ids = lax.broadcasted_iota(jnp.int32, (rank, rank), 0)
    col_ids = lax.broadcasted_iota(jnp.int32, (rank, rank), 1)
    for step, part_ref in enumerate(parts):
        place = lax.rem(spot_ref[0] + len(parts) - step, len(parts))
        work_ref[pl.ds(pl.multiple_of(place * height, height), height), :rank] = part_ref[...]
    work_ref[:, rank:] = (row_ids == col_ids).astype(jnp.float32)
    lane = lax.broadcasted_iota(jnp.int32, (BLOCK, 128), 1)
    row = lax.broadcasted_iota(jnp.int32, (BLOCK, 128), 0)
    panel_lane = lax.broadcasted_iota(jnp.int32, (BLOCK, rank), 1)

    def block_step(step, carry):
        start = pl.multiple_of(step * BLOCK, BLOCK)
        panel = work_ref[pl.ds(start, BLOCK), :]
        shifted = pltpu.roll(panel[:, :rank], rank - start, 1)[:, :128]
        rest = jnp.where(lane < BLOCK, shifted, (lane - BLOCK == row).astype(jnp.float32))
        done = []
        for tile in range(BLOCK // TILE):
            height = BLOCK - tile * TILE
            sub = lax.broadcasted_iota(jnp.int32, (height, 128), 0)
            columns = [
                jnp.broadcast_to(rest[:, tile * TILE + j : tile * TILE + j + 1], (height, 128))
                for j in range(TILE)
            ]
            for j in range(TILE):
                pivot = columns[j][j : j + 1, :]
                scale = lax.rsqrt(pivot)
                scale = scale * (1.5 - 0.5 * (pivot * scale) * scale)
                below = jnp.where(sub > j, columns[j] * scale, 0.0)
                lead = rest[j : j + 1, :] * scale
                done.append(lead)
                rest = rest - below * lead
                for m in range(j + 1, TILE):
                    columns[m] = columns[m] - below * (columns[m][j : j + 1, :] * scale)
            rest = rest[TILE:, :]
        solved = jnp.concatenate(done, axis=0)
        small = pltpu.roll(solved, 128 - BLOCK, 1)[:, :BLOCK]
        panel = dot_f32(small, panel)
        inverse_ref[pl.ds(start, BLOCK), :] = panel[:, rank:]
        later = jnp.where(panel_lane >= start + BLOCK, panel[:, :rank], 0.0)
        work_ref[...] -= dot_f32(later, panel, (((0,), (0,)), ((), ())))
        return carry

    lax.fori_loop(0, rank // BLOCK, block_step, 0)


def invert_factor(spot, parts):
    rank = parts[0].shape[1]
    return pl.pallas_call(
        invert_kernel,
        in_specs=[pl.BlockSpec(memory_space=pltpu.SMEM)]
        + [pl.BlockSpec(memory_space=pltpu.VMEM)] * len(parts),
        out_shape=jax.ShapeDtypeStruct((rank, rank), jnp.float32),
        scratch_shapes=[pltpu.VMEM((rank, 2 * rank), jnp.float32)],
        compiler_params=GRANT,
        cost_estimate=pl.CostEstimate(flops=20_000_000_000, bytes_accessed=524288, transcendentals=0),
        name="invert_factor",
    )(spot, *parts)


def moment_kernel(*refs):
    total = None
    for part_ref in refs[:-1]:
        part = whole_rows(part_ref[...])
        term = dot_f32(part, part, ROW_DIMS)
        total = term if total is None else total + term
    refs[-1][...] = total


def moment_of(parts):
    rank = 2 * parts[0].shape[2]
    return pl.pallas_call(
        moment_kernel,
        out_shape=jax.ShapeDtypeStruct((rank, rank), jnp.float32),
        compiler_params=GRANT,
        cost_estimate=pl.CostEstimate(flops=4_000_000_000, bytes_accessed=2359296, transcendentals=0),
        name="moment_of",
    )(*parts)


def whiten_kernel(spot_ref, inverse_ref, moment_ref, other_ref, *refs):
    parts, out_ref = refs[:-1], refs[-1]
    inverse = inverse_ref[...]
    rank = inverse.shape[0]
    moment = moment_ref[...] + other_ref[...]
    cov_total = dot_f32(dot_f32(inverse, moment), inverse, (((1,), (1,)), ((), ())))
    row_ids = lax.broadcasted_iota(jnp.int32, (rank, rank), 0)
    col_ids = lax.broadcasted_iota(jnp.int32, (rank, rank), 1)
    eye_matrix = (row_ids == col_ids).astype(jnp.float32)
    trace_value = jnp.sum(cov_total * eye_matrix, axis=(0, 1), keepdims=True)
    left_iter = cov_total / trace_value
    right_iter = 1.5 * eye_matrix - 0.5 * left_iter
    right_parts = split_two(right_iter)
    left_parts = split_two(dot_split(split_two(left_iter), right_parts))
    for step_index in range(1, NS_STEPS):
        middle = split_two(1.5 * eye_matrix - 0.5 * dot_split(right_parts, left_parts))
        right_iter = dot_split(middle, right_parts)
        if step_index < NS_STEPS - 1:
            left_parts = split_two(dot_split(left_parts, middle))
            right_parts = split_two(right_iter)
    factor = right_iter / jnp.sqrt(trace_value)
    weight = split_two(dot_f32(inverse, factor, ROW_DIMS))
    height = out_ref.shape[0] // len(parts)
    for step, part_ref in enumerate(parts):
        place = lax.rem(spot_ref[0] + len(parts) - step, len(parts))
        rows = pl.ds(pl.multiple_of(place * height, height), height)
        out_ref[rows, :] = dot_split(split_two(whole_rows(part_ref[...])), weight).astype(jnp.bfloat16)


def project_half(spot, inverse, moment, other, parts):
    chunk, rank = parts[0].shape[0] * parts[0].shape[1] // 2, inverse.shape[0]
    return pl.pallas_call(
        whiten_kernel,
        in_specs=[pl.BlockSpec(memory_space=pltpu.SMEM)]
        + [pl.BlockSpec(memory_space=pltpu.VMEM)] * (3 + len(parts)),
        out_shape=jax.ShapeDtypeStruct((chunk * len(parts), rank), jnp.bfloat16),
        compiler_params=GRANT,
        cost_estimate=pl.CostEstimate(flops=12_000_000_000, bytes_accessed=4194304, transcendentals=0),
        name="project_half",
    )(spot, inverse, moment, other, *parts)


def chunk_kernel(steps, spot_ref, rows_ref, sketch_ref, label_ref, *out_refs):
    core, here, line = (spot_ref[i] for i in range(3))
    rank = sketch_ref.shape[1]
    width = out_refs[0].shape[1] - 128
    half = rows_ref.shape[1] // 2
    sketch = sketch_ref[...]
    mul = functools.partial(
        lax.dot_general, dimension_numbers=ROW_DIMS, preferred_element_type=jnp.float32
    )
    gram_whole = mul(sketch, sketch)
    lane = lax.broadcasted_iota(jnp.int32, (rank, 128), 1)
    mine = pl.ds(pl.multiple_of((core * line + here) * SLOTS, SLOTS), SLOTS)
    for index, step in enumerate(steps):
        chunk = lax.rem(here + step, line)
        gram = pltpu.roll(gram_whole, rank - chunk * (rank * width // half), 1)[:, :128]
        gram = jnp.where(lane < rank * width // half, gram, 0.0)
        for out_ref, place in zip(out_refs[2 * index :], (1 - core, core)):
            columns = pl.ds(pl.multiple_of(place * half + chunk * width, width), width)
            out_ref[:, :width] = mul(sketch, rows_ref[:, columns])
            out_ref[:, width:] = gram
            theirs = pl.ds(pl.multiple_of((place * line + chunk) * SLOTS, SLOTS), SLOTS)
            out_ref[mine, width:] += label_ref[theirs, :]


def cross_chunks(spot, embeddings, sketch, labels, chunks, steps):
    count = len(steps)
    depth, dim = embeddings.shape
    rank = sketch.shape[1]
    width = dim // 2 // chunks
    shape = jax.ShapeDtypeStruct((rank, width + 128), jnp.float32)
    return pl.pallas_call(
        functools.partial(chunk_kernel, steps),
        in_specs=[pl.BlockSpec(memory_space=pltpu.SMEM)]
        + [pl.BlockSpec(memory_space=pltpu.VMEM)] * 3,
        out_shape=[shape] * (2 * count),
        compiler_params=GRANT,
        cost_estimate=pl.CostEstimate(
            flops=4 * depth * rank * width * count, bytes_accessed=3000000, transcendentals=0
        ),
        name="cross_chunks",
    )(spot, embeddings, sketch, labels)


def join_kernel(side, keep_ref, got_ref, extra_ref, out_ref):
    height = extra_ref.shape[0]
    out_ref[...] = keep_ref[...] + got_ref[...]
    out_ref[side * height : (side + 1) * height, :] += extra_ref[...]


def join_chunk(keep, got, extra, side):
    return pl.pallas_call(
        functools.partial(join_kernel, side),
        out_shape=jax.ShapeDtypeStruct(keep.shape, jnp.float32),
        compiler_params=GRANT,
        cost_estimate=pl.CostEstimate(flops=400000, bytes_accessed=2000000, transcendentals=0),
        name="join_chunk",
    )(keep, got, extra)


def line_kernel(gram_piece, *refs):
    parts, out_ref = refs[:-1], refs[-1]
    plane = out_ref.shape[0]
    total = parts[0][...] + parts[1][...]
    for part_ref in parts[2:]:
        total = total + part_ref[...]
    rank, width = total.shape[0], total.shape[1] - 128
    piece = width // plane
    turned = total[:, :width].T.reshape(plane, piece, rank)
    out_ref[:, :piece, :] = turned[:, :, :128]
    out_ref[:, piece : 2 * piece, :] = turned[:, :, 128:]
    tail = total[:, width:].T.reshape(2, plane, gram_piece, rank)
    gram, labels = tail[0], tail[1][:, :1, :128]
    fill = jnp.zeros((plane, out_ref.shape[1] - 2 * (piece + gram_piece) - 1, 128), jnp.float32)
    out_ref[:, 2 * piece :, :] = jnp.concatenate(
        [gram[:, :, :128], gram[:, :, 128:], labels, fill], axis=1
    )


def line_total(parts, plane, gram_piece):
    width = parts[0].shape[1] - 128
    rows = 2 * (width // plane + gram_piece) + 1
    rows += -rows % 8
    return pl.pallas_call(
        functools.partial(line_kernel, gram_piece),
        out_shape=jax.ShapeDtypeStruct((plane, rows, 128), jnp.float32),
        compiler_params=GRANT,
        cost_estimate=pl.CostEstimate(flops=1000000, bytes_accessed=4000000, transcendentals=0),
        name="line_total",
    )(*parts)


def plane_kernel(label_row, parts_ref, out_ref, label_ref):
    out_ref[...] = jnp.broadcast_to(jnp.sum(parts_ref[...], axis=0, keepdims=True), out_ref.shape)
    label_ref[...] = parts_ref[:, label_row, :].astype(jnp.int32) - 1


def plane_total(parts, label_row):
    plane, _, lanes = parts.shape
    return pl.pallas_call(
        functools.partial(plane_kernel, label_row),
        out_shape=[
            jax.ShapeDtypeStruct(parts.shape, jnp.float32),
            jax.ShapeDtypeStruct((plane, lanes), jnp.int32),
        ],
        compiler_params=GRANT,
        cost_estimate=pl.CostEstimate(flops=1000000, bytes_accessed=1600000, transcendentals=0),
        name="plane_total",
    )(parts)


def whole_rows(part):
    plane, pair, lanes = part.shape
    sides = [part[:, : pair // 2], part[:, pair // 2 :]]
    return jnp.concatenate([t.reshape(plane * pair // 2, lanes) for t in sides], axis=1)


def gram_kernel(piece, gram_piece, parts_ref, out_ref):
    start = 2 * piece
    out_ref[...] = whole_rows(parts_ref[:, start : start + 2 * gram_piece, :])


def gram_rows(parts, piece, gram_piece):
    plane, _, lanes = parts.shape
    return pl.pallas_call(
        functools.partial(gram_kernel, piece, gram_piece),
        out_shape=jax.ShapeDtypeStruct((plane * gram_piece, 2 * lanes), jnp.float32),
        compiler_params=GRANT,
        cost_estimate=pl.CostEstimate(flops=10000, bytes_accessed=200000, transcendentals=0),
        name="gram_rows",
    )(parts)


def product_kernel(core_ref, rows_ref, basis_ref, *refs):
    half, width = basis_ref.shape[0], 512
    total = None if len(refs) == 1 else refs[0][...]
    for step in range(half // width):
        columns = pl.ds(pl.multiple_of(core_ref[0] * half + step * width, width), width)
        basis = basis_ref[step * width : (step + 1) * width, :]
        term = jnp.dot(rows_ref[:, columns], basis, preferred_element_type=jnp.float32)
        total = term if total is None else total + term
    refs[-1][...] = total.astype(refs[-1].dtype)


def product_of_half(half, embeddings, basis, begin, out_type):
    depth, dim = embeddings.shape
    rank = basis.shape[1]
    extra = [] if begin is None else [begin]
    return pl.pallas_call(
        product_kernel,
        in_specs=[pl.BlockSpec(memory_space=pltpu.SMEM)]
        + [pl.BlockSpec(memory_space=pltpu.VMEM)] * (2 + len(extra)),
        out_shape=jax.ShapeDtypeStruct((depth, rank), out_type),
        compiler_params=GRANT,
        cost_estimate=pl.CostEstimate(
            flops=depth * dim * rank, bytes_accessed=depth * dim + dim * rank, transcendentals=0
        ),
        name="product_of_half",
    )(half, embeddings, basis, *extra)


def route_kernel(capacity, line, plane, ids_ref, map_ref, dest_ref, label_ref):
    ids = jnp.concatenate([ids_ref[k : k + 1, :] for k in range(ids_ref.shape[0])], axis=1)
    count, (high, low) = ids.shape[1], map_ref.shape
    owner_count = 2 * plane * line
    bf16 = jnp.bfloat16

    def rows_of(size):
        return lax.broadcasted_iota(jnp.int32, (size, count), 0)

    picked = (rows_of(high) == ids // low).astype(bf16)
    found = lax.dot_general(
        map_ref[...].astype(bf16), picked, ROW_DIMS, preferred_element_type=jnp.float32
    )
    owner = jnp.sum(jnp.where(rows_of(low) == ids % low, found, 0.0), axis=0, keepdims=True)
    owner = owner.astype(jnp.int32)
    mine = rows_of(owner_count) == owner
    order = lax.broadcasted_iota(jnp.int32, (count, count), 1)
    earlier = (lax.broadcasted_iota(jnp.int32, (count, count), 0) < order).astype(bf16)
    before = jnp.dot(mine.astype(bf16), earlier, preferred_element_type=jnp.float32)
    slot = jnp.sum(jnp.where(mine, before, 0.0), axis=0, keepdims=True).astype(jnp.int32)
    dest_ref[...] = owner * capacity + slot
    value = ids + 1
    core, chip = owner // (plane * line), owner % (plane * line)
    row = (core * line + chip % line) * SLOTS + slot
    lane = rows_of(128) == 64 + 2 * (chip // line)
    lane = lane.astype(bf16)
    labels = None
    for digit in range(3):
        short = (value // 128**digit) % 128
        spread = jnp.where(rows_of(2 * line * SLOTS) == row, short.astype(jnp.float32), 0.0)
        term = lax.dot_general(
            spread.astype(bf16),
            lane,
            (((1,), (1,)), ((), ())),
            preferred_element_type=jnp.float32,
        )
        labels = term if labels is None else labels + term * 128**digit
    label_ref[...] = labels


def route_rows(list_ids, owner_map, capacity, line, plane):
    count = list_ids.shape[0]
    return pl.pallas_call(
        functools.partial(route_kernel, capacity, line, plane),
        out_shape=[
            jax.ShapeDtypeStruct((1, count), jnp.int32),
            jax.ShapeDtypeStruct((2 * line * SLOTS, 128), jnp.float32),
        ],
        compiler_params=GRANT,
        cost_estimate=pl.CostEstimate(
            flops=2_000_000_000, bytes_accessed=1048576, transcendentals=0
        ),
        name="route_rows",
    )(list_ids.reshape(-1, 128), owner_map.reshape(-1, 128))


def place_kernel(capacity, first_target, second_target, first_ref, second_ref, out_ref):
    pairs, _, width = out_ref.shape
    count = pairs * 2 * capacity
    slots = pl.program_id(0) * count + lax.broadcasted_iota(
        jnp.int32, (count, first_ref.shape[0]), 0
    )
    found = []
    for target_ref, rows_ref in ((first_target, first_ref), (second_target, second_ref)):
        onehot = (slots == target_ref[...]).astype(jnp.bfloat16)
        term = jnp.dot(onehot, rows_ref[...], preferred_element_type=jnp.float32)
        found.append(term.reshape(pairs, 2 * capacity, width))
    a, b = found
    out_ref[...] = jnp.concatenate(
        [a[:, :capacity], b[:, :capacity], a[:, capacity:], b[:, capacity:]], axis=1
    ).astype(jnp.bfloat16)


def place_rows(targets, first, second, chips, capacity):
    pairs = 16
    depth, width = first.shape
    return pl.pallas_call(
        functools.partial(place_kernel, capacity),
        grid=(chips // 2 // pairs,),
        in_specs=[pl.BlockSpec((1, depth), lambda i: (0, 0))] * 2
        + [pl.BlockSpec((depth, width), lambda i: (0, 0))] * 2,
        out_specs=pl.BlockSpec((pairs, 4 * capacity, width), lambda i: (i, 0, 0)),
        out_shape=jax.ShapeDtypeStruct((chips // 2, 4 * capacity, width), jnp.bfloat16),
        compiler_params=GRANT,
        cost_estimate=pl.CostEstimate(
            flops=4 * chips * capacity * depth * width,
            bytes_accessed=8 * chips * capacity * width,
            transcendentals=0,
        ),
        name="place_rows",
    )(*targets, first, second)


def shift(value, axis, step):
    size = lax.axis_size(axis)
    return lax.ppermute(value, axis, [(i, (i + step) % size) for i in range(size)])


def local(embeddings, sketch_seed, list_ids, owner_map):
    row_count, dim = embeddings.shape
    rank = sketch_seed.shape[1]
    cores, line = lax.axis_size("narrow"), lax.axis_size("x")
    plane = lax.axis_size("y") * lax.axis_size("z")
    chips = plane * line
    dev_count = cores * chips
    core = lax.axis_index("narrow")
    spot = lax.axis_index("x").reshape(1)
    own_half, other_half = core.reshape(1), (1 - core).reshape(1)
    piece, gram_piece = dim // dev_count, rank // chips
    seed_matrix = sketch_seed.astype(jnp.bfloat16)
    sketch = jnp.dot(embeddings, seed_matrix, preferred_element_type=jnp.float32).astype(
        jnp.bfloat16
    )

    capacity = 4 * row_count // dev_count
    here = lax.axis_index("x")
    dest_index, labels = route_rows(list_ids, owner_map, capacity, line, plane)

    spots = jnp.stack([core, here, jnp.int32(line)])

    def chunks_at(*steps):
        pairs = cross_chunks(spots, embeddings, sketch, labels, line, steps)
        return [(pairs[2 * i + 1], shift(pairs[2 * i], "narrow", 1)) for i in range(len(steps))]

    (far,) = chunks_at(2)
    up, down, near = chunks_at(1, 3, 0)
    far = far[0] + far[1]
    from_below = shift(far[: rank // 2], "x", 1)
    from_above = shift(far[rank // 2 :], "x", line - 1)
    from_below = shift(join_chunk(*up, from_below, 0), "x", 1)
    from_above = shift(join_chunk(*down, from_above, 1), "x", line - 1)

    def target_of(dest):
        owner = dest // capacity
        return jnp.where(owner // chips == core, (owner % chips) * capacity + dest % capacity, -1)

    def by_core(own, other):
        return jnp.where(core == 0, own, other), jnp.where(core == 0, other, own)

    targets = by_core(target_of(dest_index), target_of(shift(dest_index, "narrow", 1)))

    packed = line_total([*near, from_below, from_above], plane, gram_piece)
    packed, targets = lax.optimization_barrier((packed, targets))
    packed = lax.all_to_all(packed, PLANE, 0, 0, tiled=True)
    packed, arrived_labels = plane_total(packed, 2 * (piece + gram_piece))
    packed = lax.all_to_all(packed, PLANE, 0, 0, tiled=True)
    gram_line = gram_rows(packed, piece, gram_piece)
    gram_parts = [gram_line] + [shift(gram_line, "x", step) for step in range(1, line)]
    packed, gram_parts[1] = lax.optimization_barrier((packed, gram_parts[1]))
    cross_line = packed[:, : 2 * piece]
    cross_parts = [cross_line] + [shift(cross_line, "x", step) for step in range(1, line)]
    arrived_labels = arrived_labels[:, : cores * line * SLOTS].reshape(plane, cores, line, SLOTS)
    arrived_labels = arrived_labels[..., :capacity].transpose(1, 0, 2, 3)

    inverse = invert_factor(spot, gram_parts)
    inverse, cross_parts = lax.optimization_barrier((inverse, cross_parts))
    moment = moment_of(cross_parts)
    basis = project_half(spot, inverse, moment, shift(moment, "narrow", 1), cross_parts)
    other_basis = shift(basis, "narrow", 1)
    begun = product_of_half(own_half, embeddings, basis, None, jnp.float32)
    reduced = product_of_half(other_half, embeddings, other_basis, begun, jnp.bfloat16)
    rows = by_core(reduced, shift(reduced, "narrow", 1))
    send_rows = place_rows(targets, *rows, chips, capacity)
    send_rows = send_rows.reshape(chips, cores * capacity, rank)
    arrived = lax.all_to_all(send_rows, ("y", "z", "x"), 0, 0, tiled=True)
    arrived = arrived.reshape(chips, cores, capacity, rank).transpose(1, 0, 2, 3)
    return (
        arrived.reshape(1, dev_count, capacity, rank),
        arrived_labels.reshape(1, dev_count, capacity),
    )


def solution(mesh):
    grid = Mesh(mesh.devices.reshape(2, 4, 8, 4), ALL)
    in_specs = (P(ALL, None), P(), P(ALL), P())
    out_specs = (P(ALL, None, None, None), P(ALL, None, None))
    return jax.shard_map(local, mesh=grid, in_specs=in_specs, out_specs=out_specs, check_vma=False)
```

```python
import functools

import jax
import jax.numpy as jnp
from jax import lax
from jax.experimental import pallas as pl
from jax.experimental.pallas import tpu as pltpu
from jax.sharding import Mesh
from jax.sharding import PartitionSpec as P

NS_STEPS = 6
BLOCK = 64
TILE = 16
ALL = ("narrow", "y", "z", "x")
PLANE = ("y", "z")
HIGHEST = lax.Precision.HIGHEST
ROW_DIMS = (((0,), (0,)), ((), ()))
SLOTS = 16
GRANT = pltpu.CompilerParams(vmem_limit_bytes=16 * 2**20)


def dot_f32(a, b, dims=(((1,), (0,)), ((), ()))):
    return lax.dot_general(a, b, dims, precision=HIGHEST, preferred_element_type=jnp.float32)


def split_two(a):
    high = a.astype(jnp.bfloat16)
    return high, (a - high.astype(jnp.float32)).astype(jnp.bfloat16)


def dot_split(a, b):
    (ah, al), (bh, bl) = a, b
    mul = functools.partial(jnp.dot, preferred_element_type=jnp.float32)
    return mul(ah, bh) + (mul(ah, bl) + mul(al, bh))


POWERS = (64, 32, 16, 8, 4)


def scaled(value):
    top = jnp.max(jnp.abs(value), axis=(0, 1), keepdims=True)
    factor, power = jnp.ones_like(top), jnp.zeros_like(top)
    for p in POWERS:
        large = top * factor >= 2.0 ** (11 + p)
        factor = jnp.where(large, factor * 2.0**-p, factor)
        power = jnp.where(large, power - p, power)
    for p in POWERS:
        small = top * factor < 2.0 ** (15 - p)
        factor = jnp.where(small, factor * 2.0**p, factor)
        power = jnp.where(small, power + p, power)
    return value * factor, power


def unscale_factor(power):
    factor = jnp.ones_like(power)
    for p in POWERS:
        up, down = power >= p, power <= -p
        factor = jnp.where(up, factor * 2.0**-p, jnp.where(down, factor * 2.0**p, factor))
        power = jnp.where(up, power - p, jnp.where(down, power + p, power))
    return factor


def invert_kernel(spot_ref, *refs):
    parts, inverse_ref, work_ref = refs[:-2], refs[-2], refs[-1]
    rank = inverse_ref.shape[0]
    height = rank // len(parts)
    row_ids = lax.broadcasted_iota(jnp.int32, (rank, rank), 0)
    col_ids = lax.broadcasted_iota(jnp.int32, (rank, rank), 1)
    for step, part_ref in enumerate(parts):
        place = lax.rem(spot_ref[0] + len(parts) - step, len(parts))
        work_ref[pl.ds(pl.multiple_of(place * height, height), height), :rank] = part_ref[...]
    work_ref[:, rank:] = (row_ids == col_ids).astype(jnp.float32)
    lane = lax.broadcasted_iota(jnp.int32, (BLOCK, 128), 1)
    row = lax.broadcasted_iota(jnp.int32, (BLOCK, 128), 0)
    panel_lane = lax.broadcasted_iota(jnp.int32, (BLOCK, rank), 1)

    def block_step(step, carry):
        start = pl.multiple_of(step * BLOCK, BLOCK)
        panel = work_ref[pl.ds(start, BLOCK), :]
        shifted = pltpu.roll(panel[:, :rank], rank - start, 1)[:, :128]
        rest = jnp.where(lane < BLOCK, shifted, (lane - BLOCK == row).astype(jnp.float32))
        done = []
        for tile in range(BLOCK // TILE):
            height = BLOCK - tile * TILE
            sub = lax.broadcasted_iota(jnp.int32, (height, 128), 0)
            columns = [
                jnp.broadcast_to(rest[:, tile * TILE + j : tile * TILE + j + 1], (height, 128))
                for j in range(TILE)
            ]
            for j in range(TILE):
                pivot = columns[j][j : j + 1, :]
                scale = lax.rsqrt(pivot)
                scale = scale * (1.5 - 0.5 * (pivot * scale) * scale)
                below = jnp.where(sub > j, columns[j] * scale, 0.0)
                lead = rest[j : j + 1, :] * scale
                done.append(lead)
                rest = rest - below * lead
                for m in range(j + 1, TILE):
                    columns[m] = columns[m] - below * (columns[m][j : j + 1, :] * scale)
            rest = rest[TILE:, :]
        solved = jnp.concatenate(done, axis=0)
        small = pltpu.roll(solved, 128 - BLOCK, 1)[:, :BLOCK]
        panel = dot_f32(small, panel)
        inverse_ref[pl.ds(start, BLOCK), :] = panel[:, rank:]
        later = jnp.where(panel_lane >= start + BLOCK, panel[:, :rank], 0.0)
        work_ref[...] -= dot_f32(later, panel, (((0,), (0,)), ((), ())))
        return carry

    lax.fori_loop(0, rank // BLOCK, block_step, 0)


def invert_factor(spot, parts):
    rank = parts[0].shape[1]
    return pl.pallas_call(
        invert_kernel,
        in_specs=[pl.BlockSpec(memory_space=pltpu.SMEM)]
        + [pl.BlockSpec(memory_space=pltpu.VMEM)] * len(parts),
        out_shape=jax.ShapeDtypeStruct((rank, rank), jnp.float32),
        scratch_shapes=[pltpu.VMEM((rank, 2 * rank), jnp.float32)],
        compiler_params=GRANT,
        cost_estimate=pl.CostEstimate(flops=20_000_000_000, bytes_accessed=524288, transcendentals=0),
        name="invert_factor",
    )(spot, *parts)


def moment_kernel(*refs):
    total = None
    for part_ref in refs[:-1]:
        part = plain_rows(part_ref)
        term = dot_f32(part, part, ROW_DIMS)
        total = term if total is None else total + term
    refs[-1][...] = total


def moment_of(parts):
    rank = 2 * parts[0].shape[2]
    return pl.pallas_call(
        moment_kernel,
        out_shape=jax.ShapeDtypeStruct((rank, rank), jnp.float32),
        compiler_params=GRANT,
        cost_estimate=pl.CostEstimate(flops=4_000_000_000, bytes_accessed=2359296, transcendentals=0),
        name="moment_of",
    )(*parts)


def whiten_kernel(spot_ref, inverse_ref, moment_ref, other_ref, *refs):
    parts, out_ref = refs[:-1], refs[-1]
    inverse = inverse_ref[...]
    rank = inverse.shape[0]
    moment = moment_ref[...] + other_ref[...]
    cov_total = dot_f32(dot_f32(inverse, moment), inverse, (((1,), (1,)), ((), ())))
    row_ids = lax.broadcasted_iota(jnp.int32, (rank, rank), 0)
    col_ids = lax.broadcasted_iota(jnp.int32, (rank, rank), 1)
    eye_matrix = (row_ids == col_ids).astype(jnp.float32)
    trace_value = jnp.sum(cov_total * eye_matrix, axis=(0, 1), keepdims=True)
    left_iter = cov_total / trace_value
    right_iter = 1.5 * eye_matrix - 0.5 * left_iter
    right_parts = split_two(right_iter)
    left_parts = split_two(dot_split(split_two(left_iter), right_parts))
    for step_index in range(1, NS_STEPS):
        middle = split_two(1.5 * eye_matrix - 0.5 * dot_split(right_parts, left_parts))
        right_iter = dot_split(middle, right_parts)
        if step_index < NS_STEPS - 1:
            left_parts = split_two(dot_split(left_parts, middle))
            right_parts = split_two(right_iter)
    factor = right_iter / jnp.sqrt(trace_value)
    weight = split_two(dot_f32(inverse, factor, ROW_DIMS))
    height = out_ref.shape[0] // len(parts)
    for step, part_ref in enumerate(parts):
        place = lax.rem(spot_ref[0] + len(parts) - step, len(parts))
        rows = pl.ds(pl.multiple_of(place * height, height), height)
        out_ref[rows, :] = dot_split(split_two(plain_rows(part_ref)), weight).astype(jnp.bfloat16)


def project_half(spot, inverse, moment, other, parts):
    chunk, rank = parts[0].shape[0] * (parts[0].shape[1] - 8) // 2, inverse.shape[0]
    return pl.pallas_call(
        whiten_kernel,
        in_specs=[pl.BlockSpec(memory_space=pltpu.SMEM)]
        + [pl.BlockSpec(memory_space=pltpu.VMEM)] * (3 + len(parts)),
        out_shape=jax.ShapeDtypeStruct((chunk * len(parts), rank), jnp.bfloat16),
        compiler_params=GRANT,
        cost_estimate=pl.CostEstimate(flops=12_000_000_000, bytes_accessed=4194304, transcendentals=0),
        name="project_half",
    )(spot, inverse, moment, other, *parts)


def chunk_kernel(steps, spot_ref, rows_ref, sketch_ref, label_ref, *out_refs):
    core, here, line = (spot_ref[i] for i in range(3))
    rank = sketch_ref.shape[1]
    width = out_refs[0].shape[1] - 128
    half = rows_ref.shape[1] // 2
    sketch = sketch_ref[...]
    mul = functools.partial(
        lax.dot_general, dimension_numbers=ROW_DIMS, preferred_element_type=jnp.float32
    )
    gram_whole = mul(sketch, sketch)
    lane = lax.broadcasted_iota(jnp.int32, (rank, 128), 1)
    mine = pl.ds(pl.multiple_of((core * line + here) * SLOTS, SLOTS), SLOTS)
    for index, step in enumerate(steps):
        chunk = lax.rem(here + step, line)
        gram = pltpu.roll(gram_whole, rank - chunk * (rank * width // half), 1)[:, :128]
        gram = jnp.where(lane < rank * width // half, gram, 0.0)
        for out_ref, place in zip(out_refs[2 * index :], (1 - core, core)):
            columns = pl.ds(pl.multiple_of(place * half + chunk * width, width), width)
            out_ref[:, :width] = mul(sketch, rows_ref[:, columns])
            out_ref[:, width:] = gram
            theirs = pl.ds(pl.multiple_of((place * line + chunk) * SLOTS, SLOTS), SLOTS)
            out_ref[mine, width:] += label_ref[theirs, :]


def cross_chunks(spot, embeddings, sketch, labels, chunks, steps):
    count = len(steps)
    depth, dim = embeddings.shape
    rank = sketch.shape[1]
    width = dim // 2 // chunks
    shape = jax.ShapeDtypeStruct((rank, width + 128), jnp.float32)
    return pl.pallas_call(
        functools.partial(chunk_kernel, steps),
        in_specs=[pl.BlockSpec(memory_space=pltpu.SMEM)]
        + [pl.BlockSpec(memory_space=pltpu.VMEM)] * 3,
        out_shape=[shape] * (2 * count),
        compiler_params=GRANT,
        cost_estimate=pl.CostEstimate(
            flops=4 * depth * rank * width * count, bytes_accessed=3000000, transcendentals=0
        ),
        name="cross_chunks",
    )(spot, embeddings, sketch, labels)


def join_kernel(side, keep_ref, got_ref, extra_ref, body_ref, tail_ref):
    rank, width = body_ref.shape
    total = keep_ref[...] + got_ref[...]
    extra = jnp.concatenate(
        [extra_ref[...], jnp.zeros_like(extra_ref)][:: 1 - 2 * side], axis=0
    )
    total = total + extra
    body, power = scaled(total[:, :width])
    body_ref[...] = body
    tail = total[:, width:]
    row = lax.broadcasted_iota(jnp.int32, tail.shape, 0)
    lane = lax.broadcasted_iota(jnp.int32, tail.shape, 1)
    tail_ref[...] = jnp.where((row == rank - 1) & (lane >= 64), power, tail)


def join_chunk(keep, got, extra, side):
    rank, width = keep.shape
    body, tail = pl.pallas_call(
        functools.partial(join_kernel, side),
        out_shape=[
            jax.ShapeDtypeStruct((rank, width - 128), jnp.float32),
            jax.ShapeDtypeStruct((rank, 128), jnp.float32),
        ],
        compiler_params=GRANT,
        cost_estimate=pl.CostEstimate(flops=400000, bytes_accessed=2000000, transcendentals=0),
        name="join_chunk",
    )(keep, got, extra)
    return body.astype(jnp.float16), tail


def line_kernel(gram_piece, *refs):
    first, second, out_ref = refs[0], refs[1], refs[-1]
    plane = out_ref.shape[0]
    total = first[...] + second[...]
    rank, width = total.shape[0], total.shape[1] - 128
    body, tail = total[:, :width], total[:, width:]
    for body_ref, tail_ref in zip(refs[2:-1:2], refs[3:-1:2]):
        more = tail_ref[...]
        body = body + body_ref[...] * unscale_factor(more[rank - 1 :, 127:])
        tail = tail + more
    piece = width // plane
    turned = body.T.reshape(plane, piece, rank)
    out_ref[:, :piece, :] = turned[:, :, :128]
    out_ref[:, piece : 2 * piece, :] = turned[:, :, 128:]
    tail = tail.T.reshape(2, plane, gram_piece, rank)
    gram, labels = tail[0], tail[1][:, :1, :128]
    fill = jnp.zeros((plane, out_ref.shape[1] - 2 * (piece + gram_piece) - 1, 128), jnp.float32)
    out_ref[:, 2 * piece :, :] = jnp.concatenate(
        [gram[:, :, :128], gram[:, :, 128:], labels, fill], axis=1
    )


def line_total(parts, plane, gram_piece):
    width = parts[0].shape[1] - 128
    rows = 2 * (width // plane + gram_piece) + 1
    rows += -rows % 8
    return pl.pallas_call(
        functools.partial(line_kernel, gram_piece),
        out_shape=jax.ShapeDtypeStruct((plane, rows, 128), jnp.float32),
        compiler_params=GRANT,
        cost_estimate=pl.CostEstimate(flops=1000000, bytes_accessed=4000000, transcendentals=0),
        name="line_total",
    )(*parts)


def plane_kernel(piece, gram_piece, parts_ref, out_ref, label_ref):
    cut, end = 2 * piece, 2 * (piece + gram_piece)
    total = jnp.sum(parts_ref[:, :end, :], axis=0)
    rows, power = scaled(total[:cut])
    gram, gram_power = scaled(total[cut:])
    lanes = total.shape[1]
    pieces = [rows, jnp.broadcast_to(power, (1, lanes))]
    for term in range(3):
        short = gram.astype(jnp.bfloat16).astype(jnp.float32)
        pieces.append(short)
        gram = gram - short
    pieces.append(jnp.broadcast_to(gram_power, (1, lanes)))
    filled = sum(p.shape[0] for p in pieces)
    pieces.append(jnp.zeros((out_ref.shape[0] - filled, lanes), jnp.float32))
    out_ref[...] = jnp.concatenate(pieces, axis=0)
    label_ref[...] = parts_ref[:, end, :].astype(jnp.int32) - 1


def plane_total(parts, piece, gram_piece):
    plane, _, lanes = parts.shape
    rows = 2 * piece + 6 * gram_piece + 2
    rows += -rows % 16
    return pl.pallas_call(
        functools.partial(plane_kernel, piece, gram_piece),
        out_shape=[
            jax.ShapeDtypeStruct((rows, lanes), jnp.float32),
            jax.ShapeDtypeStruct((plane, lanes), jnp.int32),
        ],
        compiler_params=GRANT,
        cost_estimate=pl.CostEstimate(flops=1000000, bytes_accessed=1600000, transcendentals=0),
        name="plane_total",
    )(parts)


def plain_rows(part_ref):
    part = part_ref[...]
    cut = part.shape[1] - 8
    return whole_rows(part[:, :cut] * unscale_factor(part[:, cut : cut + 1]))


def whole_rows(part):
    plane, pair, lanes = part.shape
    sides = [part[:, : pair // 2], part[:, pair // 2 :]]
    return jnp.concatenate([t.reshape(plane * pair // 2, lanes) for t in sides], axis=1)


def gram_kernel(parts_ref, out_ref):
    pair = 2 * out_ref.shape[0] // parts_ref.shape[0]
    terms = [parts_ref[:, 1 + t * pair : 1 + (t + 1) * pair, :] for t in range(3)]
    power = parts_ref[:, 1 + 3 * pair : 2 + 3 * pair, :]
    out_ref[...] = whole_rows((terms[0] + (terms[1] + terms[2])) * unscale_factor(power))


def gram_rows(parts, gram_piece):
    plane, _, lanes = parts.shape
    return pl.pallas_call(
        gram_kernel,
        out_shape=jax.ShapeDtypeStruct((plane * gram_piece, 2 * lanes), jnp.float32),
        compiler_params=GRANT,
        cost_estimate=pl.CostEstimate(flops=10000, bytes_accessed=200000, transcendentals=0),
        name="gram_rows",
    )(parts)


def product_kernel(core_ref, rows_ref, basis_ref, *refs):
    half, width = basis_ref.shape[0], 512
    total = None if len(refs) == 1 else refs[0][...]
    for step in range(half // width):
        columns = pl.ds(pl.multiple_of(core_ref[0] * half + step * width, width), width)
        basis = basis_ref[step * width : (step + 1) * width, :]
        term = jnp.dot(rows_ref[:, columns], basis, preferred_element_type=jnp.float32)
        total = term if total is None else total + term
    refs[-1][...] = total.astype(refs[-1].dtype)


def product_of_half(half, embeddings, basis, begin, out_type):
    depth, dim = embeddings.shape
    rank = basis.shape[1]
    extra = [] if begin is None else [begin]
    return pl.pallas_call(
        product_kernel,
        in_specs=[pl.BlockSpec(memory_space=pltpu.SMEM)]
        + [pl.BlockSpec(memory_space=pltpu.VMEM)] * (2 + len(extra)),
        out_shape=jax.ShapeDtypeStruct((depth, rank), out_type),
        compiler_params=GRANT,
        cost_estimate=pl.CostEstimate(
            flops=depth * dim * rank, bytes_accessed=depth * dim + dim * rank, transcendentals=0
        ),
        name="product_of_half",
    )(half, embeddings, basis, *extra)


def route_kernel(capacity, line, plane, ids_ref, map_ref, dest_ref, label_ref):
    ids = jnp.concatenate([ids_ref[k : k + 1, :] for k in range(ids_ref.shape[0])], axis=1)
    count, (high, low) = ids.shape[1], map_ref.shape
    owner_count = 2 * plane * line
    bf16 = jnp.bfloat16

    def rows_of(size):
        return lax.broadcasted_iota(jnp.int32, (size, count), 0)

    picked = (rows_of(high) == ids // low).astype(bf16)
    found = lax.dot_general(
        map_ref[...].astype(bf16), picked, ROW_DIMS, preferred_element_type=jnp.float32
    )
    owner = jnp.sum(jnp.where(rows_of(low) == ids % low, found, 0.0), axis=0, keepdims=True)
    owner = owner.astype(jnp.int32)
    mine = rows_of(owner_count) == owner
    order = lax.broadcasted_iota(jnp.int32, (count, count), 1)
    earlier = (lax.broadcasted_iota(jnp.int32, (count, count), 0) < order).astype(bf16)
    before = jnp.dot(mine.astype(bf16), earlier, preferred_element_type=jnp.float32)
    slot = jnp.sum(jnp.where(mine, before, 0.0), axis=0, keepdims=True).astype(jnp.int32)
    dest_ref[...] = owner * capacity + slot
    value = ids + 1
    core, chip = owner // (plane * line), owner % (plane * line)
    row = (core * line + chip % line) * SLOTS + slot
    lane = rows_of(128) == 64 + 2 * (chip // line)
    lane = lane.astype(bf16)
    labels = None
    for digit in range(3):
        short = (value // 128**digit) % 128
        spread = jnp.where(rows_of(2 * line * SLOTS) == row, short.astype(jnp.float32), 0.0)
        term = lax.dot_general(
            spread.astype(bf16),
            lane,
            (((1,), (1,)), ((), ())),
            preferred_element_type=jnp.float32,
        )
        labels = term if labels is None else labels + term * 128**digit
    label_ref[...] = labels


def route_rows(list_ids, owner_map, capacity, line, plane):
    count = list_ids.shape[0]
    return pl.pallas_call(
        functools.partial(route_kernel, capacity, line, plane),
        out_shape=[
            jax.ShapeDtypeStruct((1, count), jnp.int32),
            jax.ShapeDtypeStruct((2 * line * SLOTS, 128), jnp.float32),
        ],
        compiler_params=GRANT,
        cost_estimate=pl.CostEstimate(
            flops=2_000_000_000, bytes_accessed=1048576, transcendentals=0
        ),
        name="route_rows",
    )(list_ids.reshape(-1, 128), owner_map.reshape(-1, 128))


def place_kernel(capacity, first_target, second_target, first_ref, second_ref, out_ref):
    pairs, _, width = out_ref.shape
    count = pairs * 2 * capacity
    slots = pl.program_id(0) * count + lax.broadcasted_iota(
        jnp.int32, (count, first_ref.shape[0]), 0
    )
    found = []
    for target_ref, rows_ref in ((first_target, first_ref), (second_target, second_ref)):
        onehot = (slots == target_ref[...]).astype(jnp.bfloat16)
        term = jnp.dot(onehot, rows_ref[...], preferred_element_type=jnp.float32)
        found.append(term.reshape(pairs, 2 * capacity, width))
    a, b = found
    out_ref[...] = jnp.concatenate(
        [a[:, :capacity], b[:, :capacity], a[:, capacity:], b[:, capacity:]], axis=1
    ).astype(jnp.bfloat16)


def place_rows(targets, first, second, chips, capacity):
    pairs = 16
    depth, width = first.shape
    return pl.pallas_call(
        functools.partial(place_kernel, capacity),
        grid=(chips // 2 // pairs,),
        in_specs=[pl.BlockSpec((1, depth), lambda i: (0, 0))] * 2
        + [pl.BlockSpec((depth, width), lambda i: (0, 0))] * 2,
        out_specs=pl.BlockSpec((pairs, 4 * capacity, width), lambda i: (i, 0, 0)),
        out_shape=jax.ShapeDtypeStruct((chips // 2, 4 * capacity, width), jnp.bfloat16),
        compiler_params=GRANT,
        cost_estimate=pl.CostEstimate(
            flops=4 * chips * capacity * depth * width,
            bytes_accessed=8 * chips * capacity * width,
            transcendentals=0,
        ),
        name="place_rows",
    )(*targets, first, second)


def shift(value, axis, step):
    size = lax.axis_size(axis)
    return lax.ppermute(value, axis, [(i, (i + step) % size) for i in range(size)])


def local(embeddings, sketch_seed, list_ids, owner_map):
    row_count, dim = embeddings.shape
    rank = sketch_seed.shape[1]
    cores, line = lax.axis_size("narrow"), lax.axis_size("x")
    plane = lax.axis_size("y") * lax.axis_size("z")
    chips = plane * line
    dev_count = cores * chips
    core = lax.axis_index("narrow")
    spot = lax.axis_index("x").reshape(1)
    own_half, other_half = core.reshape(1), (1 - core).reshape(1)
    piece, gram_piece = dim // dev_count, rank // chips
    seed_matrix = sketch_seed.astype(jnp.bfloat16)
    sketch = jnp.dot(embeddings, seed_matrix, preferred_element_type=jnp.float32).astype(
        jnp.bfloat16
    )

    capacity = 4 * row_count // dev_count
    here = lax.axis_index("x")
    dest_index, labels = route_rows(list_ids, owner_map, capacity, line, plane)

    spots = jnp.stack([core, here, jnp.int32(line)])

    def chunks_at(*steps):
        pairs = cross_chunks(spots, embeddings, sketch, labels, line, steps)
        return [(pairs[2 * i + 1], shift(pairs[2 * i], "narrow", 1)) for i in range(len(steps))]

    (far,) = chunks_at(2)
    up, down, near = chunks_at(1, 3, 0)
    far = far[0] + far[1]
    from_below = shift(far[: rank // 2], "x", 1)
    from_above = shift(far[rank // 2 :], "x", line - 1)
    from_below = [shift(part, "x", 1) for part in join_chunk(*up, from_below, 0)]
    from_above = [shift(part, "x", line - 1) for part in join_chunk(*down, from_above, 1)]
    arrived = [part.astype(jnp.float32) for part in from_below + from_above]

    def target_of(dest):
        owner = dest // capacity
        return jnp.where(owner // chips == core, (owner % chips) * capacity + dest % capacity, -1)

    def by_core(own, other):
        return jnp.where(core == 0, own, other), jnp.where(core == 0, other, own)

    targets = by_core(target_of(dest_index), target_of(shift(dest_index, "narrow", 1)))

    packed = line_total([*near, *arrived], plane, gram_piece)
    packed, targets = lax.optimization_barrier((packed, targets))
    packed = lax.all_to_all(packed, PLANE, 0, 0, tiled=True)
    packed, arrived_labels = plane_total(packed, piece, gram_piece)
    packed = jnp.broadcast_to(packed.astype(jnp.float16)[None], (plane,) + packed.shape)
    packed = lax.all_to_all(packed, PLANE, 0, 0, tiled=True)
    gram_line = gram_rows(packed[:, 2 * piece :].astype(jnp.float32), gram_piece)
    gram_parts = [gram_line] + [shift(gram_line, "x", step) for step in range(1, line)]
    packed, gram_parts[1] = lax.optimization_barrier((packed, gram_parts[1]))
    cross_line = packed[:, : 2 * piece + 8]
    cross_parts = [cross_line] + [shift(cross_line, "x", step) for step in range(1, line)]
    cross_parts = [part.astype(jnp.float32) for part in cross_parts]
    arrived_labels = arrived_labels[:, : cores * line * SLOTS].reshape(plane, cores, line, SLOTS)
    arrived_labels = arrived_labels[..., :capacity].transpose(1, 0, 2, 3)

    inverse = invert_factor(spot, gram_parts)
    inverse, cross_parts = lax.optimization_barrier((inverse, cross_parts))
    moment = moment_of(cross_parts)
    basis = project_half(spot, inverse, moment, shift(moment, "narrow", 1), cross_parts)
    other_basis = shift(basis, "narrow", 1)
    begun = product_of_half(own_half, embeddings, basis, None, jnp.float32)
    reduced = product_of_half(other_half, embeddings, other_basis, begun, jnp.bfloat16)
    rows = by_core(reduced, shift(reduced, "narrow", 1))
    send_rows = place_rows(targets, *rows, chips, capacity)
    send_rows = send_rows.reshape(chips, cores * capacity, rank)
    arrived = lax.all_to_all(send_rows, ("y", "z", "x"), 0, 0, tiled=True)
    arrived = arrived.reshape(chips, cores, capacity, rank).transpose(1, 0, 2, 3)
    return (
        arrived.reshape(1, dev_count, capacity, rank),
        arrived_labels.reshape(1, dev_count, capacity),
    )


def solution(mesh):
    grid = Mesh(mesh.devices.reshape(2, 4, 8, 4), ALL)
    in_specs = (P(ALL, None), P(), P(ALL), P())
    out_specs = (P(ALL, None, None, None), P(ALL, None, None))
    return jax.shard_map(local, mesh=grid, in_specs=in_specs, out_specs=out_specs, check_vma=False)
```

```python
import functools

import jax
import jax.numpy as jnp
from jax import lax
from jax.experimental import pallas as pl
from jax.experimental.pallas import tpu as pltpu
from jax.sharding import Mesh
from jax.sharding import PartitionSpec as P

NS_STEPS = 6
BLOCK = 64
TILE = 16
ALL = ("narrow", "y", "z", "x")
PLANE = ("y", "z")
HIGHEST = lax.Precision.HIGHEST
ROW_DIMS = (((0,), (0,)), ((), ()))
SLOTS = 16
GRANT = pltpu.CompilerParams(vmem_limit_bytes=16 * 2**20)


def dot_f32(a, b, dims=(((1,), (0,)), ((), ()))):
    return lax.dot_general(a, b, dims, precision=HIGHEST, preferred_element_type=jnp.float32)


def split_two(a):
    high = a.astype(jnp.bfloat16)
    return high, (a - high.astype(jnp.float32)).astype(jnp.bfloat16)


def dot_split(a, b):
    (ah, al), (bh, bl) = a, b
    mul = functools.partial(jnp.dot, preferred_element_type=jnp.float32)
    return mul(ah, bh) + (mul(ah, bl) + mul(al, bh))


POWERS = (64, 32, 16, 8, 4)


def scaled(value):
    top = jnp.max(jnp.abs(value), axis=(0, 1), keepdims=True)
    factor, power = jnp.ones_like(top), jnp.zeros_like(top)
    for p in POWERS:
        large = top * factor >= 2.0 ** (11 + p)
        factor = jnp.where(large, factor * 2.0**-p, factor)
        power = jnp.where(large, power - p, power)
    for p in POWERS:
        small = top * factor < 2.0 ** (15 - p)
        factor = jnp.where(small, factor * 2.0**p, factor)
        power = jnp.where(small, power + p, power)
    return value * factor, power


def unscale_factor(power):
    factor = jnp.ones_like(power)
    for p in POWERS:
        up, down = power >= p, power <= -p
        factor = jnp.where(up, factor * 2.0**-p, jnp.where(down, factor * 2.0**p, factor))
        power = jnp.where(up, power - p, jnp.where(down, power + p, power))
    return factor


def spread_rows(rows, gram, extra, count):
    def leaf(value):
        flat, power = scaled(value.reshape(-1, value.shape[2]))
        shape = (value.shape[0], 1, value.shape[2])
        return flat.reshape(value.shape), jnp.broadcast_to(power[None], shape)

    pieces = list(leaf(rows))
    gram, gram_power = leaf(gram)
    for term in range(3):
        short = gram.astype(jnp.bfloat16).astype(jnp.float32)
        pieces.append(short)
        gram = gram - short
    pieces += [gram_power] + extra
    filled = sum(p.shape[1] for p in pieces)
    if filled < count:
        shape = (rows.shape[0], count - filled, rows.shape[2])
        pieces.append(jnp.zeros(shape, jnp.float32))
    return jnp.concatenate(pieces, axis=1)


def joined_gram(parts, start, pair):
    terms = [parts[:, start + t * pair : start + (t + 1) * pair, :] for t in range(3)]
    power = parts[:, start + 3 * pair : start + 3 * pair + 1, :]
    return (terms[0] + (terms[1] + terms[2])) * unscale_factor(power)


def invert_kernel(spot_ref, *refs):
    parts, inverse_ref, work_ref = refs[:-2], refs[-2], refs[-1]
    rank = inverse_ref.shape[0]
    height = rank // len(parts)
    row_ids = lax.broadcasted_iota(jnp.int32, (rank, rank), 0)
    col_ids = lax.broadcasted_iota(jnp.int32, (rank, rank), 1)
    for step, part_ref in enumerate(parts):
        place = lax.rem(spot_ref[0] + len(parts) - step, len(parts))
        work_ref[pl.ds(pl.multiple_of(place * height, height), height), :rank] = part_ref[...]
    work_ref[:, rank:] = (row_ids == col_ids).astype(jnp.float32)
    lane = lax.broadcasted_iota(jnp.int32, (BLOCK, 128), 1)
    row = lax.broadcasted_iota(jnp.int32, (BLOCK, 128), 0)
    panel_lane = lax.broadcasted_iota(jnp.int32, (BLOCK, rank), 1)

    def block_step(step, carry):
        start = pl.multiple_of(step * BLOCK, BLOCK)
        panel = work_ref[pl.ds(start, BLOCK), :]
        shifted = pltpu.roll(panel[:, :rank], rank - start, 1)[:, :128]
        rest = jnp.where(lane < BLOCK, shifted, (lane - BLOCK == row).astype(jnp.float32))
        done = []
        for tile in range(BLOCK // TILE):
            height = BLOCK - tile * TILE
            sub = lax.broadcasted_iota(jnp.int32, (height, 128), 0)
            columns = [
                jnp.broadcast_to(rest[:, tile * TILE + j : tile * TILE + j + 1], (height, 128))
                for j in range(TILE)
            ]
            for j in range(TILE):
                pivot = columns[j][j : j + 1, :]
                scale = lax.rsqrt(pivot)
                scale = scale * (1.5 - 0.5 * (pivot * scale) * scale)
                below = jnp.where(sub > j, columns[j] * scale, 0.0)
                lead = rest[j : j + 1, :] * scale
                done.append(lead)
                rest = rest - below * lead
                for m in range(j + 1, TILE):
                    columns[m] = columns[m] - below * (columns[m][j : j + 1, :] * scale)
            rest = rest[TILE:, :]
        solved = jnp.concatenate(done, axis=0)
        small = pltpu.roll(solved, 128 - BLOCK, 1)[:, :BLOCK]
        panel = dot_f32(small, panel)
        inverse_ref[pl.ds(start, BLOCK), :] = panel[:, rank:]
        later = jnp.where(panel_lane >= start + BLOCK, panel[:, :rank], 0.0)
        work_ref[...] -= dot_f32(later, panel, (((0,), (0,)), ((), ())))
        return carry

    lax.fori_loop(0, rank // BLOCK, block_step, 0)


def invert_factor(spot, parts):
    rank = parts[0].shape[1]
    return pl.pallas_call(
        invert_kernel,
        in_specs=[pl.BlockSpec(memory_space=pltpu.SMEM)]
        + [pl.BlockSpec(memory_space=pltpu.VMEM)] * len(parts),
        out_shape=jax.ShapeDtypeStruct((rank, rank), jnp.float32),
        scratch_shapes=[pltpu.VMEM((rank, 2 * rank), jnp.float32)],
        compiler_params=GRANT,
        cost_estimate=pl.CostEstimate(flops=20_000_000_000, bytes_accessed=524288, transcendentals=0),
        name="invert_factor",
    )(spot, *parts)


def moment_kernel(*refs):
    total = None
    for part_ref in refs[:-1]:
        part = plain_rows(part_ref)
        term = dot_f32(part, part, ROW_DIMS)
        total = term if total is None else total + term
    refs[-1][...] = total


def moment_of(parts):
    rank = 2 * parts[0].shape[2]
    return pl.pallas_call(
        moment_kernel,
        out_shape=jax.ShapeDtypeStruct((rank, rank), jnp.float32),
        compiler_params=GRANT,
        cost_estimate=pl.CostEstimate(flops=4_000_000_000, bytes_accessed=2359296, transcendentals=0),
        name="moment_of",
    )(*parts)


def whiten_kernel(spot_ref, inverse_ref, moment_ref, other_ref, *refs):
    parts, out_ref = refs[:-1], refs[-1]
    inverse = inverse_ref[...]
    rank = inverse.shape[0]
    moment = moment_ref[...] + other_ref[...]
    cov_total = dot_f32(dot_f32(inverse, moment), inverse, (((1,), (1,)), ((), ())))
    row_ids = lax.broadcasted_iota(jnp.int32, (rank, rank), 0)
    col_ids = lax.broadcasted_iota(jnp.int32, (rank, rank), 1)
    eye_matrix = (row_ids == col_ids).astype(jnp.float32)
    trace_value = jnp.sum(cov_total * eye_matrix, axis=(0, 1), keepdims=True)
    left_iter = cov_total / trace_value
    right_iter = 1.5 * eye_matrix - 0.5 * left_iter
    right_parts = split_two(right_iter)
    left_parts = split_two(dot_split(split_two(left_iter), right_parts))
    for step_index in range(1, NS_STEPS):
        middle = split_two(1.5 * eye_matrix - 0.5 * dot_split(right_parts, left_parts))
        right_iter = dot_split(middle, right_parts)
        if step_index < NS_STEPS - 1:
            left_parts = split_two(dot_split(left_parts, middle))
            right_parts = split_two(right_iter)
    factor = right_iter / jnp.sqrt(trace_value)
    weight = split_two(dot_f32(inverse, factor, ROW_DIMS))
    height = out_ref.shape[0] // len(parts)
    for step, part_ref in enumerate(parts):
        place = lax.rem(spot_ref[0] + len(parts) - step, len(parts))
        rows = pl.ds(pl.multiple_of(place * height, height), height)
        out_ref[rows, :] = dot_split(split_two(plain_rows(part_ref)), weight).astype(jnp.bfloat16)


def project_half(spot, inverse, moment, other, parts):
    chunk, rank = parts[0].shape[0] * (parts[0].shape[1] - 8) // 2, inverse.shape[0]
    return pl.pallas_call(
        whiten_kernel,
        in_specs=[pl.BlockSpec(memory_space=pltpu.SMEM)]
        + [pl.BlockSpec(memory_space=pltpu.VMEM)] * (3 + len(parts)),
        out_shape=jax.ShapeDtypeStruct((chunk * len(parts), rank), jnp.bfloat16),
        compiler_params=GRANT,
        cost_estimate=pl.CostEstimate(flops=12_000_000_000, bytes_accessed=4194304, transcendentals=0),
        name="project_half",
    )(spot, inverse, moment, other, *parts)


def chunk_kernel(steps, spot_ref, rows_ref, sketch_ref, label_ref, *out_refs):
    core, here, line = (spot_ref[i] for i in range(3))
    rank = sketch_ref.shape[1]
    width = out_refs[0].shape[1] - 128
    half = rows_ref.shape[1] // 2
    sketch = sketch_ref[...]
    mul = functools.partial(
        lax.dot_general, dimension_numbers=ROW_DIMS, preferred_element_type=jnp.float32
    )
    gram_whole = mul(sketch, sketch)
    lane = lax.broadcasted_iota(jnp.int32, (rank, 128), 1)
    mine = pl.ds(pl.multiple_of((core * line + here) * SLOTS, SLOTS), SLOTS)
    for index, step in enumerate(steps):
        chunk = lax.rem(here + step, line)
        gram = pltpu.roll(gram_whole, rank - chunk * (rank * width // half), 1)[:, :128]
        gram = jnp.where(lane < rank * width // half, gram, 0.0)
        for out_ref, place in zip(out_refs[2 * index :], (1 - core, core)):
            columns = pl.ds(pl.multiple_of(place * half + chunk * width, width), width)
            out_ref[:, :width] = mul(sketch, rows_ref[:, columns])
            out_ref[:, width:] = gram
            theirs = pl.ds(pl.multiple_of((place * line + chunk) * SLOTS, SLOTS), SLOTS)
            out_ref[mine, width:] += label_ref[theirs, :]


def cross_chunks(spot, embeddings, sketch, labels, chunks, steps):
    count = len(steps)
    depth, dim = embeddings.shape
    rank = sketch.shape[1]
    width = dim // 2 // chunks
    shape = jax.ShapeDtypeStruct((rank, width + 128), jnp.float32)
    return pl.pallas_call(
        functools.partial(chunk_kernel, steps),
        in_specs=[pl.BlockSpec(memory_space=pltpu.SMEM)]
        + [pl.BlockSpec(memory_space=pltpu.VMEM)] * 3,
        out_shape=[shape] * (2 * count),
        compiler_params=GRANT,
        cost_estimate=pl.CostEstimate(
            flops=4 * depth * rank * width * count, bytes_accessed=3000000, transcendentals=0
        ),
        name="cross_chunks",
    )(spot, embeddings, sketch, labels)


def join_kernel(side, keep_ref, got_ref, extra_ref, body_ref, tail_ref):
    rank, width = body_ref.shape
    total = keep_ref[...] + got_ref[...]
    extra = jnp.concatenate(
        [extra_ref[...], jnp.zeros_like(extra_ref)][:: 1 - 2 * side], axis=0
    )
    total = total + extra
    body, power = scaled(total[:, :width])
    body_ref[...] = body
    tail = total[:, width:]
    row = lax.broadcasted_iota(jnp.int32, tail.shape, 0)
    lane = lax.broadcasted_iota(jnp.int32, tail.shape, 1)
    tail_ref[...] = jnp.where((row == rank - 1) & (lane >= 64), power, tail)


def join_chunk(keep, got, extra, side):
    rank, width = keep.shape
    body, tail = pl.pallas_call(
        functools.partial(join_kernel, side),
        out_shape=[
            jax.ShapeDtypeStruct((rank, width - 128), jnp.float32),
            jax.ShapeDtypeStruct((rank, 128), jnp.float32),
        ],
        compiler_params=GRANT,
        cost_estimate=pl.CostEstimate(flops=400000, bytes_accessed=2000000, transcendentals=0),
        name="join_chunk",
    )(keep, got, extra)
    return body.astype(jnp.float16), tail


def line_kernel(gram_piece, *refs):
    first, second, out_ref = refs[0], refs[1], refs[-1]
    plane = out_ref.shape[0]
    total = first[...] + second[...]
    rank, width = total.shape[0], total.shape[1] - 128
    body, tail = total[:, :width], total[:, width:]
    for body_ref, tail_ref in zip(refs[2:-1:2], refs[3:-1:2]):
        more = tail_ref[...]
        body = body + body_ref[...] * unscale_factor(more[rank - 1 :, 127:])
        tail = tail + more
    piece = width // plane
    turned = body.T.reshape(plane, piece, rank)
    tail = tail.T.reshape(2, plane, gram_piece, rank)
    gram, labels = tail[0], tail[1][:, :1, :128].astype(jnp.int32)
    digits = [(labels % 1024).astype(jnp.float32), (labels // 1024).astype(jnp.float32)]
    out_ref[...] = spread_rows(
        jnp.concatenate([turned[:, :, :128], turned[:, :, 128:]], axis=1),
        jnp.concatenate([gram[:, :, :128], gram[:, :, 128:]], axis=1),
        digits,
        out_ref.shape[1],
    )


def line_total(parts, plane, gram_piece):
    width = parts[0].shape[1] - 128
    rows = 2 * (width // plane) + 6 * gram_piece + 4
    rows += -rows % 16
    return pl.pallas_call(
        functools.partial(line_kernel, gram_piece),
        out_shape=jax.ShapeDtypeStruct((plane, rows, 128), jnp.float32),
        compiler_params=GRANT,
        cost_estimate=pl.CostEstimate(flops=1000000, bytes_accessed=4000000, transcendentals=0),
        name="line_total",
    )(*parts)


def plane_kernel(piece, gram_piece, parts_ref, out_ref, label_ref):
    cut, pair = 2 * piece, 2 * gram_piece
    parts = parts_ref[...]
    rows = jnp.sum(parts[:, :cut, :] * unscale_factor(parts[:, cut : cut + 1, :]), axis=0)
    gram = jnp.sum(joined_gram(parts, cut + 1, pair), axis=0)
    out_ref[...] = spread_rows(rows[None], gram[None], [], out_ref.shape[0])[0]
    end = cut + 2 + 3 * pair
    labels = parts[:, end, :] + 1024.0 * parts[:, end + 1, :]
    label_ref[...] = labels.astype(jnp.int32) - 1


def plane_total(parts, piece, gram_piece):
    plane, _, lanes = parts.shape
    rows = 2 * piece + 6 * gram_piece + 2
    rows += -rows % 16
    return pl.pallas_call(
        functools.partial(plane_kernel, piece, gram_piece),
        out_shape=[
            jax.ShapeDtypeStruct((rows, lanes), jnp.float32),
            jax.ShapeDtypeStruct((plane, lanes), jnp.int32),
        ],
        compiler_params=GRANT,
        cost_estimate=pl.CostEstimate(flops=1000000, bytes_accessed=1600000, transcendentals=0),
        name="plane_total",
    )(parts)


def plain_rows(part_ref):
    part = part_ref[...]
    cut = part.shape[1] - 8
    return whole_rows(part[:, :cut] * unscale_factor(part[:, cut : cut + 1]))


def whole_rows(part):
    plane, pair, lanes = part.shape
    sides = [part[:, : pair // 2], part[:, pair // 2 :]]
    return jnp.concatenate([t.reshape(plane * pair // 2, lanes) for t in sides], axis=1)


def gram_kernel(parts_ref, out_ref):
    pair = 2 * out_ref.shape[0] // parts_ref.shape[0]
    out_ref[...] = whole_rows(joined_gram(parts_ref[...], 1, pair))


def gram_rows(parts, gram_piece):
    plane, _, lanes = parts.shape
    return pl.pallas_call(
        gram_kernel,
        out_shape=jax.ShapeDtypeStruct((plane * gram_piece, 2 * lanes), jnp.float32),
        compiler_params=GRANT,
        cost_estimate=pl.CostEstimate(flops=10000, bytes_accessed=200000, transcendentals=0),
        name="gram_rows",
    )(parts)


def product_kernel(core_ref, rows_ref, basis_ref, *refs):
    half, width = basis_ref.shape[0], 512
    total = None if len(refs) == 1 else refs[0][...]
    for step in range(half // width):
        columns = pl.ds(pl.multiple_of(core_ref[0] * half + step * width, width), width)
        basis = basis_ref[step * width : (step + 1) * width, :]
        term = jnp.dot(rows_ref[:, columns], basis, preferred_element_type=jnp.float32)
        total = term if total is None else total + term
    refs[-1][...] = total.astype(refs[-1].dtype)


def product_of_half(half, embeddings, basis, begin, out_type):
    depth, dim = embeddings.shape
    rank = basis.shape[1]
    extra = [] if begin is None else [begin]
    return pl.pallas_call(
        product_kernel,
        in_specs=[pl.BlockSpec(memory_space=pltpu.SMEM)]
        + [pl.BlockSpec(memory_space=pltpu.VMEM)] * (2 + len(extra)),
        out_shape=jax.ShapeDtypeStruct((depth, rank), out_type),
        compiler_params=GRANT,
        cost_estimate=pl.CostEstimate(
            flops=depth * dim * rank, bytes_accessed=depth * dim + dim * rank, transcendentals=0
        ),
        name="product_of_half",
    )(half, embeddings, basis, *extra)


def route_kernel(capacity, line, plane, ids_ref, map_ref, dest_ref, label_ref):
    ids = jnp.concatenate([ids_ref[k : k + 1, :] for k in range(ids_ref.shape[0])], axis=1)
    count, (high, low) = ids.shape[1], map_ref.shape
    owner_count = 2 * plane * line
    bf16 = jnp.bfloat16

    def rows_of(size):
        return lax.broadcasted_iota(jnp.int32, (size, count), 0)

    picked = (rows_of(high) == ids // low).astype(bf16)
    found = lax.dot_general(
        map_ref[...].astype(bf16), picked, ROW_DIMS, preferred_element_type=jnp.float32
    )
    owner = jnp.sum(jnp.where(rows_of(low) == ids % low, found, 0.0), axis=0, keepdims=True)
    owner = owner.astype(jnp.int32)
    mine = rows_of(owner_count) == owner
    order = lax.broadcasted_iota(jnp.int32, (count, count), 1)
    earlier = (lax.broadcasted_iota(jnp.int32, (count, count), 0) < order).astype(bf16)
    before = jnp.dot(mine.astype(bf16), earlier, preferred_element_type=jnp.float32)
    slot = jnp.sum(jnp.where(mine, before, 0.0), axis=0, keepdims=True).astype(jnp.int32)
    dest_ref[...] = owner * capacity + slot
    value = ids + 1
    core, chip = owner // (plane * line), owner % (plane * line)
    row = (core * line + chip % line) * SLOTS + slot
    lane = rows_of(128) == 64 + 2 * (chip // line)
    lane = lane.astype(bf16)
    labels = None
    for digit in range(3):
        short = (value // 128**digit) % 128
        spread = jnp.where(rows_of(2 * line * SLOTS) == row, short.astype(jnp.float32), 0.0)
        term = lax.dot_general(
            spread.astype(bf16),
            lane,
            (((1,), (1,)), ((), ())),
            preferred_element_type=jnp.float32,
        )
        labels = term if labels is None else labels + term * 128**digit
    label_ref[...] = labels


def route_rows(list_ids, owner_map, capacity, line, plane):
    count = list_ids.shape[0]
    return pl.pallas_call(
        functools.partial(route_kernel, capacity, line, plane),
        out_shape=[
            jax.ShapeDtypeStruct((1, count), jnp.int32),
            jax.ShapeDtypeStruct((2 * line * SLOTS, 128), jnp.float32),
        ],
        compiler_params=GRANT,
        cost_estimate=pl.CostEstimate(
            flops=2_000_000_000, bytes_accessed=1048576, transcendentals=0
        ),
        name="route_rows",
    )(list_ids.reshape(-1, 128), owner_map.reshape(-1, 128))


def place_kernel(capacity, first_target, second_target, first_ref, second_ref, out_ref):
    pairs, _, width = out_ref.shape
    count = pairs * 2 * capacity
    slots = pl.program_id(0) * count + lax.broadcasted_iota(
        jnp.int32, (count, first_ref.shape[0]), 0
    )
    found = []
    for target_ref, rows_ref in ((first_target, first_ref), (second_target, second_ref)):
        onehot = (slots == target_ref[...]).astype(jnp.bfloat16)
        term = jnp.dot(onehot, rows_ref[...], preferred_element_type=jnp.float32)
        found.append(term.reshape(pairs, 2 * capacity, width))
    a, b = found
    out_ref[...] = jnp.concatenate(
        [a[:, :capacity], b[:, :capacity], a[:, capacity:], b[:, capacity:]], axis=1
    ).astype(jnp.bfloat16)


def place_rows(targets, first, second, chips, capacity):
    pairs = 16
    depth, width = first.shape
    return pl.pallas_call(
        functools.partial(place_kernel, capacity),
        grid=(chips // 2 // pairs,),
        in_specs=[pl.BlockSpec((1, depth), lambda i: (0, 0))] * 2
        + [pl.BlockSpec((depth, width), lambda i: (0, 0))] * 2,
        out_specs=pl.BlockSpec((pairs, 4 * capacity, width), lambda i: (i, 0, 0)),
        out_shape=jax.ShapeDtypeStruct((chips // 2, 4 * capacity, width), jnp.bfloat16),
        compiler_params=GRANT,
        cost_estimate=pl.CostEstimate(
            flops=4 * chips * capacity * depth * width,
            bytes_accessed=8 * chips * capacity * width,
            transcendentals=0,
        ),
        name="place_rows",
    )(*targets, first, second)


def shift(value, axis, step):
    size = lax.axis_size(axis)
    return lax.ppermute(value, axis, [(i, (i + step) % size) for i in range(size)])


def local(embeddings, sketch_seed, list_ids, owner_map):
    row_count, dim = embeddings.shape
    rank = sketch_seed.shape[1]
    cores, line = lax.axis_size("narrow"), lax.axis_size("x")
    plane = lax.axis_size("y") * lax.axis_size("z")
    chips = plane * line
    dev_count = cores * chips
    core = lax.axis_index("narrow")
    spot = lax.axis_index("x").reshape(1)
    own_half, other_half = core.reshape(1), (1 - core).reshape(1)
    piece, gram_piece = dim // dev_count, rank // chips
    seed_matrix = sketch_seed.astype(jnp.bfloat16)
    sketch = jnp.dot(embeddings, seed_matrix, preferred_element_type=jnp.float32).astype(
        jnp.bfloat16
    )

    capacity = 4 * row_count // dev_count
    here = lax.axis_index("x")
    dest_index, labels = route_rows(list_ids, owner_map, capacity, line, plane)

    spots = jnp.stack([core, here, jnp.int32(line)])

    def chunks_at(*steps):
        pairs = cross_chunks(spots, embeddings, sketch, labels, line, steps)
        return [(pairs[2 * i + 1], shift(pairs[2 * i], "narrow", 1)) for i in range(len(steps))]

    (far,) = chunks_at(2)
    up, down, near = chunks_at(1, 3, 0)
    far = far[0] + far[1]
    from_below = shift(far[: rank // 2], "x", 1)
    from_above = shift(far[rank // 2 :], "x", line - 1)
    from_below = [shift(part, "x", 1) for part in join_chunk(*up, from_below, 0)]
    from_above = [shift(part, "x", line - 1) for part in join_chunk(*down, from_above, 1)]
    arrived = [part.astype(jnp.float32) for part in from_below + from_above]

    def target_of(dest):
        owner = dest // capacity
        return jnp.where(owner // chips == core, (owner % chips) * capacity + dest % capacity, -1)

    def by_core(own, other):
        return jnp.where(core == 0, own, other), jnp.where(core == 0, other, own)

    targets = by_core(target_of(dest_index), target_of(shift(dest_index, "narrow", 1)))

    packed = line_total([*near, *arrived], plane, gram_piece)
    packed, targets = lax.optimization_barrier((packed, targets))
    packed = lax.all_to_all(packed.astype(jnp.float16), PLANE, 0, 0, tiled=True)
    packed = packed.astype(jnp.float32)
    packed, arrived_labels = plane_total(packed, piece, gram_piece)
    packed = jnp.broadcast_to(packed.astype(jnp.float16)[None], (plane,) + packed.shape)
    packed = lax.all_to_all(packed, PLANE, 0, 0, tiled=True)
    gram_line = gram_rows(packed[:, 2 * piece :].astype(jnp.float32), gram_piece)
    gram_parts = [gram_line] + [shift(gram_line, "x", step) for step in range(1, line)]
    packed, gram_parts[1] = lax.optimization_barrier((packed, gram_parts[1]))
    cross_line = packed[:, : 2 * piece + 8]
    cross_parts = [cross_line] + [shift(cross_line, "x", step) for step in range(1, line)]
    cross_parts = [part.astype(jnp.float32) for part in cross_parts]
    arrived_labels = arrived_labels[:, : cores * line * SLOTS].reshape(plane, cores, line, SLOTS)
    arrived_labels = arrived_labels[..., :capacity].transpose(1, 0, 2, 3)

    inverse = invert_factor(spot, gram_parts)
    inverse, cross_parts = lax.optimization_barrier((inverse, cross_parts))
    moment = moment_of(cross_parts)
    basis = project_half(spot, inverse, moment, shift(moment, "narrow", 1), cross_parts)
    other_basis = shift(basis, "narrow", 1)
    begun = product_of_half(own_half, embeddings, basis, None, jnp.float32)
    reduced = product_of_half(other_half, embeddings, other_basis, begun, jnp.bfloat16)
    rows = by_core(reduced, shift(reduced, "narrow", 1))
    send_rows = place_rows(targets, *rows, chips, capacity)
    send_rows = send_rows.reshape(chips, cores * capacity, rank)
    arrived = lax.all_to_all(send_rows, ("y", "z", "x"), 0, 0, tiled=True)
    arrived = arrived.reshape(chips, cores, capacity, rank).transpose(1, 0, 2, 3)
    return (
        arrived.reshape(1, dev_count, capacity, rank),
        arrived_labels.reshape(1, dev_count, capacity),
    )


def solution(mesh):
    grid = Mesh(mesh.devices.reshape(2, 4, 8, 4), ALL)
    in_specs = (P(ALL, None), P(), P(ALL), P())
    out_specs = (P(ALL, None, None, None), P(ALL, None, None))
    return jax.shard_map(local, mesh=grid, in_specs=in_specs, out_specs=out_specs, check_vma=False)
```

```python
import functools

import jax
import jax.numpy as jnp
from jax import lax
from jax.experimental import pallas as pl
from jax.experimental.pallas import tpu as pltpu
from jax.sharding import Mesh
from jax.sharding import PartitionSpec as P

NS_STEPS = 6
BLOCK = 64
TILE = 16
ALL = ("narrow", "y", "z", "x")
PLANE = ("y", "z")
HIGHEST = lax.Precision.HIGHEST
ROW_DIMS = (((0,), (0,)), ((), ()))
SLOTS = 16
GRANT = pltpu.CompilerParams(vmem_limit_bytes=16 * 2**20)


def dot_f32(a, b, dims=(((1,), (0,)), ((), ()))):
    return lax.dot_general(a, b, dims, precision=HIGHEST, preferred_element_type=jnp.float32)


def split_two(a):
    high = a.astype(jnp.bfloat16)
    return high, (a - high.astype(jnp.float32)).astype(jnp.bfloat16)


def dot_split(a, b):
    (ah, al), (bh, bl) = a, b
    mul = functools.partial(jnp.dot, preferred_element_type=jnp.float32)
    return mul(ah, bh) + (mul(ah, bl) + mul(al, bh))


POWERS = (64, 32, 16, 8, 4)


def scaled(value):
    top = jnp.max(jnp.abs(value), axis=(0, 1), keepdims=True)
    factor, power = jnp.ones_like(top), jnp.zeros_like(top)
    for p in POWERS:
        large = top * factor >= 2.0 ** (11 + p)
        factor = jnp.where(large, factor * 2.0**-p, factor)
        power = jnp.where(large, power - p, power)
    for p in POWERS:
        small = top * factor < 2.0 ** (15 - p)
        factor = jnp.where(small, factor * 2.0**p, factor)
        power = jnp.where(small, power + p, power)
    return value * factor, power


def unscale_factor(power):
    factor = jnp.ones_like(power)
    for p in POWERS:
        up, down = power >= p, power <= -p
        factor = jnp.where(up, factor * 2.0**-p, jnp.where(down, factor * 2.0**p, factor))
        power = jnp.where(up, power - p, jnp.where(down, power + p, power))
    return factor


def spread_rows(rows, gram, extra, count):
    def leaf(value):
        flat, power = scaled(value.reshape(-1, value.shape[2]))
        shape = (value.shape[0], 1, value.shape[2])
        return flat.reshape(value.shape), jnp.broadcast_to(power[None], shape)

    pieces = list(leaf(rows))
    gram, gram_power = leaf(gram)
    for term in range(3):
        short = gram.astype(jnp.bfloat16).astype(jnp.float32)
        pieces.append(short)
        gram = gram - short
    pieces += [gram_power] + extra
    filled = sum(p.shape[1] for p in pieces)
    if filled < count:
        shape = (rows.shape[0], count - filled, rows.shape[2])
        pieces.append(jnp.zeros(shape, jnp.float32))
    return jnp.concatenate(pieces, axis=1)


def joined_gram(parts, start, pair):
    terms = [parts[:, start + t * pair : start + (t + 1) * pair, :] for t in range(3)]
    power = parts[:, start + 3 * pair : start + 3 * pair + 1, :]
    return (terms[0] + (terms[1] + terms[2])) * unscale_factor(power)


def invert_kernel(spot_ref, *refs):
    parts, inverse_ref, work_ref = refs[:-2], refs[-2], refs[-1]
    rank = inverse_ref.shape[0]
    height = rank // len(parts)
    row_ids = lax.broadcasted_iota(jnp.int32, (rank, rank), 0)
    col_ids = lax.broadcasted_iota(jnp.int32, (rank, rank), 1)
    for step, part_ref in enumerate(parts):
        place = lax.rem(spot_ref[0] + len(parts) - step, len(parts))
        work_ref[pl.ds(pl.multiple_of(place * height, height), height), :rank] = part_ref[...]
    work_ref[:, rank:] = (row_ids == col_ids).astype(jnp.float32)
    lane = lax.broadcasted_iota(jnp.int32, (BLOCK, 128), 1)
    row = lax.broadcasted_iota(jnp.int32, (BLOCK, 128), 0)
    panel_lane = lax.broadcasted_iota(jnp.int32, (BLOCK, rank), 1)

    def block_step(step, carry):
        start = pl.multiple_of(step * BLOCK, BLOCK)
        panel = work_ref[pl.ds(start, BLOCK), :]
        shifted = pltpu.roll(panel[:, :rank], rank - start, 1)[:, :128]
        rest = jnp.where(lane < BLOCK, shifted, (lane - BLOCK == row).astype(jnp.float32))
        done = []
        for tile in range(BLOCK // TILE):
            height = BLOCK - tile * TILE
            sub = lax.broadcasted_iota(jnp.int32, (height, 128), 0)
            columns = [
                jnp.broadcast_to(rest[:, tile * TILE + j : tile * TILE + j + 1], (height, 128))
                for j in range(TILE)
            ]
            for j in range(TILE):
                pivot = columns[j][j : j + 1, :]
                scale = lax.rsqrt(pivot)
                scale = scale * (1.5 - 0.5 * (pivot * scale) * scale)
                below = jnp.where(sub > j, columns[j] * scale, 0.0)
                lead = rest[j : j + 1, :] * scale
                done.append(lead)
                rest = rest - below * lead
                for m in range(j + 1, TILE):
                    columns[m] = columns[m] - below * (columns[m][j : j + 1, :] * scale)
            rest = rest[TILE:, :]
        solved = jnp.concatenate(done, axis=0)
        small = pltpu.roll(solved, 128 - BLOCK, 1)[:, :BLOCK]
        panel = dot_f32(small, panel)
        inverse_ref[pl.ds(start, BLOCK), :] = panel[:, rank:]
        later = jnp.where(panel_lane >= start + BLOCK, panel[:, :rank], 0.0)
        work_ref[...] -= dot_f32(later, panel, (((0,), (0,)), ((), ())))
        return carry

    lax.fori_loop(0, rank // BLOCK, block_step, 0)


def invert_factor(spot, parts):
    rank = parts[0].shape[1]
    return pl.pallas_call(
        invert_kernel,
        in_specs=[pl.BlockSpec(memory_space=pltpu.SMEM)]
        + [pl.BlockSpec(memory_space=pltpu.VMEM)] * len(parts),
        out_shape=jax.ShapeDtypeStruct((rank, rank), jnp.float32),
        scratch_shapes=[pltpu.VMEM((rank, 2 * rank), jnp.float32)],
        compiler_params=GRANT,
        cost_estimate=pl.CostEstimate(flops=20_000_000_000, bytes_accessed=524288, transcendentals=0),
        name="invert_factor",
    )(spot, *parts)


def moment_kernel(*refs):
    total = None
    for part_ref in refs[:-1]:
        part = plain_rows(part_ref)
        term = dot_f32(part, part, ROW_DIMS)
        total = term if total is None else total + term
    refs[-1][...] = total


def moment_of(parts):
    rank = 2 * parts[0].shape[2]
    return pl.pallas_call(
        moment_kernel,
        out_shape=jax.ShapeDtypeStruct((rank, rank), jnp.float32),
        compiler_params=GRANT,
        cost_estimate=pl.CostEstimate(flops=4_000_000_000, bytes_accessed=2359296, transcendentals=0),
        name="moment_of",
    )(*parts)


def whiten_kernel(spot_ref, inverse_ref, moment_ref, other_ref, *refs):
    parts, out_ref = refs[:-1], refs[-1]
    inverse = inverse_ref[...]
    rank = inverse.shape[0]
    moment = moment_ref[...] + other_ref[...]
    cov_total = dot_f32(dot_f32(inverse, moment), inverse, (((1,), (1,)), ((), ())))
    row_ids = lax.broadcasted_iota(jnp.int32, (rank, rank), 0)
    col_ids = lax.broadcasted_iota(jnp.int32, (rank, rank), 1)
    eye_matrix = (row_ids == col_ids).astype(jnp.float32)
    trace_value = jnp.sum(cov_total * eye_matrix, axis=(0, 1), keepdims=True)
    left_iter = cov_total / trace_value
    right_iter = 1.5 * eye_matrix - 0.5 * left_iter
    right_parts = split_two(right_iter)
    left_parts = split_two(dot_split(split_two(left_iter), right_parts))
    for step_index in range(1, NS_STEPS):
        middle = split_two(1.5 * eye_matrix - 0.5 * dot_split(right_parts, left_parts))
        right_iter = dot_split(middle, right_parts)
        if step_index < NS_STEPS - 1:
            left_parts = split_two(dot_split(left_parts, middle))
            right_parts = split_two(right_iter)
    factor = right_iter / jnp.sqrt(trace_value)
    weight = split_two(dot_f32(inverse, factor, ROW_DIMS))
    height = out_ref.shape[0] // len(parts)
    for step, part_ref in enumerate(parts):
        place = lax.rem(spot_ref[0] + len(parts) - step, len(parts))
        rows = pl.ds(pl.multiple_of(place * height, height), height)
        out_ref[rows, :] = dot_split(split_two(plain_rows(part_ref)), weight).astype(jnp.bfloat16)


def project_half(spot, inverse, moment, other, parts):
    chunk, rank = parts[0].shape[0] * (parts[0].shape[1] - 8) // 2, inverse.shape[0]
    return pl.pallas_call(
        whiten_kernel,
        in_specs=[pl.BlockSpec(memory_space=pltpu.SMEM)]
        + [pl.BlockSpec(memory_space=pltpu.VMEM)] * (3 + len(parts)),
        out_shape=jax.ShapeDtypeStruct((chunk * len(parts), rank), jnp.bfloat16),
        compiler_params=GRANT,
        cost_estimate=pl.CostEstimate(flops=12_000_000_000, bytes_accessed=4194304, transcendentals=0),
        name="project_half",
    )(spot, inverse, moment, other, *parts)


def chunk_kernel(steps, spot_ref, rows_ref, sketch_ref, label_ref, *out_refs):
    core, here, line = (spot_ref[i] for i in range(3))
    rank = sketch_ref.shape[1]
    width = out_refs[0].shape[1] - 128
    half = rows_ref.shape[1] // 2
    sketch = sketch_ref[...]
    mul = functools.partial(
        lax.dot_general, dimension_numbers=ROW_DIMS, preferred_element_type=jnp.float32
    )
    gram_whole = mul(sketch, sketch)
    lane = lax.broadcasted_iota(jnp.int32, (rank, 128), 1)
    mine = pl.ds(pl.multiple_of((core * line + here) * SLOTS, SLOTS), SLOTS)
    for index, step in enumerate(steps):
        chunk = lax.rem(here + step, line)
        gram = pltpu.roll(gram_whole, rank - chunk * (rank * width // half), 1)[:, :128]
        gram = jnp.where(lane < rank * width // half, gram, 0.0)
        for out_ref, place in zip(out_refs[2 * index :], (1 - core, core)):
            columns = pl.ds(pl.multiple_of(place * half + chunk * width, width), width)
            out_ref[:, :width] = mul(sketch, rows_ref[:, columns])
            out_ref[:, width:] = gram
            theirs = pl.ds(pl.multiple_of((place * line + chunk) * SLOTS, SLOTS), SLOTS)
            out_ref[mine, width:] += label_ref[theirs, :]


def cross_chunks(spot, embeddings, sketch, labels, chunks, steps):
    count = len(steps)
    depth, dim = embeddings.shape
    rank = sketch.shape[1]
    width = dim // 2 // chunks
    shape = jax.ShapeDtypeStruct((rank, width + 128), jnp.float32)
    return pl.pallas_call(
        functools.partial(chunk_kernel, steps),
        in_specs=[pl.BlockSpec(memory_space=pltpu.SMEM)]
        + [pl.BlockSpec(memory_space=pltpu.VMEM)] * 3,
        out_shape=[shape] * (2 * count),
        compiler_params=GRANT,
        cost_estimate=pl.CostEstimate(
            flops=4 * depth * rank * width * count, bytes_accessed=3000000, transcendentals=0
        ),
        name="cross_chunks",
    )(spot, embeddings, sketch, labels)


def join_kernel(side, keep_ref, got_ref, extra_ref, body_ref, tail_ref):
    rank, width = body_ref.shape
    total = keep_ref[...] + got_ref[...]
    extra = jnp.concatenate(
        [extra_ref[...], jnp.zeros_like(extra_ref)][:: 1 - 2 * side], axis=0
    )
    total = total + extra
    body, power = scaled(total[:, :width])
    body_ref[...] = body
    tail = total[:, width:]
    row = lax.broadcasted_iota(jnp.int32, tail.shape, 0)
    lane = lax.broadcasted_iota(jnp.int32, tail.shape, 1)
    tail_ref[...] = jnp.where((row == rank - 1) & (lane >= 64), power, tail)


def join_chunk(keep, got, extra, side):
    rank, width = keep.shape
    body, tail = pl.pallas_call(
        functools.partial(join_kernel, side),
        out_shape=[
            jax.ShapeDtypeStruct((rank, width - 128), jnp.float32),
            jax.ShapeDtypeStruct((rank, 128), jnp.float32),
        ],
        compiler_params=GRANT,
        cost_estimate=pl.CostEstimate(flops=400000, bytes_accessed=2000000, transcendentals=0),
        name="join_chunk",
    )(keep, got, extra)
    return body.astype(jnp.float16), tail


def line_kernel(gram_piece, *refs):
    first, second, out_ref = refs[0], refs[1], refs[-1]
    plane = out_ref.shape[0]
    total = first[...] + second[...]
    rank, width = total.shape[0], total.shape[1] - 128
    body, tail = total[:, :width], total[:, width:]
    for body_ref, tail_ref in zip(refs[2:-1:2], refs[3:-1:2]):
        more = tail_ref[...]
        body = body + body_ref[...] * unscale_factor(more[rank - 1 :, 127:])
        tail = tail + more
    piece = width // plane
    turned = body.T.reshape(plane, piece, rank)
    tail = tail.T.reshape(2, plane, gram_piece, rank)
    gram, labels = tail[0], tail[1][:, :1, :128].astype(jnp.int32)
    digits = [(labels % 1024).astype(jnp.float32), (labels // 1024).astype(jnp.float32)]
    out_ref[...] = spread_rows(
        jnp.concatenate([turned[:, :, :128], turned[:, :, 128:]], axis=1),
        jnp.concatenate([gram[:, :, :128], gram[:, :, 128:]], axis=1),
        digits,
        out_ref.shape[1],
    )


def line_total(parts, plane, gram_piece):
    width = parts[0].shape[1] - 128
    rows = 2 * (width // plane) + 6 * gram_piece + 4
    rows += -rows % 16
    return pl.pallas_call(
        functools.partial(line_kernel, gram_piece),
        out_shape=jax.ShapeDtypeStruct((plane, rows, 128), jnp.float32),
        compiler_params=GRANT,
        cost_estimate=pl.CostEstimate(flops=1000000, bytes_accessed=4000000, transcendentals=0),
        name="line_total",
    )(*parts)


def plane_kernel(piece, gram_piece, parts_ref, out_ref, label_ref):
    cut, pair = 2 * piece, 2 * gram_piece
    parts = parts_ref[...]
    rows = jnp.sum(parts[:, :cut, :] * unscale_factor(parts[:, cut : cut + 1, :]), axis=0)
    gram = jnp.sum(joined_gram(parts, cut + 1, pair), axis=0)
    out_ref[...] = spread_rows(rows[None], gram[None], [], out_ref.shape[0])[0]
    end = cut + 2 + 3 * pair
    labels = parts[:, end, :] + 1024.0 * parts[:, end + 1, :]
    label_ref[...] = labels.astype(jnp.int32) - 1


def plane_total(parts, piece, gram_piece):
    plane, _, lanes = parts.shape
    rows = 2 * piece + 6 * gram_piece + 2
    rows += -rows % 16
    return pl.pallas_call(
        functools.partial(plane_kernel, piece, gram_piece),
        out_shape=[
            jax.ShapeDtypeStruct((rows, lanes), jnp.float32),
            jax.ShapeDtypeStruct((plane, lanes), jnp.int32),
        ],
        compiler_params=GRANT,
        cost_estimate=pl.CostEstimate(flops=1000000, bytes_accessed=1600000, transcendentals=0),
        name="plane_total",
    )(parts)


def plain_rows(part_ref):
    part = part_ref[...]
    cut = part.shape[1] - 8
    return whole_rows(part[:, :cut] * unscale_factor(part[:, cut : cut + 1]))


def whole_rows(part):
    plane, pair, lanes = part.shape
    sides = [part[:, : pair // 2], part[:, pair // 2 :]]
    return jnp.concatenate([t.reshape(plane * pair // 2, lanes) for t in sides], axis=1)


def gram_kernel(parts_ref, out_ref):
    pair = 2 * out_ref.shape[0] // parts_ref.shape[0]
    out_ref[...] = whole_rows(joined_gram(parts_ref[...], 1, pair))


def gram_rows(parts, gram_piece):
    plane, _, lanes = parts.shape
    return pl.pallas_call(
        gram_kernel,
        out_shape=jax.ShapeDtypeStruct((plane * gram_piece, 2 * lanes), jnp.float32),
        compiler_params=GRANT,
        cost_estimate=pl.CostEstimate(flops=10000, bytes_accessed=200000, transcendentals=0),
        name="gram_rows",
    )(parts)


def product_kernel(own, core_ref, rows_ref, basis_ref, *refs):
    place = core_ref[0] if own else 1 - core_ref[0]
    half, width = basis_ref.shape[0], 512
    total = None if len(refs) == 1 else refs[0][...]
    for step in range(half // width):
        columns = pl.ds(pl.multiple_of(place * half + step * width, width), width)
        basis = basis_ref[step * width : (step + 1) * width, :]
        term = jnp.dot(rows_ref[:, columns], basis, preferred_element_type=jnp.float32)
        total = term if total is None else total + term
    refs[-1][...] = total.astype(refs[-1].dtype)


def product_of_half(core, own, embeddings, basis, begin, out_type):
    depth, dim = embeddings.shape
    rank = basis.shape[1]
    extra = [] if begin is None else [begin]
    return pl.pallas_call(
        functools.partial(product_kernel, own),
        in_specs=[pl.BlockSpec(memory_space=pltpu.SMEM)]
        + [pl.BlockSpec(memory_space=pltpu.VMEM)] * (2 + len(extra)),
        out_shape=jax.ShapeDtypeStruct((depth, rank), out_type),
        compiler_params=GRANT,
        cost_estimate=pl.CostEstimate(
            flops=depth * dim * rank, bytes_accessed=depth * dim + dim * rank, transcendentals=0
        ),
        name="product_of_half",
    )(core, embeddings, basis, *extra)


def route_kernel(capacity, line, plane, ids_ref, map_ref, dest_ref, label_ref):
    ids = jnp.concatenate([ids_ref[k : k + 1, :] for k in range(ids_ref.shape[0])], axis=1)
    count, (high, low) = ids.shape[1], map_ref.shape
    owner_count = 2 * plane * line
    bf16 = jnp.bfloat16

    def rows_of(size):
        return lax.broadcasted_iota(jnp.int32, (size, count), 0)

    picked = (rows_of(high) == ids // low).astype(bf16)
    found = lax.dot_general(
        map_ref[...].astype(bf16), picked, ROW_DIMS, preferred_element_type=jnp.float32
    )
    owner = jnp.sum(jnp.where(rows_of(low) == ids % low, found, 0.0), axis=0, keepdims=True)
    owner = owner.astype(jnp.int32)
    mine = rows_of(owner_count) == owner
    order = lax.broadcasted_iota(jnp.int32, (count, count), 1)
    earlier = (lax.broadcasted_iota(jnp.int32, (count, count), 0) < order).astype(bf16)
    before = jnp.dot(mine.astype(bf16), earlier, preferred_element_type=jnp.float32)
    slot = jnp.sum(jnp.where(mine, before, 0.0), axis=0, keepdims=True).astype(jnp.int32)
    dest_ref[...] = owner * capacity + slot
    value = ids + 1
    core, chip = owner // (plane * line), owner % (plane * line)
    row = (core * line + chip % line) * SLOTS + slot
    lane = rows_of(128) == 64 + 2 * (chip // line)
    lane = lane.astype(bf16)
    labels = None
    for digit in range(3):
        short = (value // 128**digit) % 128
        spread = jnp.where(rows_of(2 * line * SLOTS) == row, short.astype(jnp.float32), 0.0)
        term = lax.dot_general(
            spread.astype(bf16),
            lane,
            (((1,), (1,)), ((), ())),
            preferred_element_type=jnp.float32,
        )
        labels = term if labels is None else labels + term * 128**digit
    label_ref[...] = labels


def route_rows(list_ids, owner_map, capacity, line, plane):
    count = list_ids.shape[0]
    return pl.pallas_call(
        functools.partial(route_kernel, capacity, line, plane),
        out_shape=[
            jax.ShapeDtypeStruct((1, count), jnp.int32),
            jax.ShapeDtypeStruct((2 * line * SLOTS, 128), jnp.float32),
        ],
        compiler_params=GRANT,
        cost_estimate=pl.CostEstimate(
            flops=2_000_000_000, bytes_accessed=1048576, transcendentals=0
        ),
        name="route_rows",
    )(list_ids.reshape(-1, 128), owner_map.reshape(-1, 128))


def place_kernel(capacity, core_ref, own_target, other_target, own_ref, other_ref, out_ref):
    pairs, _, width = out_ref.shape
    count = pairs * 2 * capacity
    slots = pl.program_id(0) * count + lax.broadcasted_iota(
        jnp.int32, (count, own_ref.shape[0]), 0
    )
    found = []
    for target_ref, rows_ref in ((own_target, own_ref), (other_target, other_ref)):
        onehot = (slots == target_ref[...]).astype(jnp.bfloat16)
        term = jnp.dot(onehot, rows_ref[...], preferred_element_type=jnp.float32)
        found.append(term.reshape(pairs, 2 * capacity, width))
    first = core_ref[0] == 0
    a = jnp.where(first, found[0], found[1])
    b = jnp.where(first, found[1], found[0])
    out_ref[...] = jnp.concatenate(
        [a[:, :capacity], b[:, :capacity], a[:, capacity:], b[:, capacity:]], axis=1
    ).astype(jnp.bfloat16)


def place_rows(core, targets, own, other, chips, capacity):
    pairs = 16
    depth, width = own.shape
    return pl.pallas_call(
        functools.partial(place_kernel, capacity),
        grid=(chips // 2 // pairs,),
        in_specs=[pl.BlockSpec(memory_space=pltpu.SMEM)]
        + [pl.BlockSpec((1, depth), lambda i: (0, 0))] * 2
        + [pl.BlockSpec((depth, width), lambda i: (0, 0))] * 2,
        out_specs=pl.BlockSpec((pairs, 4 * capacity, width), lambda i: (i, 0, 0)),
        out_shape=jax.ShapeDtypeStruct((chips // 2, 4 * capacity, width), jnp.bfloat16),
        compiler_params=GRANT,
        cost_estimate=pl.CostEstimate(
            flops=4 * chips * capacity * depth * width,
            bytes_accessed=8 * chips * capacity * width,
            transcendentals=0,
        ),
        name="place_rows",
    )(core, *targets, own, other)


def shift(value, axis, step):
    size = lax.axis_size(axis)
    return lax.ppermute(value, axis, [(i, (i + step) % size) for i in range(size)])


def local(embeddings, sketch_seed, list_ids, owner_map):
    row_count, dim = embeddings.shape
    rank = sketch_seed.shape[1]
    cores, line = lax.axis_size("narrow"), lax.axis_size("x")
    plane = lax.axis_size("y") * lax.axis_size("z")
    chips = plane * line
    dev_count = cores * chips
    core = lax.axis_index("narrow")
    spot = lax.axis_index("x").reshape(1)
    piece, gram_piece = dim // dev_count, rank // chips
    seed_matrix = sketch_seed.astype(jnp.bfloat16)
    sketch = jnp.dot(embeddings, seed_matrix, preferred_element_type=jnp.float32).astype(
        jnp.bfloat16
    )

    capacity = 4 * row_count // dev_count
    here = lax.axis_index("x")
    dest_index, labels = route_rows(list_ids, owner_map, capacity, line, plane)

    spots = jnp.stack([core, here, jnp.int32(line)])

    def chunks_at(*steps):
        pairs = cross_chunks(spots, embeddings, sketch, labels, line, steps)
        return [(pairs[2 * i + 1], shift(pairs[2 * i], "narrow", 1)) for i in range(len(steps))]

    (far,) = chunks_at(2)
    up, down, near = chunks_at(1, 3, 0)
    far = far[0] + far[1]
    from_below = shift(far[: rank // 2], "x", 1)
    from_above = shift(far[rank // 2 :], "x", line - 1)
    from_below = [shift(part, "x", 1) for part in join_chunk(*up, from_below, 0)]
    from_above = [shift(part, "x", line - 1) for part in join_chunk(*down, from_above, 1)]
    arrived = [part.astype(jnp.float32) for part in from_below + from_above]

    def target_of(dest):
        owner = dest // capacity
        return jnp.where(owner // chips == core, (owner % chips) * capacity + dest % capacity, -1)

    targets = target_of(dest_index), target_of(shift(dest_index, "narrow", 1))

    packed = line_total([*near, *arrived], plane, gram_piece)
    packed, targets = lax.optimization_barrier((packed, targets))
    packed = lax.all_to_all(packed.astype(jnp.float16), PLANE, 0, 0, tiled=True)
    packed = packed.astype(jnp.float32)
    packed, arrived_labels = plane_total(packed, piece, gram_piece)
    packed = jnp.broadcast_to(packed.astype(jnp.float16)[None], (plane,) + packed.shape)
    packed = lax.all_to_all(packed, PLANE, 0, 0, tiled=True)
    gram_line = gram_rows(packed[:, 2 * piece :].astype(jnp.float32), gram_piece)
    gram_parts = [gram_line] + [shift(gram_line, "x", step) for step in range(1, line)]
    packed, gram_parts[1] = lax.optimization_barrier((packed, gram_parts[1]))
    cross_line = packed[:, : 2 * piece + 8]
    cross_parts = [cross_line] + [shift(cross_line, "x", step) for step in range(1, line)]
    cross_parts = [part.astype(jnp.float32) for part in cross_parts]
    arrived_labels = arrived_labels[:, : cores * line * SLOTS].reshape(plane, cores, line, SLOTS)
    arrived_labels = arrived_labels[..., :capacity].transpose(1, 0, 2, 3)

    inverse = invert_factor(spot, gram_parts)
    inverse, cross_parts = lax.optimization_barrier((inverse, cross_parts))
    moment = moment_of(cross_parts)
    basis = project_half(spot, inverse, moment, shift(moment, "narrow", 1), cross_parts)
    other_basis = shift(basis, "narrow", 1)
    begun = product_of_half(spots, True, embeddings, basis, None, jnp.float32)
    reduced = product_of_half(spots, False, embeddings, other_basis, begun, jnp.bfloat16)
    other = shift(reduced, "narrow", 1)
    send_rows = place_rows(spots, targets, reduced, other, chips, capacity)
    send_rows = send_rows.reshape(chips, cores * capacity, rank)
    arrived = lax.all_to_all(send_rows, ("y", "z", "x"), 0, 0, tiled=True)
    arrived = arrived.reshape(chips, cores, capacity, rank).transpose(1, 0, 2, 3)
    return (
        arrived.reshape(1, dev_count, capacity, rank),
        arrived_labels.reshape(1, dev_count, capacity),
    )


def solution(mesh):
    grid = Mesh(mesh.devices.reshape(2, 4, 8, 4), ALL)
    in_specs = (P(ALL, None), P(), P(ALL), P())
    out_specs = (P(ALL, None, None, None), P(ALL, None, None))
    return jax.shard_map(local, mesh=grid, in_specs=in_specs, out_specs=out_specs, check_vma=False)
```

```python
import functools

import jax
import jax.numpy as jnp
from jax import lax
from jax.experimental import pallas as pl
from jax.experimental.pallas import tpu as pltpu
from jax.sharding import Mesh
from jax.sharding import PartitionSpec as P

NS_STEPS = 6
BLOCK = 64
TILE = 16
ALL = ("narrow", "y", "z", "x")
PLANE = ("y", "z")
HIGHEST = lax.Precision.HIGHEST
ROW_DIMS = (((0,), (0,)), ((), ()))
SLOTS = 16
GRANT = pltpu.CompilerParams(vmem_limit_bytes=16 * 2**20)


def dot_f32(a, b, dims=(((1,), (0,)), ((), ()))):
    return lax.dot_general(a, b, dims, precision=HIGHEST, preferred_element_type=jnp.float32)


def split_two(a):
    high = a.astype(jnp.bfloat16)
    return high, (a - high.astype(jnp.float32)).astype(jnp.bfloat16)


def dot_split(a, b):
    (ah, al), (bh, bl) = a, b
    mul = functools.partial(jnp.dot, preferred_element_type=jnp.float32)
    return mul(ah, bh) + (mul(ah, bl) + mul(al, bh))


POWERS = (64, 32, 16, 8, 4)


def scaled(value):
    top = jnp.max(jnp.abs(value), axis=(0, 1), keepdims=True)
    factor, power = jnp.ones_like(top), jnp.zeros_like(top)
    for p in POWERS:
        large = top * factor >= 2.0 ** (11 + p)
        factor = jnp.where(large, factor * 2.0**-p, factor)
        power = jnp.where(large, power - p, power)
    for p in POWERS:
        small = top * factor < 2.0 ** (15 - p)
        factor = jnp.where(small, factor * 2.0**p, factor)
        power = jnp.where(small, power + p, power)
    return value * factor, power


def unscale_factor(power):
    factor = jnp.ones_like(power)
    for p in POWERS:
        up, down = power >= p, power <= -p
        factor = jnp.where(up, factor * 2.0**-p, jnp.where(down, factor * 2.0**p, factor))
        power = jnp.where(up, power - p, jnp.where(down, power + p, power))
    return factor


def spread_rows(rows, gram, extra, count):
    def leaf(value):
        flat, power = scaled(value.reshape(-1, value.shape[2]))
        shape = (value.shape[0], 1, value.shape[2])
        return flat.reshape(value.shape), jnp.broadcast_to(power[None], shape)

    pieces = list(leaf(rows))
    gram, gram_power = leaf(gram)
    for term in range(3):
        short = gram.astype(jnp.bfloat16).astype(jnp.float32)
        pieces.append(short)
        gram = gram - short
    pieces += [gram_power] + extra
    filled = sum(p.shape[1] for p in pieces)
    if filled < count:
        shape = (rows.shape[0], count - filled, rows.shape[2])
        pieces.append(jnp.zeros(shape, jnp.float32))
    return jnp.concatenate(pieces, axis=1)


def joined_gram(parts, start, pair):
    terms = [parts[:, start + t * pair : start + (t + 1) * pair, :] for t in range(3)]
    power = parts[:, start + 3 * pair : start + 3 * pair + 1, :]
    return (terms[0] + (terms[1] + terms[2])) * unscale_factor(power)


def invert_kernel(spot_ref, *refs):
    parts, inverse_ref, work_ref = refs[:-2], refs[-2], refs[-1]
    rank = inverse_ref.shape[0]
    height = rank // len(parts)
    row_ids = lax.broadcasted_iota(jnp.int32, (rank, rank), 0)
    col_ids = lax.broadcasted_iota(jnp.int32, (rank, rank), 1)
    for step, part_ref in enumerate(parts):
        place = lax.rem(spot_ref[0] + len(parts) - step, len(parts))
        work_ref[pl.ds(pl.multiple_of(place * height, height), height), :rank] = part_ref[...]
    work_ref[:, rank:] = (row_ids == col_ids).astype(jnp.float32)
    lane = lax.broadcasted_iota(jnp.int32, (BLOCK, 128), 1)
    row = lax.broadcasted_iota(jnp.int32, (BLOCK, 128), 0)
    panel_lane = lax.broadcasted_iota(jnp.int32, (BLOCK, rank), 1)

    def block_step(step, carry):
        start = pl.multiple_of(step * BLOCK, BLOCK)
        panel = work_ref[pl.ds(start, BLOCK), :]
        shifted = pltpu.roll(panel[:, :rank], rank - start, 1)[:, :128]
        rest = jnp.where(lane < BLOCK, shifted, (lane - BLOCK == row).astype(jnp.float32))
        done = []
        for tile in range(BLOCK // TILE):
            height = BLOCK - tile * TILE
            sub = lax.broadcasted_iota(jnp.int32, (height, 128), 0)
            columns = [
                jnp.broadcast_to(rest[:, tile * TILE + j : tile * TILE + j + 1], (height, 128))
                for j in range(TILE)
            ]
            for j in range(TILE):
                pivot = columns[j][j : j + 1, :]
                scale = lax.rsqrt(pivot)
                scale = scale * (1.5 - 0.5 * (pivot * scale) * scale)
                below = jnp.where(sub > j, columns[j] * scale, 0.0)
                lead = rest[j : j + 1, :] * scale
                done.append(lead)
                rest = rest - below * lead
                for m in range(j + 1, TILE):
                    columns[m] = columns[m] - below * (columns[m][j : j + 1, :] * scale)
            rest = rest[TILE:, :]
        solved = jnp.concatenate(done, axis=0)
        small = pltpu.roll(solved, 128 - BLOCK, 1)[:, :BLOCK]
        panel = dot_f32(small, panel)
        inverse_ref[pl.ds(start, BLOCK), :] = panel[:, rank:]
        later = jnp.where(panel_lane >= start + BLOCK, panel[:, :rank], 0.0)
        work_ref[...] -= dot_f32(later, panel, (((0,), (0,)), ((), ())))
        return carry

    lax.fori_loop(0, rank // BLOCK, block_step, 0)


def invert_factor(spot, parts):
    rank = parts[0].shape[1]
    return pl.pallas_call(
        invert_kernel,
        in_specs=[pl.BlockSpec(memory_space=pltpu.SMEM)]
        + [pl.BlockSpec(memory_space=pltpu.VMEM)] * len(parts),
        out_shape=jax.ShapeDtypeStruct((rank, rank), jnp.float32),
        scratch_shapes=[pltpu.VMEM((rank, 2 * rank), jnp.float32)],
        compiler_params=GRANT,
        cost_estimate=pl.CostEstimate(flops=20_000_000_000, bytes_accessed=524288, transcendentals=0),
        name="invert_factor",
    )(spot, *parts)


def moment_kernel(*refs):
    total = None
    for part_ref in refs[:-1]:
        part = plain_rows(part_ref)
        term = dot_f32(part, part, ROW_DIMS)
        total = term if total is None else total + term
    refs[-1][...] = total


def moment_of(parts):
    rank = 2 * parts[0].shape[2]
    return pl.pallas_call(
        moment_kernel,
        out_shape=jax.ShapeDtypeStruct((rank, rank), jnp.float32),
        compiler_params=GRANT,
        cost_estimate=pl.CostEstimate(flops=4_000_000_000, bytes_accessed=2359296, transcendentals=0),
        name="moment_of",
    )(*parts)


def whiten_kernel(spot_ref, inverse_ref, moment_ref, other_ref, *refs):
    parts, out_ref = refs[:-1], refs[-1]
    inverse = inverse_ref[...]
    rank = inverse.shape[0]
    moment = moment_ref[...] + other_ref[...]
    cov_total = dot_f32(dot_f32(inverse, moment), inverse, (((1,), (1,)), ((), ())))
    row_ids = lax.broadcasted_iota(jnp.int32, (rank, rank), 0)
    col_ids = lax.broadcasted_iota(jnp.int32, (rank, rank), 1)
    eye_matrix = (row_ids == col_ids).astype(jnp.float32)
    trace_value = jnp.sum(cov_total * eye_matrix, axis=(0, 1), keepdims=True)
    left_iter = cov_total / trace_value
    right_iter = 1.5 * eye_matrix - 0.5 * left_iter
    right_parts = split_two(right_iter)
    left_parts = split_two(dot_split(split_two(left_iter), right_parts))
    for step_index in range(1, NS_STEPS):
        middle = split_two(1.5 * eye_matrix - 0.5 * dot_split(right_parts, left_parts))
        right_iter = dot_split(middle, right_parts)
        if step_index < NS_STEPS - 1:
            left_parts = split_two(dot_split(left_parts, middle))
            right_parts = split_two(right_iter)
    factor = right_iter / jnp.sqrt(trace_value)
    weight = split_two(dot_f32(inverse, factor, ROW_DIMS))
    height = out_ref.shape[0] // len(parts)
    for step, part_ref in enumerate(parts):
        place = lax.rem(spot_ref[0] + len(parts) - step, len(parts))
        rows = pl.ds(pl.multiple_of(place * height, height), height)
        out_ref[rows, :] = dot_split(split_two(plain_rows(part_ref)), weight).astype(jnp.bfloat16)


def project_half(spot, inverse, moment, other, parts):
    chunk, rank = parts[0].shape[0] * (parts[0].shape[1] - 8) // 2, inverse.shape[0]
    return pl.pallas_call(
        whiten_kernel,
        in_specs=[pl.BlockSpec(memory_space=pltpu.SMEM)]
        + [pl.BlockSpec(memory_space=pltpu.VMEM)] * (3 + len(parts)),
        out_shape=jax.ShapeDtypeStruct((chunk * len(parts), rank), jnp.bfloat16),
        compiler_params=GRANT,
        cost_estimate=pl.CostEstimate(flops=12_000_000_000, bytes_accessed=4194304, transcendentals=0),
        name="project_half",
    )(spot, inverse, moment, other, *parts)


def chunk_kernel(steps, spot_ref, rows_ref, sketch_ref, label_ref, *out_refs):
    core, here, line = (spot_ref[i] for i in range(3))
    rank = sketch_ref.shape[1]
    width = out_refs[0].shape[1] - 128
    half = rows_ref.shape[1] // 2
    sketch = sketch_ref[...]
    mul = functools.partial(
        lax.dot_general, dimension_numbers=ROW_DIMS, preferred_element_type=jnp.float32
    )
    gram_whole = mul(sketch, sketch)
    lane = lax.broadcasted_iota(jnp.int32, (rank, 128), 1)
    mine = pl.ds(pl.multiple_of((core * line + here) * SLOTS, SLOTS), SLOTS)
    for index, step in enumerate(steps):
        chunk = lax.rem(here + step, line)
        gram = pltpu.roll(gram_whole, rank - chunk * (rank * width // half), 1)[:, :128]
        gram = jnp.where(lane < rank * width // half, gram, 0.0)
        for out_ref, place in zip(out_refs[2 * index :], (1 - core, core)):
            columns = pl.ds(pl.multiple_of(place * half + chunk * width, width), width)
            out_ref[:, :width] = mul(sketch, rows_ref[:, columns])
            out_ref[:, width:] = gram
            theirs = pl.ds(pl.multiple_of((place * line + chunk) * SLOTS, SLOTS), SLOTS)
            out_ref[mine, width:] += label_ref[theirs, :]


def cross_chunks(spot, embeddings, sketch, labels, chunks, steps):
    count = len(steps)
    depth, dim = embeddings.shape
    rank = sketch.shape[1]
    width = dim // 2 // chunks
    shape = jax.ShapeDtypeStruct((rank, width + 128), jnp.float32)
    return pl.pallas_call(
        functools.partial(chunk_kernel, steps),
        in_specs=[pl.BlockSpec(memory_space=pltpu.SMEM)]
        + [pl.BlockSpec(memory_space=pltpu.VMEM)] * 3,
        out_shape=[shape] * (2 * count),
        compiler_params=GRANT,
        cost_estimate=pl.CostEstimate(
            flops=4 * depth * rank * width * count, bytes_accessed=3000000, transcendentals=0
        ),
        name="cross_chunks",
    )(spot, embeddings, sketch, labels)


def join_kernel(side, keep_ref, got_ref, extra_ref, body_ref, tail_ref):
    rank, width = body_ref.shape
    total = keep_ref[...] + got_ref[...]
    extra = jnp.concatenate(
        [extra_ref[...], jnp.zeros_like(extra_ref)][:: 1 - 2 * side], axis=0
    )
    total = total + extra
    body, power = scaled(total[:, :width])
    body_ref[...] = body
    tail = total[:, width:]
    row = lax.broadcasted_iota(jnp.int32, tail.shape, 0)
    lane = lax.broadcasted_iota(jnp.int32, tail.shape, 1)
    tail_ref[...] = jnp.where((row == rank - 1) & (lane >= 64), power, tail)


def join_chunk(keep, got, extra, side):
    rank, width = keep.shape
    body, tail = pl.pallas_call(
        functools.partial(join_kernel, side),
        out_shape=[
            jax.ShapeDtypeStruct((rank, width - 128), jnp.float32),
            jax.ShapeDtypeStruct((rank, 128), jnp.float32),
        ],
        compiler_params=GRANT,
        cost_estimate=pl.CostEstimate(flops=400000, bytes_accessed=2000000, transcendentals=0),
        name="join_chunk",
    )(keep, got, extra)
    return body.astype(jnp.float16), tail


def line_kernel(gram_piece, *refs):
    first, second, out_ref = refs[0], refs[1], refs[-1]
    plane = out_ref.shape[0]
    total = first[...] + second[...]
    rank, width = total.shape[0], total.shape[1] - 128
    body, tail = total[:, :width], total[:, width:]
    for body_ref, tail_ref in zip(refs[2:-1:2], refs[3:-1:2]):
        more = tail_ref[...]
        body = body + body_ref[...] * unscale_factor(more[rank - 1 :, 127:])
        tail = tail + more
    piece = width // plane
    turned = body.T.reshape(plane, piece, rank)
    tail = tail.T.reshape(2, plane, gram_piece, rank)
    gram, labels = tail[0], tail[1][:, :1, :128].astype(jnp.int32)
    digits = [(labels % 1024).astype(jnp.float32), (labels // 1024).astype(jnp.float32)]
    out_ref[...] = spread_rows(
        jnp.concatenate([turned[:, :, :128], turned[:, :, 128:]], axis=1),
        jnp.concatenate([gram[:, :, :128], gram[:, :, 128:]], axis=1),
        digits,
        out_ref.shape[1],
    )


def line_total(parts, plane, gram_piece):
    width = parts[0].shape[1] - 128
    rows = 2 * (width // plane) + 6 * gram_piece + 4
    rows += -rows % 16
    return pl.pallas_call(
        functools.partial(line_kernel, gram_piece),
        out_shape=jax.ShapeDtypeStruct((plane, rows, 128), jnp.float32),
        compiler_params=GRANT,
        cost_estimate=pl.CostEstimate(flops=1000000, bytes_accessed=4000000, transcendentals=0),
        name="line_total",
    )(*parts)


def plane_kernel(piece, gram_piece, parts_ref, out_ref, label_ref):
    cut, pair = 2 * piece, 2 * gram_piece
    parts = parts_ref[...]
    rows = jnp.sum(parts[:, :cut, :] * unscale_factor(parts[:, cut : cut + 1, :]), axis=0)
    gram = jnp.sum(joined_gram(parts, cut + 1, pair), axis=0)
    out_ref[...] = spread_rows(rows[None], gram[None], [], out_ref.shape[0])[0]
    end = cut + 2 + 3 * pair
    labels = parts[:, end, :] + 1024.0 * parts[:, end + 1, :]
    label_ref[...] = labels.astype(jnp.int32) - 1


def plane_total(parts, piece, gram_piece):
    plane, _, lanes = parts.shape
    rows = 2 * piece + 6 * gram_piece + 2
    rows += -rows % 16
    return pl.pallas_call(
        functools.partial(plane_kernel, piece, gram_piece),
        out_shape=[
            jax.ShapeDtypeStruct((rows, lanes), jnp.float32),
            jax.ShapeDtypeStruct((plane, lanes), jnp.int32),
        ],
        compiler_params=GRANT,
        cost_estimate=pl.CostEstimate(flops=1000000, bytes_accessed=1600000, transcendentals=0),
        name="plane_total",
    )(parts)


def plain_rows(part_ref):
    part = part_ref[...]
    cut = part.shape[1] - 8
    return whole_rows(part[:, :cut] * unscale_factor(part[:, cut : cut + 1]))


def whole_rows(part):
    plane, pair, lanes = part.shape
    sides = [part[:, : pair // 2], part[:, pair // 2 :]]
    return jnp.concatenate([t.reshape(plane * pair // 2, lanes) for t in sides], axis=1)


def gram_kernel(parts_ref, out_ref):
    pair = 2 * out_ref.shape[0] // parts_ref.shape[0]
    out_ref[...] = whole_rows(joined_gram(parts_ref[...], 1, pair))


def gram_rows(parts, gram_piece):
    plane, _, lanes = parts.shape
    return pl.pallas_call(
        gram_kernel,
        out_shape=jax.ShapeDtypeStruct((plane * gram_piece, 2 * lanes), jnp.float32),
        compiler_params=GRANT,
        cost_estimate=pl.CostEstimate(flops=10000, bytes_accessed=200000, transcendentals=0),
        name="gram_rows",
    )(parts)


def product_kernel(own, core_ref, rows_ref, basis_ref, *refs):
    place = core_ref[0] if own else 1 - core_ref[0]
    half, width = basis_ref.shape[0], 512
    total = None if len(refs) == 1 else refs[0][...]
    for step in range(half // width):
        columns = pl.ds(pl.multiple_of(place * half + step * width, width), width)
        basis = basis_ref[step * width : (step + 1) * width, :]
        term = jnp.dot(rows_ref[:, columns], basis, preferred_element_type=jnp.float32)
        total = term if total is None else total + term
    refs[-1][...] = total.astype(refs[-1].dtype)


def product_of_half(core, own, embeddings, basis, begin, out_type):
    depth, dim = embeddings.shape
    rank = basis.shape[1]
    extra = [] if begin is None else [begin]
    return pl.pallas_call(
        functools.partial(product_kernel, own),
        in_specs=[pl.BlockSpec(memory_space=pltpu.SMEM)]
        + [pl.BlockSpec(memory_space=pltpu.VMEM)] * (2 + len(extra)),
        out_shape=jax.ShapeDtypeStruct((depth, rank), out_type),
        compiler_params=GRANT,
        cost_estimate=pl.CostEstimate(
            flops=depth * dim * rank, bytes_accessed=depth * dim + dim * rank, transcendentals=0
        ),
        name="product_of_half",
    )(core, embeddings, basis, *extra)


def route_kernel(capacity, line, plane, ids_ref, map_ref, dest_ref, label_ref):
    ids = jnp.concatenate([ids_ref[k : k + 1, :] for k in range(ids_ref.shape[0])], axis=1)
    count, (high, low) = ids.shape[1], map_ref.shape
    owner_count = 2 * plane * line
    bf16 = jnp.bfloat16

    def rows_of(size):
        return lax.broadcasted_iota(jnp.int32, (size, count), 0)

    picked = (rows_of(high) == ids // low).astype(bf16)
    found = lax.dot_general(
        map_ref[...].astype(bf16), picked, ROW_DIMS, preferred_element_type=jnp.float32
    )
    owner = jnp.sum(jnp.where(rows_of(low) == ids % low, found, 0.0), axis=0, keepdims=True)
    owner = owner.astype(jnp.int32)
    mine = rows_of(owner_count) == owner
    order = lax.broadcasted_iota(jnp.int32, (count, count), 1)
    earlier = (lax.broadcasted_iota(jnp.int32, (count, count), 0) < order).astype(bf16)
    before = jnp.dot(mine.astype(bf16), earlier, preferred_element_type=jnp.float32)
    slot = jnp.sum(jnp.where(mine, before, 0.0), axis=0, keepdims=True).astype(jnp.int32)
    dest_ref[...] = owner * capacity + slot
    value = ids + 1
    core, chip = owner // (plane * line), owner % (plane * line)
    row = (core * line + chip % line) * SLOTS + slot
    lane = rows_of(128) == 64 + 2 * (chip // line)
    lane = lane.astype(bf16)
    labels = None
    for digit in range(3):
        short = (value // 128**digit) % 128
        spread = jnp.where(rows_of(2 * line * SLOTS) == row, short.astype(jnp.float32), 0.0)
        term = lax.dot_general(
            spread.astype(bf16),
            lane,
            (((1,), (1,)), ((), ())),
            preferred_element_type=jnp.float32,
        )
        labels = term if labels is None else labels + term * 128**digit
    label_ref[...] = labels


def route_rows(list_ids, owner_map, capacity, line, plane):
    count = list_ids.shape[0]
    return pl.pallas_call(
        functools.partial(route_kernel, capacity, line, plane),
        out_shape=[
            jax.ShapeDtypeStruct((1, count), jnp.int32),
            jax.ShapeDtypeStruct((2 * line * SLOTS, 128), jnp.float32),
        ],
        compiler_params=GRANT,
        cost_estimate=pl.CostEstimate(
            flops=2_000_000_000, bytes_accessed=1048576, transcendentals=0
        ),
        name="route_rows",
    )(list_ids.reshape(-1, 128), owner_map.reshape(-1, 128))


def place_kernel(capacity, core_ref, own_target, other_target, own_ref, other_ref, out_ref):
    pairs, _, width = out_ref.shape
    count = pairs * 2 * capacity
    slots = pl.program_id(0) * count + lax.broadcasted_iota(
        jnp.int32, (count, own_ref.shape[0]), 0
    )
    found = []
    for target_ref, rows_ref in ((own_target, own_ref), (other_target, other_ref)):
        onehot = (slots == target_ref[...]).astype(jnp.bfloat16)
        term = jnp.dot(onehot, rows_ref[...], preferred_element_type=jnp.float32)
        found.append(term.reshape(pairs, 2 * capacity, width))
    first = core_ref[0] == 0
    a = jnp.where(first, found[0], found[1])
    b = jnp.where(first, found[1], found[0])
    out_ref[...] = jnp.concatenate(
        [a[:, :capacity], b[:, :capacity], a[:, capacity:], b[:, capacity:]], axis=1
    ).astype(jnp.bfloat16)


def place_rows(core, targets, own, other, chips, capacity):
    pairs = 16
    depth, width = own.shape
    return pl.pallas_call(
        functools.partial(place_kernel, capacity),
        grid=(chips // 2 // pairs,),
        in_specs=[pl.BlockSpec(memory_space=pltpu.SMEM)]
        + [pl.BlockSpec((1, depth), lambda i: (0, 0))] * 2
        + [pl.BlockSpec((depth, width), lambda i: (0, 0))] * 2,
        out_specs=pl.BlockSpec((pairs, 4 * capacity, width), lambda i: (i, 0, 0)),
        out_shape=jax.ShapeDtypeStruct((chips // 2, 4 * capacity, width), jnp.bfloat16),
        compiler_params=GRANT,
        cost_estimate=pl.CostEstimate(
            flops=4 * chips * capacity * depth * width,
            bytes_accessed=8 * chips * capacity * width,
            transcendentals=0,
        ),
        name="place_rows",
    )(core, *targets, own, other)


def shift(value, axis, step):
    size = lax.axis_size(axis)
    return lax.ppermute(value, axis, [(i, (i + step) % size) for i in range(size)])


def local(embeddings, sketch_seed, list_ids, owner_map):
    row_count, dim = embeddings.shape
    rank = sketch_seed.shape[1]
    cores, line = lax.axis_size("narrow"), lax.axis_size("x")
    plane = lax.axis_size("y") * lax.axis_size("z")
    chips = plane * line
    dev_count = cores * chips
    core = lax.axis_index("narrow")
    spot = lax.axis_index("x").reshape(1)
    piece, gram_piece = dim // dev_count, rank // chips
    seed_matrix = sketch_seed.astype(jnp.bfloat16)
    sketch = jnp.dot(embeddings, seed_matrix, preferred_element_type=jnp.float32).astype(
        jnp.bfloat16
    )

    capacity = 4 * row_count // dev_count
    here = lax.axis_index("x")
    dest_index, labels = route_rows(list_ids, owner_map, capacity, line, plane)

    spots = jnp.stack([core, here, jnp.int32(line)])

    def chunks_at(*steps):
        pairs = cross_chunks(spots, embeddings, sketch, labels, line, steps)
        return [(pairs[2 * i + 1], shift(pairs[2 * i], "narrow", 1)) for i in range(len(steps))]

    (far,) = chunks_at(2)
    up, down, near = chunks_at(1, 3, 0)
    far = far[0] + far[1]
    from_below = shift(far[: rank // 2], "x", 1)
    from_above = shift(far[rank // 2 :], "x", line - 1)
    from_below = [shift(part, "x", 1) for part in join_chunk(*up, from_below, 0)]
    from_above = [shift(part, "x", line - 1) for part in join_chunk(*down, from_above, 1)]
    arrived = [part.astype(jnp.float32) for part in from_below + from_above]

    def target_of(dest):
        owner = dest // capacity
        return jnp.where(owner // chips == core, (owner % chips) * capacity + dest % capacity, -1)

    targets = target_of(dest_index), target_of(shift(dest_index, "narrow", 1))

    packed = line_total([*near, *arrived], plane, gram_piece)
    packed, targets = lax.optimization_barrier((packed, targets))
    packed = lax.all_to_all(packed.astype(jnp.float16), PLANE, 0, 0, tiled=True)
    packed = packed.astype(jnp.float32)
    packed, arrived_labels = plane_total(packed, piece, gram_piece)
    packed = jnp.broadcast_to(packed.astype(jnp.float16)[None], (plane,) + packed.shape)
    packed = lax.all_to_all(packed, PLANE, 0, 0, tiled=True)
    gram_line = gram_rows(packed[:, 2 * piece :].astype(jnp.float32), gram_piece)
    packed, gram_line = lax.optimization_barrier((packed, gram_line))
    gram_parts = [gram_line] + [shift(gram_line, "x", step) for step in range(1, line)]
    cross_line = packed[:, : 2 * piece + 8]
    cross_parts = [cross_line] + [shift(cross_line, "x", step) for step in range(1, line)]
    cross_parts = [part.astype(jnp.float32) for part in cross_parts]
    arrived_labels = arrived_labels[:, : cores * line * SLOTS].reshape(plane, cores, line, SLOTS)
    arrived_labels = arrived_labels[..., :capacity].transpose(1, 0, 2, 3)

    inverse = invert_factor(spot, gram_parts)
    inverse, cross_parts = lax.optimization_barrier((inverse, cross_parts))
    moment = moment_of(cross_parts)
    basis = project_half(spot, inverse, moment, shift(moment, "narrow", 1), cross_parts)
    other_basis = shift(basis, "narrow", 1)
    begun = product_of_half(spots, True, embeddings, basis, None, jnp.float32)
    reduced = product_of_half(spots, False, embeddings, other_basis, begun, jnp.bfloat16)
    other = shift(reduced, "narrow", 1)
    send_rows = place_rows(spots, targets, reduced, other, chips, capacity)
    send_rows = send_rows.reshape(chips, cores * capacity, rank)
    arrived = lax.all_to_all(send_rows, ("y", "z", "x"), 0, 0, tiled=True)
    arrived = arrived.reshape(chips, cores, capacity, rank).transpose(1, 0, 2, 3)
    return (
        arrived.reshape(1, dev_count, capacity, rank),
        arrived_labels.reshape(1, dev_count, capacity),
    )


def solution(mesh):
    grid = Mesh(mesh.devices.reshape(2, 4, 8, 4), ALL)
    in_specs = (P(ALL, None), P(), P(ALL), P())
    out_specs = (P(ALL, None, None, None), P(ALL, None, None))
    return jax.shard_map(local, mesh=grid, in_specs=in_specs, out_specs=out_specs, check_vma=False)
```

```python
import functools

import jax
import jax.numpy as jnp
from jax import lax
from jax.experimental import pallas as pl
from jax.experimental.pallas import tpu as pltpu
from jax.sharding import Mesh
from jax.sharding import PartitionSpec as P

NS_STEPS = 6
BLOCK = 64
TILE = 16
ALL = ("narrow", "y", "z", "x")
PLANE = ("y", "z")
HIGHEST = lax.Precision.HIGHEST
ROW_DIMS = (((0,), (0,)), ((), ()))
SLOTS = 16
GRANT = pltpu.CompilerParams(vmem_limit_bytes=16 * 2**20)


def dot_f32(a, b, dims=(((1,), (0,)), ((), ()))):
    return lax.dot_general(a, b, dims, precision=HIGHEST, preferred_element_type=jnp.float32)


def split_two(a):
    high = a.astype(jnp.bfloat16)
    return high, (a - high.astype(jnp.float32)).astype(jnp.bfloat16)


def dot_split(a, b):
    (ah, al), (bh, bl) = a, b
    mul = functools.partial(jnp.dot, preferred_element_type=jnp.float32)
    return mul(ah, bh) + (mul(ah, bl) + mul(al, bh))


POWERS = (64, 32, 16, 8, 4)


def scaled(value):
    top = jnp.max(jnp.abs(value), axis=(0, 1), keepdims=True)
    factor, power = jnp.ones_like(top), jnp.zeros_like(top)
    for p in POWERS:
        large = top * factor >= 2.0 ** (11 + p)
        factor = jnp.where(large, factor * 2.0**-p, factor)
        power = jnp.where(large, power - p, power)
    for p in POWERS:
        small = top * factor < 2.0 ** (15 - p)
        factor = jnp.where(small, factor * 2.0**p, factor)
        power = jnp.where(small, power + p, power)
    return value * factor, power


def unscale_factor(power):
    factor = jnp.ones_like(power)
    for p in POWERS:
        up, down = power >= p, power <= -p
        factor = jnp.where(up, factor * 2.0**-p, jnp.where(down, factor * 2.0**p, factor))
        power = jnp.where(up, power - p, jnp.where(down, power + p, power))
    return factor


def spread_rows(rows, gram, extra, count):
    def leaf(value):
        flat, power = scaled(value.reshape(-1, value.shape[2]))
        shape = (value.shape[0], 1, value.shape[2])
        return flat.reshape(value.shape), jnp.broadcast_to(power[None], shape)

    pieces = list(leaf(rows))
    gram, gram_power = leaf(gram)
    for term in range(3):
        short = gram.astype(jnp.bfloat16).astype(jnp.float32)
        pieces.append(short)
        gram = gram - short
    pieces += [gram_power] + extra
    filled = sum(p.shape[1] for p in pieces)
    if filled < count:
        shape = (rows.shape[0], count - filled, rows.shape[2])
        pieces.append(jnp.zeros(shape, jnp.float32))
    return jnp.concatenate(pieces, axis=1)


def joined_gram(parts, start, pair):
    terms = [parts[:, start + t * pair : start + (t + 1) * pair, :] for t in range(3)]
    power = parts[:, start + 3 * pair : start + 3 * pair + 1, :]
    return (terms[0] + (terms[1] + terms[2])) * unscale_factor(power)


def invert_kernel(spot_ref, *refs):
    parts, inverse_ref, work_ref = refs[:-2], refs[-2], refs[-1]
    rank = inverse_ref.shape[0]
    height = rank // len(parts)
    row_ids = lax.broadcasted_iota(jnp.int32, (rank, rank), 0)
    col_ids = lax.broadcasted_iota(jnp.int32, (rank, rank), 1)
    for step, part_ref in enumerate(parts):
        place = lax.rem(spot_ref[0] + len(parts) - step, len(parts))
        work_ref[pl.ds(pl.multiple_of(place * height, height), height), :rank] = part_ref[...]
    work_ref[:, rank:] = (row_ids == col_ids).astype(jnp.float32)
    lane = lax.broadcasted_iota(jnp.int32, (BLOCK, 128), 1)
    row = lax.broadcasted_iota(jnp.int32, (BLOCK, 128), 0)
    panel_lane = lax.broadcasted_iota(jnp.int32, (BLOCK, rank), 1)

    def block_step(step, carry):
        start = pl.multiple_of(step * BLOCK, BLOCK)
        panel = work_ref[pl.ds(start, BLOCK), :]
        shifted = pltpu.roll(panel[:, :rank], rank - start, 1)[:, :128]
        rest = jnp.where(lane < BLOCK, shifted, (lane - BLOCK == row).astype(jnp.float32))
        done = []
        for tile in range(BLOCK // TILE):
            height = BLOCK - tile * TILE
            sub = lax.broadcasted_iota(jnp.int32, (height, 128), 0)
            columns = [
                jnp.broadcast_to(rest[:, tile * TILE + j : tile * TILE + j + 1], (height, 128))
                for j in range(TILE)
            ]
            for j in range(TILE):
                pivot = columns[j][j : j + 1, :]
                scale = lax.rsqrt(pivot)
                scale = scale * (1.5 - 0.5 * (pivot * scale) * scale)
                below = jnp.where(sub > j, columns[j] * scale, 0.0)
                lead = rest[j : j + 1, :] * scale
                done.append(lead)
                rest = rest - below * lead
                for m in range(j + 1, TILE):
                    columns[m] = columns[m] - below * (columns[m][j : j + 1, :] * scale)
            rest = rest[TILE:, :]
        solved = jnp.concatenate(done, axis=0)
        small = pltpu.roll(solved, 128 - BLOCK, 1)[:, :BLOCK]
        panel = dot_f32(small, panel)
        inverse_ref[pl.ds(start, BLOCK), :] = panel[:, rank:]
        later = jnp.where(panel_lane >= start + BLOCK, panel[:, :rank], 0.0)
        work_ref[...] -= dot_f32(later, panel, (((0,), (0,)), ((), ())))
        return carry

    lax.fori_loop(0, rank // BLOCK, block_step, 0)


def invert_factor(spot, parts):
    rank = parts[0].shape[1]
    return pl.pallas_call(
        invert_kernel,
        in_specs=[pl.BlockSpec(memory_space=pltpu.SMEM)]
        + [pl.BlockSpec(memory_space=pltpu.VMEM)] * len(parts),
        out_shape=jax.ShapeDtypeStruct((rank, rank), jnp.float32),
        scratch_shapes=[pltpu.VMEM((rank, 2 * rank), jnp.float32)],
        compiler_params=GRANT,
        cost_estimate=pl.CostEstimate(flops=20_000_000_000, bytes_accessed=524288, transcendentals=0),
        name="invert_factor",
    )(spot, *parts)


def moment_kernel(*refs):
    total = None
    for part_ref in refs[:-1]:
        high, low = split_two(plain_rows(part_ref))
        mul = functools.partial(
            lax.dot_general, dimension_numbers=ROW_DIMS, preferred_element_type=jnp.float32
        )
        mixed = mul(high, low)
        term = mul(high, high) + ((mixed + mixed.T) + mul(low, low))
        total = term if total is None else total + term
    refs[-1][...] = total


def moment_of(parts):
    rank = 2 * parts[0].shape[2]
    return pl.pallas_call(
        moment_kernel,
        out_shape=jax.ShapeDtypeStruct((rank, rank), jnp.float32),
        compiler_params=GRANT,
        cost_estimate=pl.CostEstimate(flops=4_000_000_000, bytes_accessed=2359296, transcendentals=0),
        name="moment_of",
    )(*parts)


def whiten_kernel(spot_ref, inverse_ref, moment_ref, other_ref, *refs):
    parts, out_ref = refs[:-1], refs[-1]
    inverse = inverse_ref[...]
    rank = inverse.shape[0]
    moment = moment_ref[...] + other_ref[...]
    cov_total = dot_f32(dot_f32(inverse, moment), inverse, (((1,), (1,)), ((), ())))
    row_ids = lax.broadcasted_iota(jnp.int32, (rank, rank), 0)
    col_ids = lax.broadcasted_iota(jnp.int32, (rank, rank), 1)
    eye_matrix = (row_ids == col_ids).astype(jnp.float32)
    trace_value = jnp.sum(cov_total * eye_matrix, axis=(0, 1), keepdims=True)
    left_iter = cov_total / trace_value
    right_iter = 1.5 * eye_matrix - 0.5 * left_iter
    right_parts = split_two(right_iter)
    left_parts = split_two(dot_split(split_two(left_iter), right_parts))
    for step_index in range(1, NS_STEPS):
        middle = split_two(1.5 * eye_matrix - 0.5 * dot_split(right_parts, left_parts))
        right_iter = dot_split(middle, right_parts)
        if step_index < NS_STEPS - 1:
            left_parts = split_two(dot_split(left_parts, middle))
            right_parts = split_two(right_iter)
    factor = right_iter / jnp.sqrt(trace_value)
    weight = split_two(dot_f32(inverse, factor, ROW_DIMS))
    height = out_ref.shape[0] // len(parts)
    for step, part_ref in enumerate(parts):
        place = lax.rem(spot_ref[0] + len(parts) - step, len(parts))
        rows = pl.ds(pl.multiple_of(place * height, height), height)
        out_ref[rows, :] = dot_split(split_two(plain_rows(part_ref)), weight).astype(jnp.bfloat16)


def project_half(spot, inverse, moment, other, parts):
    chunk, rank = parts[0].shape[0] * (parts[0].shape[1] - 8) // 2, inverse.shape[0]
    return pl.pallas_call(
        whiten_kernel,
        in_specs=[pl.BlockSpec(memory_space=pltpu.SMEM)]
        + [pl.BlockSpec(memory_space=pltpu.VMEM)] * (3 + len(parts)),
        out_shape=jax.ShapeDtypeStruct((chunk * len(parts), rank), jnp.bfloat16),
        compiler_params=GRANT,
        cost_estimate=pl.CostEstimate(flops=12_000_000_000, bytes_accessed=4194304, transcendentals=0),
        name="project_half",
    )(spot, inverse, moment, other, *parts)


def chunk_kernel(steps, spot_ref, rows_ref, sketch_ref, label_ref, *out_refs):
    core, here, line = (spot_ref[i] for i in range(3))
    rank = sketch_ref.shape[1]
    width = out_refs[0].shape[1] - 128
    half = rows_ref.shape[1] // 2
    sketch = sketch_ref[...]
    mul = functools.partial(
        lax.dot_general, dimension_numbers=ROW_DIMS, preferred_element_type=jnp.float32
    )
    gram_whole = mul(sketch, sketch)
    lane = lax.broadcasted_iota(jnp.int32, (rank, 128), 1)
    mine = pl.ds(pl.multiple_of((core * line + here) * SLOTS, SLOTS), SLOTS)
    for index, step in enumerate(steps):
        chunk = lax.rem(here + step, line)
        gram = pltpu.roll(gram_whole, rank - chunk * (rank * width // half), 1)[:, :128]
        gram = jnp.where(lane < rank * width // half, gram, 0.0)
        for out_ref, place in zip(out_refs[2 * index :], (1 - core, core)):
            columns = pl.ds(pl.multiple_of(place * half + chunk * width, width), width)
            out_ref[:, :width] = mul(sketch, rows_ref[:, columns])
            out_ref[:, width:] = gram
            theirs = pl.ds(pl.multiple_of((place * line + chunk) * SLOTS, SLOTS), SLOTS)
            out_ref[mine, width:] += label_ref[theirs, :]


def cross_chunks(spot, embeddings, sketch, labels, chunks, steps):
    count = len(steps)
    depth, dim = embeddings.shape
    rank = sketch.shape[1]
    width = dim // 2 // chunks
    shape = jax.ShapeDtypeStruct((rank, width + 128), jnp.float32)
    return pl.pallas_call(
        functools.partial(chunk_kernel, steps),
        in_specs=[pl.BlockSpec(memory_space=pltpu.SMEM)]
        + [pl.BlockSpec(memory_space=pltpu.VMEM)] * 3,
        out_shape=[shape] * (2 * count),
        compiler_params=GRANT,
        cost_estimate=pl.CostEstimate(
            flops=4 * depth * rank * width * count, bytes_accessed=3000000, transcendentals=0
        ),
        name="cross_chunks",
    )(spot, embeddings, sketch, labels)


def far_kernel(keep_ref, got_ref, *out_refs):
    height = out_refs[0].shape[0]
    for half in range(2):
        rows = slice(half * height, (half + 1) * height)
        total = keep_ref[rows, :] + got_ref[rows, :]
        body, power = scaled(total[:, :-128])
        out_refs[2 * half][...] = body
        tail = total[:, -128:]
        lane = lax.broadcasted_iota(jnp.int32, tail.shape, 1)
        out_refs[2 * half + 1][...] = jnp.where(lane == 127, power, tail)


def far_halves(keep, got):
    rank, width = keep.shape
    shapes = [
        jax.ShapeDtypeStruct((rank // 2, width - 128), jnp.float32),
        jax.ShapeDtypeStruct((rank // 2, 128), jnp.float32),
    ]
    a, a_tail, b, b_tail = pl.pallas_call(
        far_kernel,
        out_shape=shapes * 2,
        compiler_params=GRANT,
        cost_estimate=pl.CostEstimate(flops=400000, bytes_accessed=2000000, transcendentals=0),
        name="far_halves",
    )(keep, got)
    return (a.astype(jnp.float16), a_tail), (b.astype(jnp.float16), b_tail)


def join_kernel(side, keep_ref, got_ref, extra_ref, extra_tail_ref, body_ref, tail_ref):
    rank, width = body_ref.shape
    total = keep_ref[...] + got_ref[...]
    extra_tail = extra_tail_ref[...]
    extra = extra_ref[...] * unscale_factor(extra_tail[:1, 127:])
    extra = jnp.concatenate([extra, extra_tail], axis=1)
    extra = jnp.concatenate([extra, jnp.zeros_like(extra)][:: 1 - 2 * side], axis=0)
    total = total + extra
    body, power = scaled(total[:, :width])
    body_ref[...] = body
    tail = total[:, width:]
    row = lax.broadcasted_iota(jnp.int32, tail.shape, 0)
    lane = lax.broadcasted_iota(jnp.int32, tail.shape, 1)
    tail_ref[...] = jnp.where((row == rank - 1) & (lane >= 64), power, tail)


def join_chunk(keep, got, extra, side):
    rank, width = keep.shape
    body, tail = pl.pallas_call(
        functools.partial(join_kernel, side),
        out_shape=[
            jax.ShapeDtypeStruct((rank, width - 128), jnp.float32),
            jax.ShapeDtypeStruct((rank, 128), jnp.float32),
        ],
        compiler_params=GRANT,
        cost_estimate=pl.CostEstimate(flops=400000, bytes_accessed=2000000, transcendentals=0),
        name="join_chunk",
    )(keep, got, extra[0].astype(jnp.float32), extra[1])
    return body.astype(jnp.float16), tail


def line_kernel(gram_piece, *refs):
    first, second, out_ref = refs[0], refs[1], refs[-1]
    plane = out_ref.shape[0]
    total = first[...] + second[...]
    rank, width = total.shape[0], total.shape[1] - 128
    body, tail = total[:, :width], total[:, width:]
    for body_ref, tail_ref in zip(refs[2:-1:2], refs[3:-1:2]):
        more = tail_ref[...]
        body = body + body_ref[...] * unscale_factor(more[rank - 1 :, 127:])
        tail = tail + more
    piece = width // plane
    turned = body.T.reshape(plane, piece, rank)
    tail = tail.T.reshape(2, plane, gram_piece, rank)
    gram, labels = tail[0], tail[1][:, :1, :128].astype(jnp.int32)
    digits = [(labels % 1024).astype(jnp.float32), (labels // 1024).astype(jnp.float32)]
    out_ref[...] = spread_rows(
        jnp.concatenate([turned[:, :, :128], turned[:, :, 128:]], axis=1),
        jnp.concatenate([gram[:, :, :128], gram[:, :, 128:]], axis=1),
        digits,
        out_ref.shape[1],
    )


def line_total(parts, plane, gram_piece):
    width = parts[0].shape[1] - 128
    rows = 2 * (width // plane) + 6 * gram_piece + 4
    rows += -rows % 16
    return pl.pallas_call(
        functools.partial(line_kernel, gram_piece),
        out_shape=jax.ShapeDtypeStruct((plane, rows, 128), jnp.float32),
        compiler_params=GRANT,
        cost_estimate=pl.CostEstimate(flops=1000000, bytes_accessed=4000000, transcendentals=0),
        name="line_total",
    )(*parts)


def plane_kernel(piece, gram_piece, parts_ref, out_ref, label_ref):
    cut, pair = 2 * piece, 2 * gram_piece
    parts = parts_ref[...]
    rows = jnp.sum(parts[:, :cut, :] * unscale_factor(parts[:, cut : cut + 1, :]), axis=0)
    gram = jnp.sum(joined_gram(parts, cut + 1, pair), axis=0)
    out_ref[...] = spread_rows(rows[None], gram[None], [], out_ref.shape[0])[0]
    end = cut + 2 + 3 * pair
    labels = parts[:, end, :] + 1024.0 * parts[:, end + 1, :]
    label_ref[...] = labels.astype(jnp.int32) - 1


def plane_total(parts, piece, gram_piece):
    plane, _, lanes = parts.shape
    rows = 2 * piece + 6 * gram_piece + 2
    rows += -rows % 16
    return pl.pallas_call(
        functools.partial(plane_kernel, piece, gram_piece),
        out_shape=[
            jax.ShapeDtypeStruct((rows, lanes), jnp.float32),
            jax.ShapeDtypeStruct((plane, lanes), jnp.int32),
        ],
        compiler_params=GRANT,
        cost_estimate=pl.CostEstimate(flops=1000000, bytes_accessed=1600000, transcendentals=0),
        name="plane_total",
    )(parts)


def plain_rows(part_ref):
    part = part_ref[...]
    cut = part.shape[1] - 8
    return whole_rows(part[:, :cut] * unscale_factor(part[:, cut : cut + 1]))


def whole_rows(part):
    plane, pair, lanes = part.shape
    sides = [part[:, : pair // 2], part[:, pair // 2 :]]
    return jnp.concatenate([t.reshape(plane * pair // 2, lanes) for t in sides], axis=1)


def gram_kernel(parts_ref, out_ref):
    pair = 2 * out_ref.shape[0] // parts_ref.shape[0]
    out_ref[...] = whole_rows(joined_gram(parts_ref[...], 1, pair))


def gram_rows(parts, gram_piece):
    plane, _, lanes = parts.shape
    return pl.pallas_call(
        gram_kernel,
        out_shape=jax.ShapeDtypeStruct((plane * gram_piece, 2 * lanes), jnp.float32),
        compiler_params=GRANT,
        cost_estimate=pl.CostEstimate(flops=10000, bytes_accessed=200000, transcendentals=0),
        name="gram_rows",
    )(parts)


def product_kernel(own, core_ref, rows_ref, basis_ref, *refs):
    place = core_ref[0] if own else 1 - core_ref[0]
    half, width = basis_ref.shape[0], 512
    total = None if len(refs) == 1 else refs[0][...]
    for step in range(half // width):
        columns = pl.ds(pl.multiple_of(place * half + step * width, width), width)
        basis = basis_ref[step * width : (step + 1) * width, :]
        term = jnp.dot(rows_ref[:, columns], basis, preferred_element_type=jnp.float32)
        total = term if total is None else total + term
    refs[-1][...] = total.astype(refs[-1].dtype)


def product_of_half(core, own, embeddings, basis, begin, out_type):
    depth, dim = embeddings.shape
    rank = basis.shape[1]
    extra = [] if begin is None else [begin]
    return pl.pallas_call(
        functools.partial(product_kernel, own),
        in_specs=[pl.BlockSpec(memory_space=pltpu.SMEM)]
        + [pl.BlockSpec(memory_space=pltpu.VMEM)] * (2 + len(extra)),
        out_shape=jax.ShapeDtypeStruct((depth, rank), out_type),
        compiler_params=GRANT,
        cost_estimate=pl.CostEstimate(
            flops=depth * dim * rank, bytes_accessed=depth * dim + dim * rank, transcendentals=0
        ),
        name="product_of_half",
    )(core, embeddings, basis, *extra)


def route_kernel(capacity, line, plane, ids_ref, map_ref, dest_ref, label_ref):
    ids = jnp.concatenate([ids_ref[k : k + 1, :] for k in range(ids_ref.shape[0])], axis=1)
    count, (high, low) = ids.shape[1], map_ref.shape
    owner_count = 2 * plane * line
    bf16 = jnp.bfloat16

    def rows_of(size):
        return lax.broadcasted_iota(jnp.int32, (size, count), 0)

    picked = (rows_of(high) == ids // low).astype(bf16)
    found = lax.dot_general(
        map_ref[...].astype(bf16), picked, ROW_DIMS, preferred_element_type=jnp.float32
    )
    owner = jnp.sum(jnp.where(rows_of(low) == ids % low, found, 0.0), axis=0, keepdims=True)
    owner = owner.astype(jnp.int32)
    mine = rows_of(owner_count) == owner
    order = lax.broadcasted_iota(jnp.int32, (count, count), 1)
    earlier = (lax.broadcasted_iota(jnp.int32, (count, count), 0) < order).astype(bf16)
    before = jnp.dot(mine.astype(bf16), earlier, preferred_element_type=jnp.float32)
    slot = jnp.sum(jnp.where(mine, before, 0.0), axis=0, keepdims=True).astype(jnp.int32)
    dest_ref[...] = owner * capacity + slot
    value = ids + 1
    core, chip = owner // (plane * line), owner % (plane * line)
    row = (core * line + chip % line) * SLOTS + slot
    lane = rows_of(128) == 64 + 2 * (chip // line)
    lane = lane.astype(bf16)
    labels = None
    for digit in range(3):
        short = (value // 128**digit) % 128
        spread = jnp.where(rows_of(2 * line * SLOTS) == row, short.astype(jnp.float32), 0.0)
        term = lax.dot_general(
            spread.astype(bf16),
            lane,
            (((1,), (1,)), ((), ())),
            preferred_element_type=jnp.float32,
        )
        labels = term if labels is None else labels + term * 128**digit
    label_ref[...] = labels


def route_rows(list_ids, owner_map, capacity, line, plane):
    count = list_ids.shape[0]
    return pl.pallas_call(
        functools.partial(route_kernel, capacity, line, plane),
        out_shape=[
            jax.ShapeDtypeStruct((1, count), jnp.int32),
            jax.ShapeDtypeStruct((2 * line * SLOTS, 128), jnp.float32),
        ],
        compiler_params=GRANT,
        cost_estimate=pl.CostEstimate(
            flops=2_000_000_000, bytes_accessed=1048576, transcendentals=0
        ),
        name="route_rows",
    )(list_ids.reshape(-1, 128), owner_map.reshape(-1, 128))


def place_kernel(capacity, core_ref, own_target, other_target, own_ref, other_ref, out_ref):
    pairs, _, width = out_ref.shape
    count = pairs * 2 * capacity
    slots = pl.program_id(0) * count + lax.broadcasted_iota(
        jnp.int32, (count, own_ref.shape[0]), 0
    )
    found = []
    for target_ref, rows_ref in ((own_target, own_ref), (other_target, other_ref)):
        onehot = (slots == target_ref[...]).astype(jnp.bfloat16)
        term = jnp.dot(onehot, rows_ref[...], preferred_element_type=jnp.float32)
        found.append(term.reshape(pairs, 2 * capacity, width))
    first = core_ref[0] == 0
    a = jnp.where(first, found[0], found[1])
    b = jnp.where(first, found[1], found[0])
    out_ref[...] = jnp.concatenate(
        [a[:, :capacity], b[:, :capacity], a[:, capacity:], b[:, capacity:]], axis=1
    ).astype(jnp.bfloat16)


def place_rows(core, targets, own, other, chips, capacity):
    pairs = 32
    depth, width = own.shape
    return pl.pallas_call(
        functools.partial(place_kernel, capacity),
        grid=(chips // 2 // pairs,),
        in_specs=[pl.BlockSpec(memory_space=pltpu.SMEM)]
        + [pl.BlockSpec((1, depth), lambda i: (0, 0))] * 2
        + [pl.BlockSpec((depth, width), lambda i: (0, 0))] * 2,
        out_specs=pl.BlockSpec((pairs, 4 * capacity, width), lambda i: (i, 0, 0)),
        out_shape=jax.ShapeDtypeStruct((chips // 2, 4 * capacity, width), jnp.bfloat16),
        compiler_params=GRANT,
        cost_estimate=pl.CostEstimate(
            flops=4 * chips * capacity * depth * width,
            bytes_accessed=8 * chips * capacity * width,
            transcendentals=0,
        ),
        name="place_rows",
    )(core, *targets, own, other)


def shift(value, axis, step):
    size = lax.axis_size(axis)
    return lax.ppermute(value, axis, [(i, (i + step) % size) for i in range(size)])


def local(embeddings, sketch_seed, list_ids, owner_map):
    row_count, dim = embeddings.shape
    rank = sketch_seed.shape[1]
    cores, line = lax.axis_size("narrow"), lax.axis_size("x")
    plane = lax.axis_size("y") * lax.axis_size("z")
    chips = plane * line
    dev_count = cores * chips
    core = lax.axis_index("narrow")
    spot = lax.axis_index("x").reshape(1)
    piece, gram_piece = dim // dev_count, rank // chips
    seed_matrix = sketch_seed.astype(jnp.bfloat16)
    sketch = jnp.dot(embeddings, seed_matrix, preferred_element_type=jnp.float32).astype(
        jnp.bfloat16
    )

    capacity = 4 * row_count // dev_count
    here = lax.axis_index("x")
    dest_index, labels = route_rows(list_ids, owner_map, capacity, line, plane)

    spots = jnp.stack([core, here, jnp.int32(line)])

    def chunks_at(*steps):
        pairs = cross_chunks(spots, embeddings, sketch, labels, line, steps)
        return [(pairs[2 * i + 1], shift(pairs[2 * i], "narrow", 1)) for i in range(len(steps))]

    (far,) = chunks_at(2)
    up, down, near = chunks_at(1, 3, 0)
    first, last = far_halves(*far)
    from_below = [shift(part, "x", 1) for part in first]
    from_above = [shift(part, "x", line - 1) for part in last]
    from_below = [shift(part, "x", 1) for part in join_chunk(*up, from_below, 0)]
    from_above = [shift(part, "x", line - 1) for part in join_chunk(*down, from_above, 1)]
    arrived = [part.astype(jnp.float32) for part in from_below + from_above]

    def target_of(dest):
        owner = dest // capacity
        return jnp.where(owner // chips == core, (owner % chips) * capacity + dest % capacity, -1)

    targets = target_of(dest_index), target_of(shift(dest_index, "narrow", 1))

    packed = line_total([*near, *arrived], plane, gram_piece)
    packed, targets = lax.optimization_barrier((packed, targets))
    packed = lax.all_to_all(packed.astype(jnp.float16), PLANE, 0, 0, tiled=True)
    packed = packed.astype(jnp.float32)
    packed, arrived_labels = plane_total(packed, piece, gram_piece)
    packed = jnp.broadcast_to(packed.astype(jnp.float16)[None], (plane,) + packed.shape)
    packed = lax.all_to_all(packed, PLANE, 0, 0, tiled=True)
    gram_line = gram_rows(packed[:, 2 * piece :].astype(jnp.float32), gram_piece)
    packed, gram_line = lax.optimization_barrier((packed, gram_line))
    gram_parts = [gram_line] + [shift(gram_line, "x", step) for step in range(1, line)]
    cross_line = packed[:, : 2 * piece + 8]
    cross_parts = [cross_line] + [shift(cross_line, "x", step) for step in range(1, line)]
    cross_parts = [part.astype(jnp.float32) for part in cross_parts]
    arrived_labels = arrived_labels[:, : cores * line * SLOTS].reshape(plane, cores, line, SLOTS)
    arrived_labels = arrived_labels[..., :capacity].transpose(1, 0, 2, 3)

    inverse = invert_factor(spot, gram_parts)
    inverse, cross_parts = lax.optimization_barrier((inverse, cross_parts))
    moment = moment_of(cross_parts)
    basis = project_half(spot, inverse, moment, shift(moment, "narrow", 1), cross_parts)
    other_basis = shift(basis, "narrow", 1)
    begun = product_of_half(spots, True, embeddings, basis, None, jnp.float32)
    reduced = product_of_half(spots, False, embeddings, other_basis, begun, jnp.bfloat16)
    other = shift(reduced, "narrow", 1)
    send_rows = place_rows(spots, targets, reduced, other, chips, capacity)
    send_rows = send_rows.reshape(chips, cores * capacity, rank)
    arrived = lax.all_to_all(send_rows, ("y", "z", "x"), 0, 0, tiled=True)
    arrived = arrived.reshape(chips, cores, capacity, rank).transpose(1, 0, 2, 3)
    return (
        arrived.reshape(1, dev_count, capacity, rank),
        arrived_labels.reshape(1, dev_count, capacity),
    )


def solution(mesh):
    grid = Mesh(mesh.devices.reshape(2, 4, 8, 4), ALL)
    in_specs = (P(ALL, None), P(), P(ALL), P())
    out_specs = (P(ALL, None, None, None), P(ALL, None, None))
    return jax.shard_map(local, mesh=grid, in_specs=in_specs, out_specs=out_specs, check_vma=False)
```

```python
import functools

import jax
import jax.numpy as jnp
from jax import lax
from jax.experimental import pallas as pl
from jax.experimental.pallas import tpu as pltpu
from jax.sharding import Mesh
from jax.sharding import PartitionSpec as P

NS_STEPS = 6
BLOCK = 64
TILE = 16
ALL = ("narrow", "y", "z", "x")
PLANE = ("y", "z")
HIGHEST = lax.Precision.HIGHEST
ROW_DIMS = (((0,), (0,)), ((), ()))
SLOTS = 16
GRANT = pltpu.CompilerParams(vmem_limit_bytes=16 * 2**20)


def dot_f32(a, b, dims=(((1,), (0,)), ((), ()))):
    return lax.dot_general(a, b, dims, precision=HIGHEST, preferred_element_type=jnp.float32)


def split_two(a):
    high = a.astype(jnp.bfloat16)
    return high, (a - high.astype(jnp.float32)).astype(jnp.bfloat16)


def dot_split(a, b):
    (ah, al), (bh, bl) = a, b
    mul = functools.partial(jnp.dot, preferred_element_type=jnp.float32)
    return mul(ah, bh) + (mul(ah, bl) + mul(al, bh))


POWERS = (64, 32, 16, 8, 4)


def scaled(value):
    top = jnp.max(jnp.abs(value), axis=(0, 1), keepdims=True)
    factor, power = jnp.ones_like(top), jnp.zeros_like(top)
    for p in POWERS:
        large = top * factor >= 2.0 ** (11 + p)
        factor = jnp.where(large, factor * 2.0**-p, factor)
        power = jnp.where(large, power - p, power)
    for p in POWERS:
        small = top * factor < 2.0 ** (15 - p)
        factor = jnp.where(small, factor * 2.0**p, factor)
        power = jnp.where(small, power + p, power)
    return value * factor, power


def unscale_factor(power):
    factor = jnp.ones_like(power)
    for p in POWERS:
        up, down = power >= p, power <= -p
        factor = jnp.where(up, factor * 2.0**-p, jnp.where(down, factor * 2.0**p, factor))
        power = jnp.where(up, power - p, jnp.where(down, power + p, power))
    return factor


def spread_rows(rows, gram, extra, count):
    def leaf(value):
        flat, power = scaled(value.reshape(-1, value.shape[2]))
        shape = (value.shape[0], 1, value.shape[2])
        return flat.reshape(value.shape), jnp.broadcast_to(power[None], shape)

    pieces = list(leaf(rows))
    gram, gram_power = leaf(gram)
    for term in range(3):
        short = gram.astype(jnp.bfloat16).astype(jnp.float32)
        pieces.append(short)
        gram = gram - short
    pieces += [gram_power] + extra
    filled = sum(p.shape[1] for p in pieces)
    if filled < count:
        shape = (rows.shape[0], count - filled, rows.shape[2])
        pieces.append(jnp.zeros(shape, jnp.float32))
    return jnp.concatenate(pieces, axis=1)


def joined_gram(parts, start, pair):
    terms = [parts[:, start + t * pair : start + (t + 1) * pair, :] for t in range(3)]
    power = parts[:, start + 3 * pair : start + 3 * pair + 1, :]
    return (terms[0] + (terms[1] + terms[2])) * unscale_factor(power)


def invert_kernel(spot_ref, *refs):
    parts, inverse_ref, work_ref = refs[:-2], refs[-2], refs[-1]
    rank = inverse_ref.shape[0]
    height = rank // len(parts)
    row_ids = lax.broadcasted_iota(jnp.int32, (rank, rank), 0)
    col_ids = lax.broadcasted_iota(jnp.int32, (rank, rank), 1)
    for step, part_ref in enumerate(parts):
        place = lax.rem(spot_ref[0] + len(parts) - step, len(parts))
        work_ref[pl.ds(pl.multiple_of(place * height, height), height), :rank] = part_ref[...]
    work_ref[:, rank:] = (row_ids == col_ids).astype(jnp.float32)
    lane = lax.broadcasted_iota(jnp.int32, (BLOCK, 128), 1)
    row = lax.broadcasted_iota(jnp.int32, (BLOCK, 128), 0)
    panel_lane = lax.broadcasted_iota(jnp.int32, (BLOCK, rank), 1)

    def block_step(step, carry):
        start = pl.multiple_of(step * BLOCK, BLOCK)
        panel = work_ref[pl.ds(start, BLOCK), :]
        shifted = pltpu.roll(panel[:, :rank], rank - start, 1)[:, :128]
        rest = jnp.where(lane < BLOCK, shifted, (lane - BLOCK == row).astype(jnp.float32))
        done = []
        for tile in range(BLOCK // TILE):
            height = BLOCK - tile * TILE
            sub = lax.broadcasted_iota(jnp.int32, (height, 128), 0)
            columns = [
                jnp.broadcast_to(rest[:, tile * TILE + j : tile * TILE + j + 1], (height, 128))
                for j in range(TILE)
            ]
            for j in range(TILE):
                pivot = columns[j][j : j + 1, :]
                scale = lax.rsqrt(pivot)
                scale = scale * (1.5 - 0.5 * (pivot * scale) * scale)
                below = jnp.where(sub > j, columns[j] * scale, 0.0)
                lead = rest[j : j + 1, :] * scale
                done.append(lead)
                rest = rest - below * lead
                for m in range(j + 1, TILE):
                    columns[m] = columns[m] - below * (columns[m][j : j + 1, :] * scale)
            rest = rest[TILE:, :]
        solved = jnp.concatenate(done, axis=0)
        small = pltpu.roll(solved, 128 - BLOCK, 1)[:, :BLOCK]
        panel = dot_f32(small, panel)
        inverse_ref[pl.ds(start, BLOCK), :] = panel[:, rank:]
        later = jnp.where(panel_lane >= start + BLOCK, panel[:, :rank], 0.0)
        work_ref[...] -= dot_f32(later, panel, (((0,), (0,)), ((), ())))
        return carry

    lax.fori_loop(0, rank // BLOCK, block_step, 0)


def invert_factor(spot, parts):
    rank = parts[0].shape[1]
    return pl.pallas_call(
        invert_kernel,
        in_specs=[pl.BlockSpec(memory_space=pltpu.SMEM)]
        + [pl.BlockSpec(memory_space=pltpu.VMEM)] * len(parts),
        out_shape=jax.ShapeDtypeStruct((rank, rank), jnp.float32),
        scratch_shapes=[pltpu.VMEM((rank, 2 * rank), jnp.float32)],
        compiler_params=GRANT,
        cost_estimate=pl.CostEstimate(flops=20_000_000_000, bytes_accessed=524288, transcendentals=0),
        name="invert_factor",
    )(spot, *parts)


def moment_kernel(*refs):
    total = None
    for part_ref in refs[:-1]:
        high, low = split_two(plain_rows(part_ref))
        mul = functools.partial(
            lax.dot_general, dimension_numbers=ROW_DIMS, preferred_element_type=jnp.float32
        )
        mixed = mul(high, low)
        term = mul(high, high) + ((mixed + mixed.T) + mul(low, low))
        total = term if total is None else total + term
    refs[-1][...] = total


def moment_of(parts):
    rank = 2 * parts[0].shape[2]
    return pl.pallas_call(
        moment_kernel,
        out_shape=jax.ShapeDtypeStruct((rank, rank), jnp.float32),
        compiler_params=GRANT,
        cost_estimate=pl.CostEstimate(flops=4_000_000_000, bytes_accessed=2359296, transcendentals=0),
        name="moment_of",
    )(*parts)


def whiten_kernel(spot_ref, inverse_ref, moment_ref, other_ref, *refs):
    parts, out_ref = refs[:-1], refs[-1]
    inverse = inverse_ref[...]
    rank = inverse.shape[0]
    moment = moment_ref[...] + other_ref[...]
    cov_total = dot_f32(dot_f32(inverse, moment), inverse, (((1,), (1,)), ((), ())))
    row_ids = lax.broadcasted_iota(jnp.int32, (rank, rank), 0)
    col_ids = lax.broadcasted_iota(jnp.int32, (rank, rank), 1)
    eye_matrix = (row_ids == col_ids).astype(jnp.float32)
    trace_value = jnp.sum(cov_total * eye_matrix, axis=(0, 1), keepdims=True)
    left_iter = cov_total / trace_value
    right_iter = 1.5 * eye_matrix - 0.5 * left_iter
    right_parts = split_two(right_iter)
    left_parts = split_two(dot_split(split_two(left_iter), right_parts))
    for step_index in range(1, NS_STEPS):
        middle = split_two(1.5 * eye_matrix - 0.5 * dot_split(right_parts, left_parts))
        right_iter = dot_split(middle, right_parts)
        if step_index < NS_STEPS - 1:
            left_parts = split_two(dot_split(left_parts, middle))
            right_parts = split_two(right_iter)
    factor = right_iter / jnp.sqrt(trace_value)
    weight = split_two(dot_f32(inverse, factor, ROW_DIMS))
    height = out_ref.shape[0] // len(parts)
    for step, part_ref in enumerate(parts):
        place = lax.rem(spot_ref[0] + len(parts) - step, len(parts))
        rows = pl.ds(pl.multiple_of(place * height, height), height)
        out_ref[rows, :] = dot_split(split_two(plain_rows(part_ref)), weight).astype(jnp.bfloat16)


def project_half(spot, inverse, moment, other, parts):
    chunk, rank = parts[0].shape[0] * (parts[0].shape[1] - 8) // 2, inverse.shape[0]
    return pl.pallas_call(
        whiten_kernel,
        in_specs=[pl.BlockSpec(memory_space=pltpu.SMEM)]
        + [pl.BlockSpec(memory_space=pltpu.VMEM)] * (3 + len(parts)),
        out_shape=jax.ShapeDtypeStruct((chunk * len(parts), rank), jnp.bfloat16),
        compiler_params=GRANT,
        cost_estimate=pl.CostEstimate(flops=12_000_000_000, bytes_accessed=4194304, transcendentals=0),
        name="project_half",
    )(spot, inverse, moment, other, *parts)


def chunk_kernel(steps, spot_ref, rows_ref, sketch_ref, label_ref, *out_refs):
    core, here, line = (spot_ref[i] for i in range(3))
    rank = sketch_ref.shape[1]
    width = out_refs[0].shape[1] - 128
    half = rows_ref.shape[1] // 2
    sketch = sketch_ref[...]
    mul = functools.partial(
        lax.dot_general, dimension_numbers=ROW_DIMS, preferred_element_type=jnp.float32
    )
    gram_whole = mul(sketch, sketch)
    lane = lax.broadcasted_iota(jnp.int32, (rank, 128), 1)
    mine = pl.ds(pl.multiple_of((core * line + here) * SLOTS, SLOTS), SLOTS)
    for index, step in enumerate(steps):
        chunk = lax.rem(here + step, line)
        gram = pltpu.roll(gram_whole, rank - chunk * (rank * width // half), 1)[:, :128]
        gram = jnp.where(lane < rank * width // half, gram, 0.0)
        for out_ref, place in zip(out_refs[2 * index :], (1 - core, core)):
            columns = pl.ds(pl.multiple_of(place * half + chunk * width, width), width)
            out_ref[:, :width] = mul(sketch, rows_ref[:, columns])
            out_ref[:, width:] = gram
            theirs = pl.ds(pl.multiple_of((place * line + chunk) * SLOTS, SLOTS), SLOTS)
            out_ref[mine, width:] += label_ref[theirs, :]


def cross_chunks(spot, embeddings, sketch, labels, chunks, steps):
    count = len(steps)
    depth, dim = embeddings.shape
    rank = sketch.shape[1]
    width = dim // 2 // chunks
    shape = jax.ShapeDtypeStruct((rank, width + 128), jnp.float32)
    return pl.pallas_call(
        functools.partial(chunk_kernel, steps),
        in_specs=[pl.BlockSpec(memory_space=pltpu.SMEM)]
        + [pl.BlockSpec(memory_space=pltpu.VMEM)] * 3,
        out_shape=[shape] * (2 * count),
        compiler_params=GRANT,
        cost_estimate=pl.CostEstimate(
            flops=4 * depth * rank * width * count, bytes_accessed=3000000, transcendentals=0
        ),
        name="cross_chunks",
    )(spot, embeddings, sketch, labels)


def join_kernel(side, keep_ref, got_ref, extra_ref, body_ref, tail_ref):
    rank, width = body_ref.shape
    total = keep_ref[...] + got_ref[...]
    extra = jnp.concatenate(
        [extra_ref[...], jnp.zeros_like(extra_ref)][:: 1 - 2 * side], axis=0
    )
    total = total + extra
    body, power = scaled(total[:, :width])
    body_ref[...] = body
    tail = total[:, width:]
    row = lax.broadcasted_iota(jnp.int32, tail.shape, 0)
    lane = lax.broadcasted_iota(jnp.int32, tail.shape, 1)
    tail_ref[...] = jnp.where((row == rank - 1) & (lane >= 64), power, tail)


def join_chunk(keep, got, extra, side):
    rank, width = keep.shape
    body, tail = pl.pallas_call(
        functools.partial(join_kernel, side),
        out_shape=[
            jax.ShapeDtypeStruct((rank, width - 128), jnp.float32),
            jax.ShapeDtypeStruct((rank, 128), jnp.float32),
        ],
        compiler_params=GRANT,
        cost_estimate=pl.CostEstimate(flops=400000, bytes_accessed=2000000, transcendentals=0),
        name="join_chunk",
    )(keep, got, extra)
    return body.astype(jnp.float16), tail


def line_kernel(gram_piece, *refs):
    first, second, out_ref = refs[0], refs[1], refs[-1]
    plane = out_ref.shape[0]
    total = first[...] + second[...]
    rank, width = total.shape[0], total.shape[1] - 128
    body, tail = total[:, :width], total[:, width:]
    for body_ref, tail_ref in zip(refs[2:-1:2], refs[3:-1:2]):
        more = tail_ref[...]
        body = body + body_ref[...] * unscale_factor(more[rank - 1 :, 127:])
        tail = tail + more
    piece = width // plane
    turned = body.T.reshape(plane, piece, rank)
    tail = tail.T.reshape(2, plane, gram_piece, rank)
    gram, labels = tail[0], tail[1][:, :1, :128].astype(jnp.int32)
    digits = [(labels % 1024).astype(jnp.float32), (labels // 1024).astype(jnp.float32)]
    out_ref[...] = spread_rows(
        jnp.concatenate([turned[:, :, :128], turned[:, :, 128:]], axis=1),
        jnp.concatenate([gram[:, :, :128], gram[:, :, 128:]], axis=1),
        digits,
        out_ref.shape[1],
    )


def line_total(parts, plane, gram_piece):
    width = parts[0].shape[1] - 128
    rows = 2 * (width // plane) + 6 * gram_piece + 4
    rows += -rows % 16
    return pl.pallas_call(
        functools.partial(line_kernel, gram_piece),
        out_shape=jax.ShapeDtypeStruct((plane, rows, 128), jnp.float32),
        compiler_params=GRANT,
        cost_estimate=pl.CostEstimate(flops=1000000, bytes_accessed=4000000, transcendentals=0),
        name="line_total",
    )(*parts)


def plane_kernel(piece, gram_piece, parts_ref, out_ref, label_ref):
    cut, pair = 2 * piece, 2 * gram_piece
    parts = parts_ref[...]
    rows = jnp.sum(parts[:, :cut, :] * unscale_factor(parts[:, cut : cut + 1, :]), axis=0)
    gram = jnp.sum(joined_gram(parts, cut + 1, pair), axis=0)
    out_ref[...] = spread_rows(rows[None], gram[None], [], out_ref.shape[0])[0]
    end = cut + 2 + 3 * pair
    labels = parts[:, end, :] + 1024.0 * parts[:, end + 1, :]
    label_ref[...] = labels.astype(jnp.int32) - 1


def plane_total(parts, piece, gram_piece):
    plane, _, lanes = parts.shape
    rows = 2 * piece + 6 * gram_piece + 2
    rows += -rows % 16
    return pl.pallas_call(
        functools.partial(plane_kernel, piece, gram_piece),
        out_shape=[
            jax.ShapeDtypeStruct((rows, lanes), jnp.float32),
            jax.ShapeDtypeStruct((plane, lanes), jnp.int32),
        ],
        compiler_params=GRANT,
        cost_estimate=pl.CostEstimate(flops=1000000, bytes_accessed=1600000, transcendentals=0),
        name="plane_total",
    )(parts)


def plain_rows(part_ref):
    part = part_ref[...]
    cut = part.shape[1] - 8
    return whole_rows(part[:, :cut] * unscale_factor(part[:, cut : cut + 1]))


def whole_rows(part):
    plane, pair, lanes = part.shape
    sides = [part[:, : pair // 2], part[:, pair // 2 :]]
    return jnp.concatenate([t.reshape(plane * pair // 2, lanes) for t in sides], axis=1)


def gram_kernel(parts_ref, out_ref):
    pair = 2 * out_ref.shape[0] // parts_ref.shape[0]
    out_ref[...] = whole_rows(joined_gram(parts_ref[...], 1, pair))


def gram_rows(parts, gram_piece):
    plane, _, lanes = parts.shape
    return pl.pallas_call(
        gram_kernel,
        out_shape=jax.ShapeDtypeStruct((plane * gram_piece, 2 * lanes), jnp.float32),
        compiler_params=GRANT,
        cost_estimate=pl.CostEstimate(flops=10000, bytes_accessed=200000, transcendentals=0),
        name="gram_rows",
    )(parts)


def product_kernel(own, core_ref, rows_ref, basis_ref, *refs):
    place = core_ref[0] if own else 1 - core_ref[0]
    half, width = basis_ref.shape[0], 512
    total = None if len(refs) == 1 else refs[0][...]
    for step in range(half // width):
        columns = pl.ds(pl.multiple_of(place * half + step * width, width), width)
        basis = basis_ref[step * width : (step + 1) * width, :]
        term = jnp.dot(rows_ref[:, columns], basis, preferred_element_type=jnp.float32)
        total = term if total is None else total + term
    refs[-1][...] = total.astype(refs[-1].dtype)


def product_of_half(core, own, embeddings, basis, begin, out_type):
    depth, dim = embeddings.shape
    rank = basis.shape[1]
    extra = [] if begin is None else [begin]
    return pl.pallas_call(
        functools.partial(product_kernel, own),
        in_specs=[pl.BlockSpec(memory_space=pltpu.SMEM)]
        + [pl.BlockSpec(memory_space=pltpu.VMEM)] * (2 + len(extra)),
        out_shape=jax.ShapeDtypeStruct((depth, rank), out_type),
        compiler_params=GRANT,
        cost_estimate=pl.CostEstimate(
            flops=depth * dim * rank, bytes_accessed=depth * dim + dim * rank, transcendentals=0
        ),
        name="product_of_half",
    )(core, embeddings, basis, *extra)


def route_kernel(capacity, line, plane, ids_ref, map_ref, dest_ref, label_ref):
    ids = jnp.concatenate([ids_ref[k : k + 1, :] for k in range(ids_ref.shape[0])], axis=1)
    count, (high, low) = ids.shape[1], map_ref.shape
    owner_count = 2 * plane * line
    bf16 = jnp.bfloat16

    def rows_of(size):
        return lax.broadcasted_iota(jnp.int32, (size, count), 0)

    picked = (rows_of(high) == ids // low).astype(bf16)
    found = lax.dot_general(
        map_ref[...].astype(bf16), picked, ROW_DIMS, preferred_element_type=jnp.float32
    )
    owner = jnp.sum(jnp.where(rows_of(low) == ids % low, found, 0.0), axis=0, keepdims=True)
    owner = owner.astype(jnp.int32)
    mine = rows_of(owner_count) == owner
    order = lax.broadcasted_iota(jnp.int32, (count, count), 1)
    earlier = (lax.broadcasted_iota(jnp.int32, (count, count), 0) < order).astype(bf16)
    before = jnp.dot(mine.astype(bf16), earlier, preferred_element_type=jnp.float32)
    slot = jnp.sum(jnp.where(mine, before, 0.0), axis=0, keepdims=True).astype(jnp.int32)
    dest_ref[...] = owner * capacity + slot
    value = ids + 1
    core, chip = owner // (plane * line), owner % (plane * line)
    row = (core * line + chip % line) * SLOTS + slot
    lane = rows_of(128) == 64 + 2 * (chip // line)
    lane = lane.astype(bf16)
    labels = None
    for digit in range(3):
        short = (value // 128**digit) % 128
        spread = jnp.where(rows_of(2 * line * SLOTS) == row, short.astype(jnp.float32), 0.0)
        term = lax.dot_general(
            spread.astype(bf16),
            lane,
            (((1,), (1,)), ((), ())),
            preferred_element_type=jnp.float32,
        )
        labels = term if labels is None else labels + term * 128**digit
    label_ref[...] = labels


def route_rows(list_ids, owner_map, capacity, line, plane):
    count = list_ids.shape[0]
    return pl.pallas_call(
        functools.partial(route_kernel, capacity, line, plane),
        out_shape=[
            jax.ShapeDtypeStruct((1, count), jnp.int32),
            jax.ShapeDtypeStruct((2 * line * SLOTS, 128), jnp.float32),
        ],
        compiler_params=GRANT,
        cost_estimate=pl.CostEstimate(
            flops=2_000_000_000, bytes_accessed=1048576, transcendentals=0
        ),
        name="route_rows",
    )(list_ids.reshape(-1, 128), owner_map.reshape(-1, 128))


def place_kernel(capacity, core_ref, own_target, other_target, own_ref, other_ref, out_ref):
    pairs, _, width = out_ref.shape
    count = pairs * 2 * capacity
    slots = pl.program_id(0) * count + lax.broadcasted_iota(
        jnp.int32, (count, own_ref.shape[0]), 0
    )
    found = []
    for target_ref, rows_ref in ((own_target, own_ref), (other_target, other_ref)):
        onehot = (slots == target_ref[...]).astype(jnp.bfloat16)
        term = jnp.dot(onehot, rows_ref[...], preferred_element_type=jnp.float32)
        found.append(term.reshape(pairs, 2 * capacity, width))
    first = core_ref[0] == 0
    a = jnp.where(first, found[0], found[1])
    b = jnp.where(first, found[1], found[0])
    out_ref[...] = jnp.concatenate(
        [a[:, :capacity], b[:, :capacity], a[:, capacity:], b[:, capacity:]], axis=1
    ).astype(jnp.bfloat16)


def place_rows(core, targets, own, other, chips, capacity):
    pairs = 32
    depth, width = own.shape
    return pl.pallas_call(
        functools.partial(place_kernel, capacity),
        grid=(chips // 2 // pairs,),
        in_specs=[pl.BlockSpec(memory_space=pltpu.SMEM)]
        + [pl.BlockSpec((1, depth), lambda i: (0, 0))] * 2
        + [pl.BlockSpec((depth, width), lambda i: (0, 0))] * 2,
        out_specs=pl.BlockSpec((pairs, 4 * capacity, width), lambda i: (i, 0, 0)),
        out_shape=jax.ShapeDtypeStruct((chips // 2, 4 * capacity, width), jnp.bfloat16),
        compiler_params=GRANT,
        cost_estimate=pl.CostEstimate(
            flops=4 * chips * capacity * depth * width,
            bytes_accessed=8 * chips * capacity * width,
            transcendentals=0,
        ),
        name="place_rows",
    )(core, *targets, own, other)


def shift(value, axis, step):
    size = lax.axis_size(axis)
    return lax.ppermute(value, axis, [(i, (i + step) % size) for i in range(size)])


def local(embeddings, sketch_seed, list_ids, owner_map):
    row_count, dim = embeddings.shape
    rank = sketch_seed.shape[1]
    cores, line = lax.axis_size("narrow"), lax.axis_size("x")
    plane = lax.axis_size("y") * lax.axis_size("z")
    chips = plane * line
    dev_count = cores * chips
    core = lax.axis_index("narrow")
    spot = lax.axis_index("x").reshape(1)
    piece, gram_piece = dim // dev_count, rank // chips
    seed_matrix = sketch_seed.astype(jnp.bfloat16)
    sketch = jnp.dot(embeddings, seed_matrix, preferred_element_type=jnp.float32).astype(
        jnp.bfloat16
    )

    capacity = 4 * row_count // dev_count
    here = lax.axis_index("x")
    dest_index, labels = route_rows(list_ids, owner_map, capacity, line, plane)

    spots = jnp.stack([core, here, jnp.int32(line)])

    def chunks_at(*steps):
        pairs = cross_chunks(spots, embeddings, sketch, labels, line, steps)
        return [(pairs[2 * i + 1], shift(pairs[2 * i], "narrow", 1)) for i in range(len(steps))]

    (far,) = chunks_at(2)
    up, down, near = chunks_at(1, 3, 0)
    far = far[0] + far[1]
    from_below = shift(far[: rank // 2], "x", 1)
    from_above = shift(far[rank // 2 :], "x", line - 1)
    from_below = [shift(part, "x", 1) for part in join_chunk(*up, from_below, 0)]
    from_above = [shift(part, "x", line - 1) for part in join_chunk(*down, from_above, 1)]
    arrived = [part.astype(jnp.float32) for part in from_below + from_above]

    def target_of(dest):
        owner = dest // capacity
        return jnp.where(owner // chips == core, (owner % chips) * capacity + dest % capacity, -1)

    targets = target_of(dest_index), target_of(shift(dest_index, "narrow", 1))

    packed = line_total([*near, *arrived], plane, gram_piece)
    packed, targets = lax.optimization_barrier((packed, targets))
    packed = lax.all_to_all(packed.astype(jnp.float16), PLANE, 0, 0, tiled=True)
    packed = packed.astype(jnp.float32)
    packed, arrived_labels = plane_total(packed, piece, gram_piece)
    packed = jnp.broadcast_to(packed.astype(jnp.float16)[None], (plane,) + packed.shape)
    packed = lax.all_to_all(packed, PLANE, 0, 0, tiled=True)
    gram_line = gram_rows(packed[:, 2 * piece :].astype(jnp.float32), gram_piece)
    packed, gram_line = lax.optimization_barrier((packed, gram_line))
    gram_parts = [gram_line] + [shift(gram_line, "x", step) for step in range(1, line)]
    cross_line = packed[:, : 2 * piece + 8]
    cross_parts = [cross_line] + [shift(cross_line, "x", step) for step in range(1, line)]
    cross_parts = [part.astype(jnp.float32) for part in cross_parts]
    arrived_labels = arrived_labels[:, : cores * line * SLOTS].reshape(plane, cores, line, SLOTS)
    arrived_labels = arrived_labels[..., :capacity].transpose(1, 0, 2, 3)

    inverse = invert_factor(spot, gram_parts)
    inverse, cross_parts = lax.optimization_barrier((inverse, cross_parts))
    moment = moment_of(cross_parts)
    basis = project_half(spot, inverse, moment, shift(moment, "narrow", 1), cross_parts)
    other_basis = shift(basis, "narrow", 1)
    begun = product_of_half(spots, True, embeddings, basis, None, jnp.float32)
    reduced = product_of_half(spots, False, embeddings, other_basis, begun, jnp.bfloat16)
    other = shift(reduced, "narrow", 1)
    send_rows = place_rows(spots, targets, reduced, other, chips, capacity)
    send_rows = send_rows.reshape(chips, cores * capacity, rank)
    arrived = lax.all_to_all(send_rows, ("y", "z", "x"), 0, 0, tiled=True)
    arrived = arrived.reshape(chips, cores, capacity, rank).transpose(1, 0, 2, 3)
    return (
        arrived.reshape(1, dev_count, capacity, rank),
        arrived_labels.reshape(1, dev_count, capacity),
    )


def solution(mesh):
    grid = Mesh(mesh.devices.reshape(2, 4, 8, 4), ALL)
    in_specs = (P(ALL, None), P(), P(ALL), P())
    out_specs = (P(ALL, None, None, None), P(ALL, None, None))
    return jax.shard_map(local, mesh=grid, in_specs=in_specs, out_specs=out_specs, check_vma=False)
```
